256 devices in a mesh: group: 2 (over y_lo), seq: 16 (over z, y_hi), fsdp: 8 (over x, core).
Axes of the slice: x: 4, y: 4 (y_hi: 2, y_lo: 2; y = y_hi * 2 + y_lo), z: 8, core: 2. Of those that a mesh axis runs over, the one named last changes fastest.
Arguments:
- block_input: bfloat16 [2, 4096, 2560], P('group', 'seq', 'fsdp'), may hold values from -60 to 60
- head_outputs: bfloat16 [2, 4096, 3072], P('group', 'seq'), may hold values from -6 to 6
- out_master: float32 [2, 3072, 2560], P('group', 'seq', 'fsdp'), may hold values from -0.109375 to 0.109375
- first_moment: float32 [2, 3072, 2560], P('group', 'seq', 'fsdp'), may hold values from -3 to 3
- second_moment: float32 [2, 3072, 2560], P('group', 'seq', 'fsdp'), may hold values from 0.5 to 2
- score_qkv: bfloat16 [2, 3, 3072, 2560], P('group', None, 'fsdp', 'seq'), may hold values from -0.125 to 0.125
- teacher_out: bfloat16 [3072, 2560], P('seq', 'fsdp'), may hold values from -0.109375 to 0.109375
- noise: bfloat16 [4096, 2560], P('seq', 'fsdp'), may hold values from -6 to 6
- timestep: int32 [1], replicated, may hold values from 300 to 700
- fake_target: bfloat16 [4096, 2560], P('seq', 'fsdp'), may hold values from -6 to 6
Outputs:
- new_master: float32 [2, 3072, 2560], P('group', 'seq', 'fsdp')
- new_first: float32 [2, 3072, 2560], P('group', 'seq', 'fsdp')
- new_second: float32 [2, 3072, 2560], P('group', 'seq', 'fsdp')
The draws below stay inside these ranges and needn't reach their ends.
All inputs are finite; a program needn't handle non-finite values. Where the reference program divides by a largest or mean magnitude, that divisor is 1e-20 or more.
Results may differ from the reference program's by a relative error of at most 0.0075.
Values may be sent and summed in bfloat16 or wider, within the bound.
A program may use at most 64 MiB of HBM per device.

```python
import math
import jax
import jax.numpy as jnp
from jax import lax

D = 2560
HEADS = 24
HEAD_DIM = 128
INNER = 3072
L = 4096


def draw_block_input(key, part):
    parts_keys = jax.random.split(key, 3)
    positions = jnp.arange(L, dtype=jnp.float32) / L
    channels = jnp.arange(D, dtype=jnp.float32) / D
    row_factor = jnp.power(10.0, positions)[None, :, None] * jax.random.uniform(parts_keys[0], (2, L, 1), jnp.float32, 1.0, 2.0)
    column_factor = jnp.power(10.0, channels)[None, None, :] * jax.random.uniform(parts_keys[1], (2, 1, D), jnp.float32, 1.0, 2.0)
    base_values = jnp.clip(jax.random.normal(parts_keys[2], (2, L, D), jnp.float32), -6.0, 6.0)
    return (base_values * row_factor * column_factor / 40.0).astype(jnp.bfloat16)


def shard_levels(rng, extent, cuts, low, top_value):
    def one(position, blocks):
        heights = jax.random.uniform(jax.random.fold_in(jax.random.fold_in(rng, 6), position), (blocks,), jnp.float32, low / len(cuts), top_value / len(cuts))
        return jnp.repeat(jnp.exp(heights), extent[position] // blocks).reshape((-1,) + (1,) * (len(extent) - position - 1))

    level = one(*cuts[0])
    for cut in cuts[1:]:
        level = level * one(*cut)
    return level


def centred(stream_key, dims, scale, reach, cuts=(), kind=jnp.bfloat16):
    result = scale * jax.random.normal(stream_key, dims, jnp.float32)
    if cuts:
        result = result * shard_levels(stream_key, dims, cuts, -0.22, 0.18)
    return jnp.clip(result, -reach, reach).astype(kind)


def setup_inputs(seed: int = 0) -> dict:
    streams_of = jax.random.split(jax.random.key(seed), 11)
    block_input = draw_block_input(jax.random.fold_in(streams_of[10], 71), 0)
    head_outputs = centred(streams_of[1], (2, L, INNER), 1.0, 6.0, ((0, 2), (1, 16)))
    out_master = centred(streams_of[2], (2, INNER, D), INNER ** -0.5, 0.109375, ((0, 2), (1, 16), (2, 8)), jnp.float32)
    first_moment = centred(streams_of[3], (2, INNER, D), 0.5, 3.0, ((0, 2), (1, 16), (2, 8)), jnp.float32)
    second_moment = jnp.clip(jnp.exp(math.log(2.0) - 1.3862944 * jax.random.uniform(streams_of[4], (2, INNER, D), jnp.float32) ** shard_levels(streams_of[4], (2, INNER, D), ((0, 2), (1, 16), (2, 8)), -0.2, 0.2)), 0.5, 2.0)
    score_qkv = centred(streams_of[5], (2, 3, INNER, D), D ** -0.5, 0.125, ((0, 2), (2, 8), (3, 16)))
    teacher_out = centred(streams_of[6], (INNER, D), INNER ** -0.5, 0.109375, ((0, 16), (1, 8)))
    noise = centred(streams_of[7], (L, D), 1.0, 6.0, ((0, 16), (1, 8)))
    timestep = jax.random.randint(streams_of[8], (1,), 300, 701).astype(jnp.int32)
    fake_target = centred(streams_of[9], (L, D), 1.0, 6.0, ((0, 16), (1, 8)))
    return {"block_input": block_input, "head_outputs": head_outputs, "out_master": out_master, "first_moment": first_moment, "second_moment": second_moment, "score_qkv": score_qkv, "teacher_out": teacher_out, "noise": noise, "timestep": timestep, "fake_target": fake_target}


norm_eps = 1e-06
first_fix = 1.0 - 0.9 ** 20
second_fix = 1.0 - 0.95 ** 20
learn_rate = 0.003

def head_norm(projected):
    shaped = projected.reshape(projected.shape[0], HEADS, HEAD_DIM)
    factor = lax.rsqrt(lax.optimization_barrier(jnp.mean(shaped * shaped, axis=2, keepdims=True)) + norm_eps)
    return (shaped * factor).reshape(projected.shape).astype(jnp.bfloat16)

def split_heads(matrix):
    return matrix.reshape(matrix.shape[0], HEADS, HEAD_DIM).transpose(1, 0, 2)

def attend(query_hat, key_hat, value_rows):

    def one_head(head_parts):
        query_head, key_head, value_head = head_parts
        scores = jnp.dot(query_head, key_head.T, preferred_element_type=jnp.float32) * (1.0 / math.sqrt(HEAD_DIM))
        weights = jnp.exp(scores)
        weight_sum = lax.optimization_barrier(jnp.sum(weights, axis=1, keepdims=True))
        numerator = jnp.dot(weights.astype(jnp.bfloat16), value_head, preferred_element_type=jnp.float32)
        return (numerator / weight_sum).astype(jnp.bfloat16)
    per_head = lax.map(one_head, (split_heads(query_hat), split_heads(key_hat), split_heads(value_rows)))
    return per_head.transpose(1, 0, 2).reshape(query_hat.shape[0], HEADS * HEAD_DIM)

def reference(block_input, head_outputs, out_master, first_moment, second_moment, score_qkv, teacher_out, noise, timestep, fake_target):
    work_weight = out_master.astype(jnp.bfloat16)
    predicted = [block_input[member].astype(jnp.float32) + jnp.dot(head_outputs[member], work_weight[member], preferred_element_type=jnp.float32) for member in range(2)]
    generated = predicted[0].astype(jnp.bfloat16)
    noise_level = timestep[0].astype(jnp.float32) / 1000.0
    noisy_rows = ((1.0 - noise_level) * generated.astype(jnp.float32) + noise_level * noise.astype(jnp.float32)).astype(jnp.bfloat16)
    widened = noisy_rows.astype(jnp.float32)
    normed = (widened * lax.rsqrt(lax.optimization_barrier(jnp.mean(widened * widened, axis=1, keepdims=True)) + norm_eps)).astype(jnp.bfloat16)
    out_pick = [teacher_out, work_weight[1]]
    branches = []
    for member in range(2):
        query_raw = jnp.dot(normed, score_qkv[member, 0].T, preferred_element_type=jnp.float32)
        key_raw = jnp.dot(normed, score_qkv[member, 1].T, preferred_element_type=jnp.float32)
        value_raw = jnp.dot(normed, score_qkv[member, 2].T, preferred_element_type=jnp.float32)
        attended = attend(head_norm(query_raw), head_norm(key_raw), value_raw.astype(jnp.bfloat16))
        branches.append(jnp.dot(attended, out_pick[member], preferred_element_type=jnp.float32))
    teacher_guess = widened + branches[0]
    gap_mean = jnp.mean(jnp.abs(generated.astype(jnp.float32) - teacher_guess))
    match_grad = ((branches[1] - branches[0]) / (gap_mean + norm_eps)).astype(jnp.bfloat16)
    regress_grad = ((predicted[1] - fake_target.astype(jnp.float32)) / math.sqrt(L)).astype(jnp.bfloat16)
    gradients = [match_grad, regress_grad]
    masters = []
    firsts = []
    seconds = []
    for member in range(2):
        weight_grad = jnp.dot(head_outputs[member].T, gradients[member], preferred_element_type=jnp.float32)
        new_first = 0.9 * first_moment[member] + 0.1 * weight_grad
        new_second = 0.95 * second_moment[member] + 0.05 * weight_grad * weight_grad
        new_master = out_master[member] - learn_rate * (new_first / first_fix) / (jnp.sqrt(new_second / second_fix) + 1e-08)
        masters.append(new_master)
        firsts.append(new_first)
        seconds.append(new_second)
    return (jnp.stack(masters), jnp.stack(firsts), jnp.stack(seconds))
```

```python
import functools
import math

import jax
import jax.numpy as jnp
from jax import lax
from jax.experimental import pallas as pl
from jax.experimental.pallas import tpu as pltpu
from jax.sharding import PartitionSpec as P

D = 2560
HEAD_DIM = 128
MESH = pl.DeviceIdType.MESH

norm_eps = 1e-06
first_fix = 1.0 - 0.9**20
second_fix = 1.0 - 0.95**20
learn_rate = 0.003


class Sends:
    def __init__(self):
        self.open = []

    def start(self, ends, send_sem, recv_sem, device, when=None):
        def make():
            src, dst = ends()
            return pltpu.make_async_remote_copy(
                src_ref=src,
                dst_ref=dst,
                send_sem=send_sem(),
                recv_sem=recv_sem(),
                device_id=device(),
                device_id_type=MESH,
            )

        make().start()
        self.open.append((make, when))

    def same(self, ref, send_sem, recv_sem, device, when=None):
        def ends():
            here = ref()
            return here, here

        self.start(ends, send_sem, recv_sem, device, when)

    def finish(self):
        for make, when in self.open:
            if when is None:
                make().wait_send()
            else:
                pl.when(when)(lambda make=make: make().wait_send())
        self.open = []


def wait_recv(dst, recv_sem):
    pltpu.make_async_copy(dst, dst, recv_sem).wait()


class Ring:
    def __init__(self, sends, place, buf, rows, sems, when=None):
        self.sends, self.place, self.buf, self.rows, self.when = sends, place, buf, rows, when
        self.ring_send, self.ring_recv, self.pair_send, self.pair_recv = sems
        self.steps = place.zs // 2

    def piece(self, zz, cc, half):
        each = self.rows // 2
        start = (2 * zz + cc) * self.rows + half * each
        return self.buf.at[pl.ds(pl.multiple_of(start, 16), each)]

    def parts(self, k):
        if k < self.steps:
            return [(0, 0), (1, 0), (0, 1), (1, 1)]
        return [(0, 0), (1, 1)]

    def zz(self, k, way):
        p = self.place
        return lax.rem(p.z + p.zs - k, p.zs) if way == 0 else lax.rem(p.z + k, p.zs)

    def send(self, k, way, half):
        p = self.place
        self.sends.same(
            lambda: self.piece(self.zz(k - 1, way), p.c, half),
            lambda: self.ring_send.at[k - 1, way, half],
            lambda: self.ring_recv.at[k - 1, way, half],
            lambda: p.dev(z=p.zp if way == 0 else p.zm),
            self.when,
        )

    def pair(self, k, way, half):
        p = self.place
        self.sends.same(
            lambda: self.piece(self.zz(k, way), p.c, half),
            lambda: self.pair_send.at[k, way, half],
            lambda: self.pair_recv.at[k, way, half],
            lambda: p.dev(c=1 - p.c),
            self.when,
        )

    def begin(self):
        for way, half in self.parts(1):
            self.send(1, way, half)
        for half in (0, 1):
            self.pair(0, 0, half)

    def advance(self, k):
        for way, half in self.parts(k):
            wait_recv(
                self.piece(self.zz(k, way), self.place.c, half),
                self.ring_recv.at[k - 1, way, half],
            )
            if k < self.steps and (way, half) in self.parts(k + 1):
                self.send(k + 1, way, half)
            self.pair(k, way, half)

    def pair_arrived(self, k):
        for way, half in self.parts(k) if k else [(0, 0), (0, 1)]:
            wait_recv(
                self.piece(self.zz(k, way), 1 - self.place.c, half),
                self.pair_recv.at[k, way, half],
            )


class Place:
    def __init__(self, zs, xs):
        self.zs, self.xs = zs, xs
        seq, fsdp = lax.axis_index("seq"), lax.axis_index("fsdp")
        self.g = lax.axis_index("group")
        self.z, self.a = seq // 2, lax.rem(seq, 2)
        self.x, self.c = fsdp // 2, lax.rem(fsdp, 2)
        self.zp = lax.rem(self.z + 1, zs)
        self.zm = lax.rem(self.z + zs - 1, zs)
        self.block = 2 * self.x + self.a
        self.kept = self.a == self.c
        self.moved = self.a != self.c

    def dev(self, g=None, z=None, a=None, x=None, c=None):
        g = self.g if g is None else g
        z = self.z if z is None else z
        a = self.a if a is None else a
        x = self.x if x is None else x
        c = self.c if c is None else c
        return {"group": g, "seq": 2 * z + a, "fsdp": 2 * x + c}

    def fan(self):
        return [(2 * dx + da, dx, da) for dx in range(self.xs) for da in range(2) if dx or da]

    def beside(self, dx, da):
        return self.dev(x=lax.rem(self.x + dx, self.xs), a=lax.rem(self.a + da, 2))


def kernel(
    zs,
    xs,
    ts_ref,
    bi_ref,
    ho_ref,
    ww_ref,
    qw_ref,
    to_ref,
    noise_ref,
    target_ref,
    out_ref,
    w_buf,
    q_buf,
    hob,
    bi_t,
    noise_t,
    target_t,
    gen,
    gen_in,
    noisy,
    norm,
    kv,
    q_hat,
    acc,
    lsum,
    att,
    pred,
    b_own,
    b_in,
    grad,
    tmp,
    rs_send,
    rs_recv,
    gap_f,
    gap_z,
    gap_c,
    wg_out,
    wg_in,
    t_send,
    t_recv,
    ho_send,
    ho_recv,
    ring_send,
    ring_recv,
    pair_send,
    pair_recv,
    fan_send,
    fan_recv,
    rs_ssem,
    rs_rsem,
    gz_send,
    gz_recv,
    one_send,
    one_recv,
    local_sem,
):
    p = Place(zs, xs)
    sends = Sends()
    tokens, inner = ho_ref.shape
    cols = bi_ref.shape[1]
    rows = ww_ref.shape[0]
    depth = qw_ref.shape[0]
    local_inner = q_hat.shape[1]
    heads = local_inner // HEAD_DIM
    steps = zs // 2
    fans = 2 * xs
    first = p.g == 0
    second = p.g == 1
    f32 = jnp.float32

    barrier = pltpu.get_barrier_semaphore()
    peers = [p.dev(z=lax.rem(p.z + dz, zs)) for dz in range(1, zs)]
    peers += [p.beside(dx, da) for _, dx, da in p.fan()]
    peers += [p.dev(c=1 - p.c), p.dev(g=1 - p.g), p.dev(a=1 - p.a, c=1 - p.c)]
    for peer in peers:
        pl.semaphore_signal(barrier, inc=1, device_id=peer, device_id_type=MESH)

    own_ho = pltpu.make_async_copy(ho_ref, hob.at[p.a], local_sem.at[0])
    own_ho.start()
    pl.semaphore_wait(barrier, len(peers))

    def rows_of(buf, each, at):
        return buf.at[pl.ds(pl.multiple_of(at * each, 16), each)]

    away, home = 2 * p.z + p.a, 2 * p.z + p.c
    swaps = [
        (ww_ref, lambda i: rows_of(w_buf.at[0], rows, i)),
        (bi_ref, lambda i: bi_t),
        (qw_ref, lambda i: rows_of(q_buf, depth, i)),
        (noise_ref, lambda i: noise_t),
        (to_ref, lambda i: rows_of(w_buf.at[1], rows, i)),
        (target_ref, lambda i: target_t),
    ]

    def swap(n):
        src, dst = swaps[n]

        @pl.when(p.kept)
        def _():
            pltpu.make_async_copy(src, dst(away), t_recv.at[n]).start()

        @pl.when(p.moved)
        def _():
            sends.start(
                lambda: (src, dst(away)),
                lambda: t_send.at[n],
                lambda: t_recv.at[n],
                lambda: p.dev(a=p.c, c=p.a),
                p.moved,
            )

    def swapped(n):
        wait_recv(swaps[n][1](home), t_recv.at[n])

    swap(0)

    share = tokens // xs

    def ho_rows(block, xx):
        return hob.at[block, pl.ds(pl.multiple_of(xx * share, 16), share)]

    @pl.when(p.kept)
    def _():
        sends.start(
            lambda: (
                ho_ref.at[pl.ds(pl.multiple_of(p.x * share, 16), share)],
                ho_rows(p.a, p.x),
            ),
            lambda: ho_send.at[0],
            lambda: ho_recv.at[0],
            lambda: p.dev(a=1 - p.a),
            p.kept,
        )

    swap(1)
    swap(2)
    swapped(0)
    ring_w = Ring(
        sends, p, w_buf.at[0], rows,
        (ring_send.at[0], ring_recv.at[0], pair_send.at[0], pair_recv.at[0]),
    )
    ring_q = Ring(
        sends, p, q_buf, depth,
        (ring_send.at[1], ring_recv.at[1], pair_send.at[1], pair_recv.at[1]),
    )
    ring_kv = Ring(
        sends, p, kv, tokens,
        (ring_send.at[2], ring_recv.at[2], pair_send.at[2], pair_recv.at[2]),
    )
    ring_t = Ring(
        sends, p, w_buf.at[1], rows,
        (ring_send.at[3], ring_recv.at[3], pair_send.at[3], pair_recv.at[3]),
        first,
    )
    ring_w.begin()

    @pl.when(p.moved)
    def _():
        wait_recv(ho_rows(p.c, p.x), ho_recv.at[0])
        for dx in range(1, xs):
            sends.same(
                lambda: ho_rows(p.c, p.x),
                lambda dx=dx: ho_send.at[dx],
                lambda dx=dx: ho_recv.at[dx],
                lambda dx=dx: p.dev(x=lax.rem(p.x + dx, xs)),
                p.moved,
            )

    swap(3)
    swap(4)
    swap(5)
    for k in range(1, steps):
        ring_w.advance(k)
    swapped(2)
    ring_q.begin()
    ring_w.advance(steps)
    own_ho.wait()

    @pl.when(p.moved)
    def _():
        for dx in range(1, xs):
            wait_recv(ho_rows(p.c, lax.rem(p.x + xs - dx, xs)), ho_recv.at[dx])
        sends.same(
            lambda: hob.at[p.c],
            lambda: ho_send.at[xs],
            lambda: ho_recv.at[xs],
            lambda: p.dev(c=1 - p.c),
            p.moved,
        )

    for k in range(steps + 1):
        ring_w.pair_arrived(k)
    swapped(1)

    wide = 2 * rows

    def project(lhs, which, out):
        def part(j, carry):
            at = pl.ds(pl.multiple_of(j * wide, 128), wide)
            out[...] += jnp.dot(
                lhs(j, at), w_buf[which, at, :], preferred_element_type=f32
            )
            return carry

        lax.fori_loop(0, inner // wide, part, 0)

    pred[...] = bi_t[...].astype(f32)
    project(lambda j, at: hob[p.c, :, at], 0, pred)

    @pl.when(first)
    def _():
        gen[...] = pred[...].astype(jnp.bfloat16)
        sends.start(
            lambda: (gen, gen_in), lambda: one_send.at[0], lambda: one_recv.at[0], lambda: p.dev(g=1), first
        )

    ring_q.advance(1)
    swapped(3)

    @pl.when(second)
    def _():
        wait_recv(gen_in, one_recv.at[0])
        gen[...] = gen_in[...]

    level = ts_ref[0].astype(f32) / 1000.0
    noisy[p.block] = (
        (1.0 - level) * gen[...].astype(f32) + level * noise_t[...].astype(f32)
    ).astype(jnp.bfloat16)

    def spread(buf, n, when=None):
        for rank, dx, da in p.fan():
            sends.same(
                lambda: buf.at[p.block],
                lambda rank=rank: fan_send.at[n, rank],
                lambda rank=rank: fan_recv.at[n, rank],
                lambda dx=dx, da=da: p.beside(dx, da),
                when,
            )

    def gathered(buf, n):
        for rank, dx, da in p.fan():
            block = 2 * lax.rem(p.x + xs - dx, xs) + lax.rem(p.a + da, 2)
            wait_recv(buf.at[block], fan_recv.at[n, rank])

    spread(noisy, 0)
    for k in range(2, steps):
        ring_q.advance(k)
    gathered(noisy, 0)

    def squares(f, total):
        block = noisy[f].astype(f32)
        return total + jnp.sum(block * block, axis=1, keepdims=True)

    total = lax.fori_loop(0, fans, squares, jnp.zeros((tokens, 1), f32))
    factor = lax.rsqrt(total * (1.0 / (fans * cols)) + norm_eps)

    def normalise(f, carry):
        norm[f] = (noisy[f].astype(f32) * factor).astype(jnp.bfloat16)
        return carry

    lax.fori_loop(0, fans, normalise, 0)
    for k in range(max(2, steps), steps + 1):
        ring_q.advance(k)
    for k in range(steps + 1):
        ring_q.pair_arrived(k)

    def head_norm(value):
        scale = lax.rsqrt(jnp.mean(value * value, axis=1, keepdims=True) + norm_eps)
        return (value * scale).astype(jnp.bfloat16)

    own_rows = pl.ds(pl.multiple_of(home * tokens, 16), tokens)

    def proj(n):
        value = jnp.zeros((tokens, local_inner), f32)
        for f in range(fans):
            value += jnp.dot(
                norm[f],
                q_buf[f * cols : (f + 1) * cols, n * local_inner : (n + 1) * local_inner],
                preferred_element_type=f32,
            )
        return value

    key_raw = proj(1)
    for h in range(heads):
        at = slice(h * HEAD_DIM, (h + 1) * HEAD_DIM)
        kv[own_rows, h * HEAD_DIM : (h + 1) * HEAD_DIM] = head_norm(key_raw[:, at])
    kv[own_rows, local_inner:] = proj(2).astype(jnp.bfloat16)
    ring_kv.begin()
    query_raw = proj(0)
    for h in range(heads):
        at = slice(h * HEAD_DIM, (h + 1) * HEAD_DIM)
        q_hat[:, at] = head_norm(query_raw[:, at])
    acc[...] = jnp.zeros_like(acc)
    lsum[...] = jnp.zeros_like(lsum)

    def attend(zz):
        at = pl.ds(pl.multiple_of(zz * 2 * tokens, 16), 2 * tokens)

        def one_head(h, carry):
            cut = pl.ds(pl.multiple_of(h * HEAD_DIM, HEAD_DIM), HEAD_DIM)
            cut_v = pl.ds(pl.multiple_of(local_inner + h * HEAD_DIM, HEAD_DIM), HEAD_DIM)
            scores = lax.dot_general(
                q_hat[:, cut], kv[at, cut], (((1,), (1,)), ((), ())), preferred_element_type=f32
            ) * (1.0 / math.sqrt(HEAD_DIM))
            weights = jnp.exp(scores)
            part = weights[:, :128]
            for j in range(1, 2 * tokens // 128):
                part += weights[:, j * 128 : (j + 1) * 128]
            lsum[h] += part
            acc[:, cut] += jnp.dot(
                weights.astype(jnp.bfloat16), kv[at, cut_v], preferred_element_type=f32
            )
            return carry

        lax.fori_loop(0, heads, one_head, 0)

    ring_kv.pair_arrived(0)
    attend(p.z)
    for k in range(1, steps + 1):
        ring_kv.advance(k)
        if k == steps:
            @pl.when(first)
            def _():
                swapped(4)
                ring_t.begin()
        if k > 1:
            ring_kv.pair_arrived(k - 1)
            for way in (0, 1):
                attend(ring_kv.zz(k - 1, way))
    ring_kv.pair_arrived(steps)
    attend(ring_kv.zz(steps, 0))

    for h in range(heads):
        at = slice(h * HEAD_DIM, (h + 1) * HEAD_DIM)
        att[p.block, :, at] = (
            acc[:, at] / jnp.sum(lsum[h], axis=1, keepdims=True)
        ).astype(jnp.bfloat16)
    spread(att, 1)

    @pl.when(first)
    def _():
        for k in range(1, steps + 1):
            ring_t.advance(k)
        for k in range(steps + 1):
            ring_t.pair_arrived(k)

    @pl.when(second)
    def _():
        swapped(4)

    gathered(att, 1)
    b_own[...] = jnp.zeros_like(b_own)
    project(lambda j, at: att[j], 1 - p.g, b_own)
    swapped(5)

    @pl.when(second)
    def _():
        sends.start(
            lambda: (b_own, b_in), lambda: one_send.at[1], lambda: one_recv.at[1], lambda: p.dev(g=0), second
        )
        grad[p.c] = (
            (pred[...] - target_t[...].astype(f32)) * (1.0 / math.sqrt(tokens * 2 * zs))
        ).astype(jnp.bfloat16)

    @pl.when(first)
    def _():
        guess = noisy[p.block].astype(f32) + b_own[...]
        gap = jnp.sum(jnp.abs(gen[...].astype(f32) - guess))
        gap_f[p.block] = jnp.full((8, 128), gap, f32)
        spread(gap_f, 2, first)
        wait_recv(b_in, one_recv.at[1])
        grad[p.c] = (b_in[...] - b_own[...]).astype(jnp.bfloat16)

    sends.same(
        lambda: grad.at[p.c], lambda: one_send.at[2], lambda: one_recv.at[2], lambda: p.dev(c=1 - p.c)
    )

    @pl.when(p.kept)
    def _():
        wait_recv(hob.at[1 - p.c], ho_recv.at[xs])

    wait_recv(grad.at[1 - p.c], one_recv.at[2])

    def partial(zz):
        at = pl.ds(pl.multiple_of(zz * wide, 128), wide)
        value = jnp.zeros((wide, cols), f32)
        for block in range(2):
            value += lax.dot_general(
                hob[block, :, at],
                grad[block],
                (((0,), (0,)), ((), ())),
                preferred_element_type=f32,
            )
        tmp[...] = value
        return tmp[pl.ds(pl.multiple_of(p.c * rows, 16), rows), :]

    def span(j, way):
        if j > 1:
            return slice(0, rows)
        return slice(0, rows // 2) if way == 0 else slice(rows // 2, rows)

    def rs_start(j, way):
        at = span(j, way)
        sends.start(
            lambda: (rs_send.at[j - 1, way, at], rs_recv.at[j - 1, way, at]),
            lambda: rs_ssem.at[j - 1, way],
            lambda: rs_rsem.at[j - 1, way],
            lambda: p.dev(z=p.zp if way == 0 else p.zm),
        )

    def rs_wait(j, way):
        wait_recv(rs_recv.at[j - 1, way, span(j, way)], rs_rsem.at[j - 1, way])

    def gap_step(j):
        if j == 1:
            gathered(gap_f, 2)
            gap_z[p.z] = jnp.sum(gap_f[...], axis=0)
            for dz in range(1, zs):
                sends.same(
                    lambda: gap_z.at[p.z],
                    lambda dz=dz: gz_send.at[dz],
                    lambda dz=dz: gz_recv.at[dz],
                    lambda dz=dz: p.dev(z=lax.rem(p.z + dz, zs)),
                    first,
                )
        if j == 2:
            for dz in range(1, zs):
                wait_recv(gap_z.at[lax.rem(p.z + zs - dz, zs)], gz_recv.at[dz])
            gap_c[p.c] = jnp.sum(gap_z[...], axis=0)
            sends.same(
                lambda: gap_c.at[p.c],
                lambda: one_send.at[3],
                lambda: one_recv.at[3],
                lambda: p.dev(c=1 - p.c),
                first,
            )
        if j == 3:
            wait_recv(gap_c.at[1 - p.c], one_recv.at[3])

    far = partial(lax.rem(p.z + steps, zs))
    for way in (0, 1):
        rs_send[0, way, span(1, way), :] = far[span(1, way)].astype(jnp.bfloat16)
        rs_start(1, way)
    pl.when(first)(lambda: gap_step(1))
    for j in range(2, steps + 1):
        for way in (0, 1):
            dist = steps - j + 1
            there = lax.rem(p.z + dist, zs) if way == 0 else lax.rem(p.z + zs - dist, zs)
            mine = partial(there)
            rs_wait(j - 1, way)
            at = span(j - 1, way)
            rs_send[j - 1, way] = mine.astype(jnp.bfloat16)
            rs_send[j - 1, way, at, :] = (
                mine[at] + rs_recv[j - 2, way, at, :].astype(f32)
            ).astype(jnp.bfloat16)
            rs_start(j, way)
        if j == 2:
            pl.when(first)(lambda: gap_step(2))
    if steps == 1:
        pl.when(first)(lambda: gap_step(2))
    mine = partial(p.z)
    pl.when(first)(lambda: gap_step(3))
    acc_w = tmp.at[0:rows]
    acc_w[...] = mine
    for way in (0, 1):
        rs_wait(steps, way)
        at = span(steps, way)
        acc_w[at, :] = acc_w[at, :] + rs_recv[steps - 1, way, at, :].astype(f32)

    @pl.when(first)
    def _():
        gap = (gap_c[0] + gap_c[1])[0:1, 0:1] * (1.0 / (tokens * 2 * zs * fans * cols))
        wg_out[...] = (acc_w[...] * (1.0 / (gap + norm_eps))).astype(jnp.bfloat16)

    @pl.when(second)
    def _():
        wg_out[...] = acc_w[...].astype(jnp.bfloat16)

    @pl.when(p.moved)
    def _():
        sends.start(
            lambda: (wg_out, wg_in),
            lambda: one_send.at[4],
            lambda: one_recv.at[4],
            lambda: p.dev(a=p.c, c=p.a),
            p.moved,
        )
        wait_recv(wg_in, one_recv.at[4])
        out_ref[...] = wg_in[...].astype(f32)

    @pl.when(p.kept)
    def _():
        out_ref[...] = wg_out[...].astype(f32)

    sends.finish()


def weight_gradient(zs, xs, ts, bi, ho, ww, qw, to, noise, target, interpret=None):
    tokens, inner = ho.shape
    cols = bi.shape[1]
    rows = ww.shape[0]
    depth, triple = qw.shape
    local_inner = triple // 3
    heads = local_inner // HEAD_DIM
    seq, fans, steps = 2 * zs, 2 * xs, zs // 2
    b16, f32 = jnp.bfloat16, jnp.float32
    vmem, dma = pltpu.VMEM, pltpu.SemaphoreType.DMA
    scratch = [
        vmem((2, inner, cols), b16),
        vmem((seq * depth, triple), b16),
        vmem((2, tokens, inner), b16),
        vmem((tokens, cols), b16),
        vmem((tokens, cols), b16),
        vmem((tokens, cols), b16),
        vmem((tokens, cols), b16),
        vmem((tokens, cols), b16),
        vmem((fans, tokens, cols), b16),
        vmem((fans, tokens, cols), b16),
        vmem((seq * tokens, 2 * local_inner), b16),
        vmem((tokens, local_inner), b16),
        vmem((tokens, local_inner), f32),
        vmem((heads, tokens, 128), f32),
        vmem((fans, tokens, local_inner), b16),
        vmem((tokens, cols), f32),
        vmem((tokens, cols), f32),
        vmem((tokens, cols), f32),
        vmem((2, tokens, cols), b16),
        vmem((2 * rows, cols), f32),
        vmem((steps, 2, rows, cols), b16),
        vmem((steps, 2, rows, cols), b16),
        vmem((fans, 8, 128), f32),
        vmem((zs, 8, 128), f32),
        vmem((2, 8, 128), f32),
        vmem((rows, cols), b16),
        vmem((rows, cols), b16),
        dma((6,)),
        dma((6,)),
        dma((xs + 1,)),
        dma((xs + 1,)),
        dma((4, steps, 2, 2)),
        dma((4, steps, 2, 2)),
        dma((4, steps + 1, 2, 2)),
        dma((4, steps + 1, 2, 2)),
        dma((3, fans)),
        dma((3, fans)),
        dma((steps, 2)),
        dma((steps, 2)),
        dma((zs,)),
        dma((zs,)),
        dma((5,)),
        dma((5,)),
        dma((1,)),
    ]
    in_vmem = pl.BlockSpec(memory_space=pltpu.VMEM)
    return pl.pallas_call(
        functools.partial(kernel, zs, xs),
        out_shape=jax.ShapeDtypeStruct((rows, cols), f32),
        in_specs=[pl.BlockSpec(memory_space=pltpu.SMEM), in_vmem, pl.BlockSpec(memory_space=pl.ANY)]
        + [in_vmem] * 5,
        out_specs=in_vmem,
        scratch_shapes=scratch,
        compiler_params=pltpu.CompilerParams(
            collective_id=0, has_side_effects=True, vmem_limit_bytes=56 * 1024 * 1024
        ),
        name="weight_gradient",
    )(ts, bi, ho, ww, qw, to, noise, target)


def body(
    block_input,
    head_outputs,
    out_master,
    first_moment,
    second_moment,
    score_qkv,
    teacher_out,
    noise,
    timestep,
    fake_target,
):
    zs, xs = lax.axis_size("seq") // 2, lax.axis_size("fsdp") // 2
    work_weight = out_master[0].astype(jnp.bfloat16)
    triple = score_qkv.shape[1] * score_qkv.shape[2]
    qw = score_qkv[0].reshape(triple, score_qkv.shape[3]).T
    weight_grad = weight_gradient(
        zs, xs, timestep, block_input[0], head_outputs[0], work_weight, qw, teacher_out, noise,
        fake_target,
    )
    new_first = 0.9 * first_moment[0] + 0.1 * weight_grad
    new_second = 0.95 * second_moment[0] + 0.05 * weight_grad * weight_grad
    new_master = out_master[0] - learn_rate * (new_first / first_fix) / (
        jnp.sqrt(new_second / second_fix) + 1e-08
    )
    return (new_master[None], new_first[None], new_second[None])


def solution(mesh):
    placed = (
        P("group", "seq", "fsdp"),
        P("group", "seq", None),
        P("group", "seq", "fsdp"),
        P("group", "seq", "fsdp"),
        P("group", "seq", "fsdp"),
        P("group", None, "fsdp", "seq"),
        P("seq", "fsdp"),
        P("seq", "fsdp"),
        P(),
        P("seq", "fsdp"),
    )
    return jax.shard_map(
        body,
        mesh=mesh,
        in_specs=placed,
        out_specs=(P("group", "seq", "fsdp"), P("group", "seq", "fsdp"), P("group", "seq", "fsdp")),
        check_vma=False,
    )
```

```python
import functools
import math

import jax
import jax.numpy as jnp
from jax import lax
from jax.experimental import pallas as pl
from jax.experimental.pallas import tpu as pltpu
from jax.sharding import PartitionSpec as P

D = 2560
HEAD_DIM = 128
MESH = pl.DeviceIdType.MESH

norm_eps = 1e-06
first_fix = 1.0 - 0.9**20
second_fix = 1.0 - 0.95**20
learn_rate = 0.003


class Sends:
    def __init__(self):
        self.open = []

    def start(self, ends, send_sem, recv_sem, device, when=None):
        def make():
            src, dst = ends()
            return pltpu.make_async_remote_copy(
                src_ref=src,
                dst_ref=dst,
                send_sem=send_sem(),
                recv_sem=recv_sem(),
                device_id=device(),
                device_id_type=MESH,
            )

        make().start()
        self.open.append((make, when))

    def same(self, ref, send_sem, recv_sem, device, when=None):
        def ends():
            here = ref()
            return here, here

        self.start(ends, send_sem, recv_sem, device, when)

    def finish(self):
        for make, when in self.open:
            if when is None:
                make().wait_send()
            else:
                pl.when(when)(lambda make=make: make().wait_send())
        self.open = []


def wait_recv(dst, recv_sem):
    pltpu.make_async_copy(dst, dst, recv_sem).wait()


class Ring:
    def __init__(self, sends, place, buf, rows, sems, when=None, split=False):
        self.sends, self.place, self.buf, self.rows, self.when = sends, place, buf, rows, when
        self.split = split
        self.ring_send, self.ring_recv, self.pair_send, self.pair_recv = sems
        self.steps = place.zs // 2

    def piece(self, zz, cc, half):
        if self.split:
            start = (2 * zz + cc) * self.rows
            return self.buf.at[half, pl.ds(pl.multiple_of(start, 16), self.rows)]
        each = self.rows // 2
        start = (2 * zz + cc) * self.rows + half * each
        return self.buf.at[pl.ds(pl.multiple_of(start, 16), each)]

    def parts(self, k):
        if k < self.steps:
            return [(0, 0), (1, 0), (0, 1), (1, 1)]
        return [(0, 0), (1, 1)]

    def zz(self, k, way):
        p = self.place
        return lax.rem(p.z + p.zs - k, p.zs) if way == 0 else lax.rem(p.z + k, p.zs)

    def send(self, k, way, half):
        p = self.place
        self.sends.same(
            lambda: self.piece(self.zz(k - 1, way), p.c, half),
            lambda: self.ring_send.at[k - 1, way, half],
            lambda: self.ring_recv.at[k - 1, way, half],
            lambda: p.dev(z=p.zp if way == 0 else p.zm),
            self.when,
        )

    def pair(self, k, way, half):
        p = self.place
        self.sends.same(
            lambda: self.piece(self.zz(k, way), p.c, half),
            lambda: self.pair_send.at[k, way, half],
            lambda: self.pair_recv.at[k, way, half],
            lambda: p.dev(c=1 - p.c),
            self.when,
        )

    def begin(self, halves=(0, 1)):
        for way, half in self.parts(1):
            if half in halves:
                self.send(1, way, half)
        for half in halves:
            self.pair(0, 0, half)

    def advance(self, k):
        for way, half in self.parts(k):
            wait_recv(
                self.piece(self.zz(k, way), self.place.c, half),
                self.ring_recv.at[k - 1, way, half],
            )
            if k < self.steps and (way, half) in self.parts(k + 1):
                self.send(k + 1, way, half)
            self.pair(k, way, half)

    def pair_arrived(self, k):
        for way, half in self.parts(k) if k else [(0, 0), (0, 1)]:
            wait_recv(
                self.piece(self.zz(k, way), 1 - self.place.c, half),
                self.pair_recv.at[k, way, half],
            )


class Across:
    def __init__(self, sends, place, buf, sems):
        self.sends, self.place, self.buf = sends, place, buf
        self.send_sem, self.recv_sem = sems
        self.rows = buf.shape[1]

    def part(self, dx, other, half, quarter=None):
        p = self.place
        block = 2 * lax.rem(p.x + dx + p.xs, p.xs) + (1 - p.a if other else p.a)
        each = self.rows // 2
        start = half * each
        if quarter is not None:
            each = each // 2
            start = start + quarter * each
        return self.buf.at[block, pl.ds(start, each)]

    def go(self, n, ref, device):
        self.sends.same(ref, lambda: self.send_sem.at[n], lambda: self.recv_sem.at[n], device)

    def beside(self, way):
        p = self.place
        return p.dev(x=lax.rem(p.x + (1 if way == 0 else p.xs - 1), p.xs))

    def cross(self, half):
        p = self.place
        self.go(half, lambda: self.part(0, False, half), lambda: p.dev(a=1 - p.a))

    def crossed(self, half):
        wait_recv(self.part(0, True, half), self.recv_sem.at[half])

    def step(self, other, half):
        for way in (0, 1):
            self.go(
                2 + 4 * other + 2 * half + way,
                lambda: self.part(0, other, half),
                lambda way=way: self.beside(way),
            )

    def forward(self, other, half):
        for way in (0, 1):
            near = -1 if way == 0 else 1
            n = 4 * other + 2 * half + way
            wait_recv(self.part(near, other, half), self.recv_sem.at[2 + n])
            self.go(
                10 + n,
                lambda near=near, way=way: self.part(near, other, half, way),
                lambda way=way: self.beside(way),
            )

    def arrived(self, half):
        for other in (0, 1):
            for way in (0, 1):
                n = 4 * other + 2 * half + way
                wait_recv(self.part(2, other, half, way), self.recv_sem.at[10 + n])

    def begin(self, half):
        self.cross(half)
        self.step(0, half)


class Place:
    def __init__(self, zs, xs):
        self.zs, self.xs = zs, xs
        seq, fsdp = lax.axis_index("seq"), lax.axis_index("fsdp")
        self.g = lax.axis_index("group")
        self.z, self.a = seq // 2, lax.rem(seq, 2)
        self.x, self.c = fsdp // 2, lax.rem(fsdp, 2)
        self.zp = lax.rem(self.z + 1, zs)
        self.zm = lax.rem(self.z + zs - 1, zs)
        self.block = 2 * self.x + self.a
        self.kept = self.a == self.c
        self.moved = self.a != self.c
        self.first = self.g == 0
        self.second = self.g == 1

    def dev(self, g=None, z=None, a=None, x=None, c=None):
        g = self.g if g is None else g
        z = self.z if z is None else z
        a = self.a if a is None else a
        x = self.x if x is None else x
        c = self.c if c is None else c
        return {"group": g, "seq": 2 * z + a, "fsdp": 2 * x + c}

    def fan(self):
        return [(2 * dx + da, dx, da) for dx in range(self.xs) for da in range(2) if dx or da]

    def beside(self, dx, da):
        return self.dev(x=lax.rem(self.x + dx, self.xs), a=lax.rem(self.a + da, 2))


def kernel(
    zs,
    xs,
    ts_ref,
    bi_ref,
    ho_ref,
    ww_ref,
    qw_ref,
    to_ref,
    noise_ref,
    target_ref,
    out_ref,
    w_buf,
    q_buf,
    hob,
    bi_t,
    noise_t,
    target_t,
    gen,
    gen_in,
    noisy,
    norm,
    kv,
    q_hat,
    acc,
    lsum,
    att,
    pred,
    b_own,
    b_in,
    grad,
    tmp,
    rs_send,
    rs_recv,
    gap_f,
    gap_z,
    gap_c,
    wg_out,
    wg_in,
    t_send,
    t_recv,
    ho_send,
    ho_recv,
    ring_send,
    ring_recv,
    pair_send,
    pair_recv,
    fan_send,
    fan_recv,
    rs_ssem,
    rs_rsem,
    gf_send,
    gf_recv,
    gz_send,
    gz_recv,
    one_send,
    one_recv,
    local_sem,
):
    p = Place(zs, xs)
    sends = Sends()
    tokens, inner = ho_ref.shape
    cols = bi_ref.shape[1]
    rows = ww_ref.shape[0]
    depth = qw_ref.shape[0]
    local_inner = q_hat.shape[1]
    heads = local_inner // HEAD_DIM
    steps = zs // 2
    fans = 2 * xs
    first = p.first
    second = p.second
    f32 = jnp.float32

    barrier = pltpu.get_barrier_semaphore()
    peers = [p.dev(z=lax.rem(p.z + dz, zs)) for dz in range(1, zs)]
    peers += [p.beside(dx, da) for _, dx, da in p.fan()]
    peers += [p.dev(c=1 - p.c), p.dev(g=1 - p.g), p.dev(a=1 - p.a, c=1 - p.c)]
    for peer in peers:
        pl.semaphore_signal(barrier, inc=1, device_id=peer, device_id_type=MESH)

    own_ho = pltpu.make_async_copy(ho_ref, hob.at[p.a], local_sem.at[0])
    own_ho.start()
    pl.semaphore_wait(barrier, len(peers))

    def rows_of(buf, each, at):
        return buf.at[pl.ds(pl.multiple_of(at * each, 16), each)]

    away, home = 2 * p.z + p.a, 2 * p.z + p.c
    swaps = [
        (ww_ref, lambda i: rows_of(w_buf.at[0], rows, i)),
        (bi_ref, lambda i: bi_t),
        (qw_ref, lambda i: rows_of(q_buf, depth, i)),
        (noise_ref, lambda i: noise_t),
        (to_ref, lambda i: rows_of(w_buf.at[1], rows, i)),
        (target_ref, lambda i: target_t),
        (ww_ref, lambda i: rows_of(w_buf.at[1], rows, i)),
    ]

    def swap(n, when):
        src, dst = swaps[n]

        @pl.when(p.kept)
        def _():
            pltpu.make_async_copy(src, dst(away), t_recv.at[n]).start()

        @pl.when(p.moved)
        def _():
            sends.start(
                lambda: (src, dst(away)),
                lambda: t_send.at[n],
                lambda: t_recv.at[n],
                lambda: p.dev(a=p.c, c=p.a),
                when,
            )

    first_moved, second_moved = first & p.moved, second & p.moved
    first_kept, second_kept = first & p.kept, second & p.kept

    def swapped(n):
        wait_recv(swaps[n][1](home), t_recv.at[n])

    share = tokens // xs

    def ho_rows(block, dx, half=None):
        start = lax.rem(p.x + dx + xs, xs) * share
        each = share
        if half is not None:
            each = share // 2
            start = start + half * each
        return hob.at[block, pl.ds(pl.multiple_of(start, 16), each)]

    def ho_cross(when):
        @pl.when(p.kept)
        def _():
            sends.start(
                lambda: (
                    ho_ref.at[pl.ds(pl.multiple_of(p.x * share, 16), share)],
                    ho_rows(p.a, 0),
                ),
                lambda: ho_send.at[0],
                lambda: ho_recv.at[0],
                lambda: p.dev(a=1 - p.a),
                when,
            )

    def beside(way):
        return p.dev(x=lax.rem(p.x + (1 if way == 0 else xs - 1), xs))

    def ho_step(when):
        @pl.when(p.moved)
        def _():
            wait_recv(ho_rows(p.c, 0), ho_recv.at[0])
            for way in (0, 1):
                sends.same(
                    lambda: ho_rows(p.c, 0),
                    lambda way=way: ho_send.at[1 + way],
                    lambda way=way: ho_recv.at[1 + way],
                    lambda way=way: beside(way),
                    when,
                )

    def ho_forward(when):
        @pl.when(p.moved)
        def _():
            for way in (0, 1):
                near = -1 if way == 0 else 1
                wait_recv(ho_rows(p.c, near), ho_recv.at[1 + way])
                sends.same(
                    lambda near=near, way=way: ho_rows(p.c, near, way),
                    lambda way=way: ho_send.at[3 + way],
                    lambda way=way: ho_recv.at[3 + way],
                    lambda way=way: beside(way),
                    when,
                )

    def ho_arrived(when):
        @pl.when(p.moved)
        def _():
            for way in (0, 1):
                wait_recv(ho_rows(p.c, 2, way), ho_recv.at[3 + way])
            sends.same(
                lambda: hob.at[p.c],
                lambda: ho_send.at[5],
                lambda: ho_recv.at[5],
                lambda: p.dev(c=1 - p.c),
                when,
            )

    def ring(buf, each, n, when=None, split=False):
        sems = (ring_send.at[n], ring_recv.at[n], pair_send.at[n], pair_recv.at[n])
        return Ring(sends, p, buf, each, sems, when, split)

    ring_w = ring(w_buf.at[0], rows, 0, first)
    ring_qs = [ring(q_buf, depth, 1, first), ring(q_buf, depth, 1, second)]
    ring_kv = ring(kv, tokens, 2, split=True)
    ring_t = ring(w_buf.at[1], rows, 3)
    over_noisy = Across(sends, p, noisy, (fan_send.at[0], fan_recv.at[0]))
    over_att = Across(sends, p, att, (fan_send.at[1], fan_recv.at[1]))

    wide = 2 * rows

    def project(lhs, which, out):
        def part(j, carry):
            at = pl.ds(pl.multiple_of(j * wide, 128), wide)
            out[...] += jnp.dot(
                lhs(j, at), w_buf[which, at, :], preferred_element_type=f32
            )
            return carry

        lax.fori_loop(0, inner // wide, part, 0)

    def gap_spread():
        for rank, dx, da in p.fan():
            sends.same(
                lambda: gap_f.at[p.block],
                lambda rank=rank: gf_send.at[rank],
                lambda rank=rank: gf_recv.at[rank],
                lambda dx=dx, da=da: p.beside(dx, da),
                first,
            )

    def gap_gathered():
        for rank, dx, da in p.fan():
            block = 2 * lax.rem(p.x + xs - dx, xs) + lax.rem(p.a + da, 2)
            wait_recv(gap_f.at[block], gf_recv.at[rank])

    def predict(which):
        pred[...] = bi_t[...].astype(f32)
        project(lambda j, at: hob[p.c, :, at], which, pred)

    half_rows = [slice(0, tokens // 2), slice(tokens // 2, tokens)]

    @pl.when(first)
    def _():
        ring_q = ring_qs[0]
        swap(0, first_moved)
        ho_cross(first_kept)
        swap(1, first_moved)
        swapped(0)
        ring_w.begin()
        swap(3, first_moved)
        swap(2, first_moved)
        ring_w.advance(1)
        ho_step(first_moved)
        ring_w.advance(2)
        ring_w.advance(3)
        ho_forward(first_moved)
        swapped(2)
        ring_q.begin()
        swap(4, first_moved)
        ring_w.advance(4)
        own_ho.wait()
        ho_arrived(first_moved)
        for k in range(steps + 1):
            ring_w.pair_arrived(k)
        swapped(1)
        predict(0)
        gen[...] = pred[...].astype(jnp.bfloat16)
        for h in (0, 1):
            sends.start(
                lambda h=h: (gen.at[half_rows[h]], gen_in.at[half_rows[h]]),
                lambda h=h: one_send.at[h],
                lambda h=h: one_recv.at[h],
                lambda: p.dev(g=1),
                first,
            )

    @pl.when(second)
    def _():
        ring_q = ring_qs[1]
        swap(2, second_moved)
        swapped(2)
        ring_q.begin()
        swap(3, second_moved)
        ring_q.advance(1)
        swap(6, second_moved)
        ring_q.advance(2)
        ho_cross(second_kept)
        swap(1, second_moved)
        ring_q.advance(3)
        ho_step(second_moved)
        swap(5, second_moved)
        ring_q.advance(4)
        ho_forward(second_moved)
        own_ho.wait()

    swapped(3)
    level = ts_ref[0].astype(f32) / 1000.0
    for h in (0, 1):
        at = half_rows[h]

        @pl.when(second)
        def _():
            wait_recv(gen_in.at[at], one_recv.at[h])
            gen[at, :] = gen_in[at, :]

        noisy[p.block, at, :] = (
            (1.0 - level) * gen[at, :].astype(f32) + level * noise_t[at, :].astype(f32)
        ).astype(jnp.bfloat16)
        over_noisy.begin(h)

    def first_q(k):
        pl.when(first)(lambda: ring_qs[0].advance(k))

    over_noisy.forward(0, 0)
    first_q(1)
    over_noisy.crossed(0)
    over_noisy.step(1, 0)
    over_noisy.forward(0, 1)
    over_noisy.crossed(1)
    over_noisy.step(1, 1)
    first_q(2)
    over_noisy.forward(1, 0)
    over_noisy.forward(1, 1)
    first_q(3)
    over_noisy.arrived(0)
    over_noisy.arrived(1)

    @pl.when(second)
    def _():
        ho_arrived(second_moved)

    def squares(f, total):
        block = noisy[f].astype(f32)
        return total + jnp.sum(block * block, axis=1, keepdims=True)

    total = lax.fori_loop(0, fans, squares, jnp.zeros((tokens, 1), f32))
    factor = lax.rsqrt(total * (1.0 / (fans * cols)) + norm_eps)

    def normalise(f, carry):
        norm[f] = (noisy[f].astype(f32) * factor).astype(jnp.bfloat16)
        return carry

    lax.fori_loop(0, fans, normalise, 0)
    first_q(4)
    for k in range(steps + 1):
        ring_qs[0].pair_arrived(k)

    def head_norm(value):
        scale = lax.rsqrt(jnp.mean(value * value, axis=1, keepdims=True) + norm_eps)
        return (value * scale).astype(jnp.bfloat16)

    own_rows = pl.ds(pl.multiple_of(home * tokens, 16), tokens)

    def proj(n):
        value = jnp.zeros((tokens, local_inner), f32)
        for f in range(fans):
            value += jnp.dot(
                norm[f],
                q_buf[f * cols : (f + 1) * cols, n * local_inner : (n + 1) * local_inner],
                preferred_element_type=f32,
            )
        return value

    key_raw = proj(1)
    for h in range(heads):
        at = slice(h * HEAD_DIM, (h + 1) * HEAD_DIM)
        kv[0, own_rows, at] = head_norm(key_raw[:, at])
    ring_kv.begin((0,))
    kv[1, own_rows, :] = proj(2).astype(jnp.bfloat16)
    ring_kv.begin((1,))
    query_raw = proj(0)
    for h in range(heads):
        at = slice(h * HEAD_DIM, (h + 1) * HEAD_DIM)
        q_hat[:, at] = head_norm(query_raw[:, at])
    acc[...] = jnp.zeros_like(acc)
    lsum[...] = jnp.zeros_like(lsum)

    def attend(zz):
        at = pl.ds(pl.multiple_of(zz * 2 * tokens, 16), 2 * tokens)

        def one_head(h, carry):
            cut = pl.ds(pl.multiple_of(h * HEAD_DIM, HEAD_DIM), HEAD_DIM)
            scores = lax.dot_general(
                q_hat[:, cut], kv[0, at, cut], (((1,), (1,)), ((), ())), preferred_element_type=f32
            ) * (1.0 / math.sqrt(HEAD_DIM))
            weights = jnp.exp(scores)
            part = weights[:, :128]
            for j in range(1, 2 * tokens // 128):
                part += weights[:, j * 128 : (j + 1) * 128]
            lsum[h] += part
            acc[:, cut] += jnp.dot(
                weights.astype(jnp.bfloat16), kv[1, at, cut], preferred_element_type=f32
            )
            return carry

        lax.fori_loop(0, heads, one_head, 0)

    ring_kv.pair_arrived(0)
    attend(p.z)
    for k in range(1, steps + 1):
        ring_kv.advance(k)
        if k == steps:
            pl.when(first)(lambda: swapped(4))
            pl.when(second)(lambda: swapped(6))
            ring_t.begin()
        if k > 1:
            ring_kv.pair_arrived(k - 1)
            for way in (0, 1):
                attend(ring_kv.zz(k - 1, way))
    ring_kv.pair_arrived(steps)
    attend(ring_kv.zz(steps, 0))

    for half in (0, 1):
        rr = half_rows[half]
        for h in range(heads):
            at = slice(h * HEAD_DIM, (h + 1) * HEAD_DIM)
            att[p.block, rr, at] = (
                acc[rr, at] / jnp.sum(lsum[h, rr, :], axis=1, keepdims=True)
            ).astype(jnp.bfloat16)
        over_att.begin(half)
    over_att.forward(0, 0)
    ring_t.advance(1)
    over_att.crossed(0)
    over_att.step(1, 0)
    over_att.forward(0, 1)
    ring_t.advance(2)
    over_att.crossed(1)
    over_att.step(1, 1)
    over_att.forward(1, 0)
    ring_t.advance(3)
    over_att.forward(1, 1)
    ring_t.advance(4)
    for k in range(steps + 1):
        ring_t.pair_arrived(k)

    def pass_branch(h):
        sends.start(
            lambda: (b_own.at[half_rows[h]], b_in.at[half_rows[h]]),
            lambda: one_send.at[2 + h],
            lambda: one_recv.at[2 + h],
            lambda: p.dev(g=0),
            second,
        )

    for h in (0, 1):
        rr = half_rows[h]
        over_att.arrived(h)
        value = jnp.zeros((tokens // 2, cols), f32)
        for j in range(fans):
            value += jnp.dot(
                att[j, rr, :], w_buf[1, j * wide : (j + 1) * wide, :], preferred_element_type=f32
            )
        b_own[rr, :] = value

        pl.when(second)(lambda: pass_branch(h))

    def pass_grad(h):
        sends.same(
            lambda h=h: grad.at[p.c, half_rows[h]],
            lambda: one_send.at[4 + h],
            lambda: one_recv.at[4 + h],
            lambda: p.dev(c=1 - p.c),
        )

    @pl.when(second)
    def _():
        swapped(1)
        swapped(5)
        predict(1)
        grad[p.c] = (
            (pred[...] - target_t[...].astype(f32)) * (1.0 / math.sqrt(tokens * 2 * zs))
        ).astype(jnp.bfloat16)

    @pl.when(first)
    def _():
        guess = noisy[p.block].astype(f32) + b_own[...]
        gap = jnp.sum(jnp.abs(gen[...].astype(f32) - guess))
        gap_f[p.block] = jnp.full((8, 128), gap, f32)
        gap_spread()

    for h in (0, 1):
        rr = half_rows[h]

        @pl.when(first)
        def _():
            wait_recv(b_in.at[rr], one_recv.at[2 + h])
            grad[p.c, rr, :] = (b_in[rr, :] - b_own[rr, :]).astype(jnp.bfloat16)

        pass_grad(h)

    @pl.when(p.kept)
    def _():
        wait_recv(hob.at[1 - p.c], ho_recv.at[5])

    for h in (0, 1):
        wait_recv(grad.at[1 - p.c, half_rows[h]], one_recv.at[4 + h])

    def partial(zz):
        at = pl.ds(pl.multiple_of(zz * wide, 128), wide)
        value = jnp.zeros((wide, cols), f32)
        for block in range(2):
            value += lax.dot_general(
                hob[block, :, at],
                grad[block],
                (((0,), (0,)), ((), ())),
                preferred_element_type=f32,
            )
        tmp[...] = value
        return tmp[pl.ds(pl.multiple_of(p.c * rows, 16), rows), :]

    def span(j, way):
        if j > 1:
            return slice(0, rows)
        return slice(0, rows // 2) if way == 0 else slice(rows // 2, rows)

    def rs_start(j, way):
        at = span(j, way)
        sends.start(
            lambda: (rs_send.at[j - 1, way, at], rs_recv.at[j - 1, way, at]),
            lambda: rs_ssem.at[j - 1, way],
            lambda: rs_rsem.at[j - 1, way],
            lambda: p.dev(z=p.zp if way == 0 else p.zm),
        )

    def rs_wait(j, way):
        wait_recv(rs_recv.at[j - 1, way, span(j, way)], rs_rsem.at[j - 1, way])

    def gap_step(j):
        if j == 1:
            gap_gathered()
            gap_z[p.z] = jnp.sum(gap_f[...], axis=0)
            for dz in range(1, zs):
                sends.same(
                    lambda: gap_z.at[p.z],
                    lambda dz=dz: gz_send.at[dz],
                    lambda dz=dz: gz_recv.at[dz],
                    lambda dz=dz: p.dev(z=lax.rem(p.z + dz, zs)),
                    first,
                )
        if j == 2:
            for dz in range(1, zs):
                wait_recv(gap_z.at[lax.rem(p.z + zs - dz, zs)], gz_recv.at[dz])
            gap_c[p.c] = jnp.sum(gap_z[...], axis=0)
            sends.same(
                lambda: gap_c.at[p.c],
                lambda: one_send.at[6],
                lambda: one_recv.at[6],
                lambda: p.dev(c=1 - p.c),
                first,
            )
        if j == 3:
            wait_recv(gap_c.at[1 - p.c], one_recv.at[6])

    far = partial(lax.rem(p.z + steps, zs))
    for way in (0, 1):
        rs_send[0, way, span(1, way), :] = far[span(1, way)].astype(jnp.bfloat16)
        rs_start(1, way)
    pl.when(first)(lambda: gap_step(1))
    for j in range(2, steps + 1):
        for way in (0, 1):
            dist = steps - j + 1
            there = lax.rem(p.z + dist, zs) if way == 0 else lax.rem(p.z + zs - dist, zs)
            mine = partial(there)
            rs_wait(j - 1, way)
            at = span(j - 1, way)
            rs_send[j - 1, way] = mine.astype(jnp.bfloat16)
            rs_send[j - 1, way, at, :] = (
                mine[at] + rs_recv[j - 2, way, at, :].astype(f32)
            ).astype(jnp.bfloat16)
            rs_start(j, way)
        if j == 2:
            pl.when(first)(lambda: gap_step(2))
    if steps == 1:
        pl.when(first)(lambda: gap_step(2))
    mine = partial(p.z)
    pl.when(first)(lambda: gap_step(3))
    acc_w = tmp.at[0:rows]
    acc_w[...] = mine
    for way in (0, 1):
        rs_wait(steps, way)
        at = span(steps, way)
        acc_w[at, :] = acc_w[at, :] + rs_recv[steps - 1, way, at, :].astype(f32)

    @pl.when(first)
    def _():
        gap = (gap_c[0] + gap_c[1])[0:1, 0:1] * (1.0 / (tokens * 2 * zs * fans * cols))
        wg_out[...] = (acc_w[...] * (1.0 / (gap + norm_eps))).astype(jnp.bfloat16)

    @pl.when(second)
    def _():
        wg_out[...] = acc_w[...].astype(jnp.bfloat16)

    @pl.when(p.moved)
    def _():
        sends.start(
            lambda: (wg_out, wg_in),
            lambda: one_send.at[7],
            lambda: one_recv.at[7],
            lambda: p.dev(a=p.c, c=p.a),
            p.moved,
        )
        wait_recv(wg_in, one_recv.at[7])
        out_ref[...] = wg_in[...].astype(f32)

    @pl.when(p.kept)
    def _():
        out_ref[...] = wg_out[...].astype(f32)

    sends.finish()


def weight_gradient(zs, xs, ts, bi, ho, ww, qw, to, noise, target, interpret=None):
    tokens, inner = ho.shape
    cols = bi.shape[1]
    rows = ww.shape[0]
    depth, triple = qw.shape
    local_inner = triple // 3
    heads = local_inner // HEAD_DIM
    seq, fans, steps = 2 * zs, 2 * xs, zs // 2
    b16, f32 = jnp.bfloat16, jnp.float32
    vmem, dma = pltpu.VMEM, pltpu.SemaphoreType.DMA
    scratch = [
        vmem((2, inner, cols), b16),
        vmem((seq * depth, triple), b16),
        vmem((2, tokens, inner), b16),
        vmem((tokens, cols), b16),
        vmem((tokens, cols), b16),
        vmem((tokens, cols), b16),
        vmem((tokens, cols), b16),
        vmem((tokens, cols), b16),
        vmem((fans, tokens, cols), b16),
        vmem((fans, tokens, cols), b16),
        vmem((2, seq * tokens, local_inner), b16),
        vmem((tokens, local_inner), b16),
        vmem((tokens, local_inner), f32),
        vmem((heads, tokens, 128), f32),
        vmem((fans, tokens, local_inner), b16),
        vmem((tokens, cols), f32),
        vmem((tokens, cols), f32),
        vmem((tokens, cols), f32),
        vmem((2, tokens, cols), b16),
        vmem((2 * rows, cols), f32),
        vmem((steps, 2, rows, cols), b16),
        vmem((steps, 2, rows, cols), b16),
        vmem((fans, 8, 128), f32),
        vmem((zs, 8, 128), f32),
        vmem((2, 8, 128), f32),
        vmem((rows, cols), b16),
        vmem((rows, cols), b16),
        dma((7,)),
        dma((7,)),
        dma((6,)),
        dma((6,)),
        dma((4, steps, 2, 2)),
        dma((4, steps, 2, 2)),
        dma((4, steps + 1, 2, 2)),
        dma((4, steps + 1, 2, 2)),
        dma((2, 18)),
        dma((2, 18)),
        dma((steps, 2)),
        dma((steps, 2)),
        dma((fans,)),
        dma((fans,)),
        dma((zs,)),
        dma((zs,)),
        dma((8,)),
        dma((8,)),
        dma((1,)),
    ]
    in_vmem = pl.BlockSpec(memory_space=pltpu.VMEM)
    return pl.pallas_call(
        functools.partial(kernel, zs, xs),
        out_shape=jax.ShapeDtypeStruct((rows, cols), f32),
        in_specs=[pl.BlockSpec(memory_space=pltpu.SMEM)] + [pl.BlockSpec(memory_space=pl.ANY)] * 7,
        out_specs=in_vmem,
        scratch_shapes=scratch,
        compiler_params=pltpu.CompilerParams(
            collective_id=0, has_side_effects=True, vmem_limit_bytes=62 * 1024 * 1024
        ),
        name="weight_gradient",
    )(ts, bi, ho, ww, qw, to, noise, target)


def body(
    block_input,
    head_outputs,
    out_master,
    first_moment,
    second_moment,
    score_qkv,
    teacher_out,
    noise,
    timestep,
    fake_target,
):
    zs, xs = lax.axis_size("seq") // 2, lax.axis_size("fsdp") // 2
    work_weight = out_master[0].astype(jnp.bfloat16)
    triple = score_qkv.shape[1] * score_qkv.shape[2]
    qw = score_qkv[0].reshape(triple, score_qkv.shape[3]).T
    weight_grad = weight_gradient(
        zs, xs, timestep, block_input[0], head_outputs[0], work_weight, qw, teacher_out, noise,
        fake_target,
    )
    new_first = 0.9 * first_moment[0] + 0.1 * weight_grad
    new_second = 0.95 * second_moment[0] + 0.05 * weight_grad * weight_grad
    new_master = out_master[0] - learn_rate * (new_first / first_fix) / (
        jnp.sqrt(new_second / second_fix) + 1e-08
    )
    return (new_master[None], new_first[None], new_second[None])


def solution(mesh):
    placed = (
        P("group", "seq", "fsdp"),
        P("group", "seq", None),
        P("group", "seq", "fsdp"),
        P("group", "seq", "fsdp"),
        P("group", "seq", "fsdp"),
        P("group", None, "fsdp", "seq"),
        P("seq", "fsdp"),
        P("seq", "fsdp"),
        P(),
        P("seq", "fsdp"),
    )
    return jax.shard_map(
        body,
        mesh=mesh,
        in_specs=placed,
        out_specs=(P("group", "seq", "fsdp"), P("group", "seq", "fsdp"), P("group", "seq", "fsdp")),
        check_vma=False,
    )
```

```python
import functools
import math

import jax
import jax.numpy as jnp
from jax import lax
from jax.experimental import pallas as pl
from jax.experimental.pallas import tpu as pltpu
from jax.sharding import PartitionSpec as P

D = 2560
HEAD_DIM = 128
MESH = pl.DeviceIdType.MESH

norm_eps = 1e-06
first_fix = 1.0 - 0.9**20
second_fix = 1.0 - 0.95**20
learn_rate = 0.003


class Sends:
    def __init__(self):
        self.open = []

    def start(self, ends, send_sem, recv_sem, device, when=None):
        def make():
            src, dst = ends()
            return pltpu.make_async_remote_copy(
                src_ref=src,
                dst_ref=dst,
                send_sem=send_sem(),
                recv_sem=recv_sem(),
                device_id=device(),
                device_id_type=MESH,
            )

        make().start()
        self.open.append((make, when))

    def same(self, ref, send_sem, recv_sem, device, when=None):
        def ends():
            here = ref()
            return here, here

        self.start(ends, send_sem, recv_sem, device, when)

    def take(self):
        taken, self.open = self.open, []
        return taken

    @staticmethod
    def finish(taken):
        for make, when in taken:
            if when is None:
                make().wait_send()
            else:
                pl.when(when)(lambda make=make: make().wait_send())


def wait_recv(dst, recv_sem):
    pltpu.make_async_copy(dst, dst, recv_sem).wait()


class Ring:
    def __init__(self, sends, place, buf, rows, sems, when=None, kind=None):
        self.sends, self.place, self.buf, self.rows, self.when = sends, place, buf, rows, when
        self.kind = kind
        self.ring_send, self.ring_recv, self.pair_send, self.pair_recv = sems
        self.steps = place.zs // 2

    def piece(self, zz, cc, half):
        if self.kind == 0:
            start = (2 * zz + cc) * self.rows
            return self.buf.at[half, pl.ds(pl.multiple_of(start, 16), self.rows)]
        each = self.rows // 2
        start = (2 * zz + cc) * self.rows + half * each
        if self.kind == 1:
            return self.buf.at[:, pl.ds(pl.multiple_of(start, 16), each), :]
        return self.buf.at[pl.ds(pl.multiple_of(start, 16), each)]

    def parts(self, k):
        if k < self.steps:
            return [(0, 0), (1, 0), (0, 1), (1, 1)]
        return [(0, 0), (1, 1)]

    def zz(self, k, way):
        p = self.place
        return lax.rem(p.z + p.zs - k, p.zs) if way == 0 else lax.rem(p.z + k, p.zs)

    def send(self, k, way, half):
        p = self.place
        self.sends.same(
            lambda: self.piece(self.zz(k - 1, way), p.c, half),
            lambda: self.ring_send.at[k - 1, way, half],
            lambda: self.ring_recv.at[k - 1, way, half],
            lambda: p.dev(z=p.zp if way == 0 else p.zm),
            self.when,
        )

    def pair(self, k, way, half):
        p = self.place
        self.sends.same(
            lambda: self.piece(self.zz(k, way), p.c, half),
            lambda: self.pair_send.at[k, way, half],
            lambda: self.pair_recv.at[k, way, half],
            lambda: p.dev(c=1 - p.c),
            self.when,
        )

    def begin(self, halves=(0, 1)):
        for way, half in self.parts(1):
            if half in halves:
                self.send(1, way, half)
        for half in halves:
            self.pair(0, 0, half)

    def advance(self, k, halves=(0, 1)):
        for way, half in self.parts(k):
            if half not in halves:
                continue
            wait_recv(
                self.piece(self.zz(k, way), self.place.c, half),
                self.ring_recv.at[k - 1, way, half],
            )
            if k < self.steps and (way, half) in self.parts(k + 1):
                self.send(k + 1, way, half)
            self.pair(k, way, half)

    def pair_arrived(self, k):
        for way, half in self.parts(k) if k else [(0, 0), (0, 1)]:
            wait_recv(
                self.piece(self.zz(k, way), 1 - self.place.c, half),
                self.pair_recv.at[k, way, half],
            )


class Across:
    def __init__(self, sends, place, buf, sems):
        self.sends, self.place, self.buf = sends, place, buf
        self.send_sem, self.recv_sem = sems
        self.rows = buf.shape[1]

    def part(self, dx, other, half, quarter=None):
        p = self.place
        block = 2 * lax.rem(p.x + dx + p.xs, p.xs) + (1 - p.a if other else p.a)
        each = self.rows // 2
        start = half * each
        if quarter is not None:
            each = each // 2
            start = start + quarter * each
        return self.buf.at[block, pl.ds(start, each)]

    def go(self, n, ref, device):
        self.sends.same(ref, lambda: self.send_sem.at[n], lambda: self.recv_sem.at[n], device)

    def beside(self, way):
        p = self.place
        return p.dev(x=lax.rem(p.x + (1 if way == 0 else p.xs - 1), p.xs))

    def cross(self, half):
        p = self.place
        self.go(half, lambda: self.part(0, False, half), lambda: p.dev(a=1 - p.a))

    def crossed(self, half):
        wait_recv(self.part(0, True, half), self.recv_sem.at[half])

    def step(self, other, half):
        for way in (0, 1):
            self.go(
                2 + 4 * other + 2 * half + way,
                lambda: self.part(0, other, half),
                lambda way=way: self.beside(way),
            )

    def forward(self, other, half):
        for way in (0, 1):
            near = -1 if way == 0 else 1
            n = 4 * other + 2 * half + way
            wait_recv(self.part(near, other, half), self.recv_sem.at[2 + n])
            self.go(
                10 + n,
                lambda near=near, way=way: self.part(near, other, half, way),
                lambda way=way: self.beside(way),
            )

    def arrived(self, half):
        for other in (0, 1):
            for way in (0, 1):
                n = 4 * other + 2 * half + way
                wait_recv(self.part(2, other, half, way), self.recv_sem.at[10 + n])

    def begin(self, half):
        self.cross(half)
        self.step(0, half)


class Place:
    def __init__(self, zs, xs):
        self.zs, self.xs = zs, xs
        seq, fsdp = lax.axis_index("seq"), lax.axis_index("fsdp")
        self.g = lax.axis_index("group")
        self.z, self.a = seq // 2, lax.rem(seq, 2)
        self.x, self.c = fsdp // 2, lax.rem(fsdp, 2)
        self.zp = lax.rem(self.z + 1, zs)
        self.zm = lax.rem(self.z + zs - 1, zs)
        self.block = 2 * self.x + self.a
        self.kept = self.a == self.c
        self.moved = self.a != self.c
        self.first = self.g == 0
        self.second = self.g == 1

    def dev(self, g=None, z=None, a=None, x=None, c=None):
        g = self.g if g is None else g
        z = self.z if z is None else z
        a = self.a if a is None else a
        x = self.x if x is None else x
        c = self.c if c is None else c
        return {"group": g, "seq": 2 * z + a, "fsdp": 2 * x + c}

    def fan(self):
        return [(2 * dx + da, dx, da) for dx in range(self.xs) for da in range(2) if dx or da]

    def beside(self, dx, da):
        return self.dev(x=lax.rem(self.x + dx, self.xs), a=lax.rem(self.a + da, 2))


def kernel(
    zs,
    xs,
    ts_ref,
    bi_ref,
    ho_ref,
    ww_ref,
    qw_ref,
    to_ref,
    noise_ref,
    target_ref,
    out_ref,
    w_buf,
    q_buf,
    hob,
    bi_t,
    noise_t,
    target_t,
    gen,
    gen_in,
    noisy,
    norm,
    kv,
    q_hat,
    acc,
    lsum,
    att,
    pred,
    b_own,
    b_in,
    grad,
    tmp,
    rs_send,
    rs_recv,
    gap_f,
    gap_z,
    gap_c,
    wg_out,
    wg_in,
    t_send,
    t_recv,
    ho_send,
    ho_recv,
    ring_send,
    ring_recv,
    pair_send,
    pair_recv,
    fan_send,
    fan_recv,
    rs_ssem,
    rs_rsem,
    gf_send,
    gf_recv,
    gz_send,
    gz_recv,
    one_send,
    one_recv,
    local_sem,
):
    p = Place(zs, xs)
    sends = Sends()
    tokens, inner = ho_ref.shape
    cols = bi_ref.shape[0]
    rows = ww_ref.shape[0]
    depth = qw_ref.shape[1]
    local_inner = q_hat.shape[1]
    heads = local_inner // HEAD_DIM
    steps = zs // 2
    fans = 2 * xs
    first = p.first
    second = p.second
    f32 = jnp.float32

    barrier = pltpu.get_barrier_semaphore()
    peers = [p.dev(z=lax.rem(p.z + dz, zs)) for dz in range(1, zs)]
    peers += [p.beside(dx, da) for _, dx, da in p.fan()]
    peers += [p.dev(c=1 - p.c), p.dev(g=1 - p.g), p.dev(a=1 - p.a, c=1 - p.c)]
    for peer in peers:
        pl.semaphore_signal(barrier, inc=1, device_id=peer, device_id_type=MESH)

    own_ho = pltpu.make_async_copy(ho_ref, hob.at[p.a], local_sem.at[0])
    own_ho.start()
    pl.semaphore_wait(barrier, len(peers))

    def rows_of(buf, each, at):
        return buf.at[pl.ds(pl.multiple_of(at * each, 16), each)]

    away, home = 2 * p.z + p.a, 2 * p.z + p.c
    swaps = [
        (ww_ref, lambda i: rows_of(w_buf.at[0], rows, i)),
        (bi_ref, lambda i: bi_t),
        (qw_ref, lambda i: q_buf.at[:, pl.ds(pl.multiple_of(i * depth, 16), depth), :]),
        (noise_ref, lambda i: noise_t),
        (to_ref, lambda i: rows_of(w_buf.at[1], rows, i)),
        (target_ref, lambda i: target_t),
        (ww_ref, lambda i: rows_of(w_buf.at[1], rows, i)),
    ]

    def swap(n, when):
        src, dst = swaps[n]

        @pl.when(p.kept)
        def _():
            pltpu.make_async_copy(src, dst(away), t_recv.at[n]).start()

        @pl.when(p.moved)
        def _():
            sends.start(
                lambda: (src, dst(away)),
                lambda: t_send.at[n],
                lambda: t_recv.at[n],
                lambda: p.dev(a=p.c, c=p.a),
                when,
            )

    first_moved, second_moved = first & p.moved, second & p.moved
    first_kept, second_kept = first & p.kept, second & p.kept

    def swapped(n):
        wait_recv(swaps[n][1](home), t_recv.at[n])

    share = tokens // xs

    def ho_rows(block, dx, half=None):
        start = lax.rem(p.x + dx + xs, xs) * share
        each = share
        if half is not None:
            each = share // 2
            start = start + half * each
        return hob.at[block, pl.ds(pl.multiple_of(start, 16), each)]

    def ho_cross(when):
        @pl.when(p.kept)
        def _():
            sends.start(
                lambda: (
                    ho_ref.at[pl.ds(pl.multiple_of(p.x * share, 16), share)],
                    ho_rows(p.a, 0),
                ),
                lambda: ho_send.at[0],
                lambda: ho_recv.at[0],
                lambda: p.dev(a=1 - p.a),
                when,
            )

    def beside(way):
        return p.dev(x=lax.rem(p.x + (1 if way == 0 else xs - 1), xs))

    def ho_step(when):
        @pl.when(p.moved)
        def _():
            wait_recv(ho_rows(p.c, 0), ho_recv.at[0])
            for way in (0, 1):
                sends.same(
                    lambda: ho_rows(p.c, 0),
                    lambda way=way: ho_send.at[1 + way],
                    lambda way=way: ho_recv.at[1 + way],
                    lambda way=way: beside(way),
                    when,
                )

    def ho_forward(when):
        @pl.when(p.moved)
        def _():
            for way in (0, 1):
                near = -1 if way == 0 else 1
                wait_recv(ho_rows(p.c, near), ho_recv.at[1 + way])
                sends.same(
                    lambda near=near, way=way: ho_rows(p.c, near, way),
                    lambda way=way: ho_send.at[3 + way],
                    lambda way=way: ho_recv.at[3 + way],
                    lambda way=way: beside(way),
                    when,
                )

    def ho_arrived(when):
        @pl.when(p.moved)
        def _():
            for way in (0, 1):
                wait_recv(ho_rows(p.c, 2, way), ho_recv.at[3 + way])
            sends.same(
                lambda: hob.at[p.c],
                lambda: ho_send.at[5],
                lambda: ho_recv.at[5],
                lambda: p.dev(c=1 - p.c),
                when,
            )

    def ring(buf, each, n, when=None, kind=None):
        sems = (ring_send.at[n], ring_recv.at[n], pair_send.at[n], pair_recv.at[n])
        return Ring(sends, p, buf, each, sems, when, kind)

    ring_w = ring(w_buf.at[0], rows, 0, first)
    ring_qs = [ring(q_buf, depth, 1, first, 1), ring(q_buf, depth, 1, second, 1)]
    ring_kv = ring(kv, tokens, 2, kind=0)
    ring_ts = [ring(w_buf.at[1], rows, 3, first), ring(w_buf.at[1], rows, 3, second)]
    over_noisy = Across(sends, p, noisy, (fan_send.at[0], fan_recv.at[0]))
    over_att = Across(sends, p, att, (fan_send.at[1], fan_recv.at[1]))

    wide = 2 * rows

    def project(lhs, which, out):
        def part(j, carry):
            at = pl.ds(pl.multiple_of(j * wide, 128), wide)
            out[...] += jnp.dot(
                lhs(j, at), w_buf[which, at, :], preferred_element_type=f32
            )
            return carry

        lax.fori_loop(0, inner // wide, part, 0)

    def gap_spread():
        for rank, dx, da in p.fan():
            sends.same(
                lambda: gap_f.at[p.block],
                lambda rank=rank: gf_send.at[rank],
                lambda rank=rank: gf_recv.at[rank],
                lambda dx=dx, da=da: p.beside(dx, da),
                first,
            )

    def gap_gathered():
        for rank, dx, da in p.fan():
            block = 2 * lax.rem(p.x + xs - dx, xs) + lax.rem(p.a + da, 2)
            wait_recv(gap_f.at[block], gf_recv.at[rank])

    def predict(which):
        pred[...] = jnp.zeros_like(pred)
        project(lambda j, at: hob[p.c, :, at], which, pred)

    half_rows = [slice(0, tokens // 2), slice(tokens // 2, tokens)]
    half_cols = [slice(0, cols // 2), slice(cols // 2, cols)]

    @pl.when(first)
    def _():
        ring_q = ring_qs[0]
        swap(0, first_moved)
        ho_cross(first_kept)
        swap(1, first_moved)
        swapped(0)
        ring_w.begin()
        swap(3, first_moved)
        swap(2, first_moved)
        ring_w.advance(1)
        ho_step(first_moved)
        ring_w.advance(2)
        ring_w.advance(3)
        ho_forward(first_moved)
        swapped(2)
        ring_q.begin()
        swap(4, first_moved)
        ring_w.advance(4)
        own_ho.wait()
        ho_arrived(first_moved)
        for k in range(steps + 1):
            ring_w.pair_arrived(k)
        swapped(1)
        predict(0)
        gen[...] = (bi_t[...].astype(f32) + pred[...].T).astype(jnp.bfloat16)
        for h in (0, 1):
            sends.start(
                lambda h=h: (gen.at[half_cols[h]], gen_in.at[half_cols[h]]),
                lambda h=h: one_send.at[h],
                lambda h=h: one_recv.at[h],
                lambda: p.dev(g=1),
                first,
            )

    @pl.when(second)
    def _():
        ring_q = ring_qs[1]
        swap(2, second_moved)
        swapped(2)
        ring_q.begin()
        swap(3, second_moved)
        ring_q.advance(1)
        swap(6, second_moved)
        ring_q.advance(2)
        ho_cross(second_kept)
        swap(1, second_moved)
        ring_q.advance(3)
        ho_step(second_moved)
        swap(5, second_moved)
        ring_q.advance(4)
        ho_forward(second_moved)
        own_ho.wait()
        swapped(6)
        ring_ts[1].begin()

    swapped(3)
    level = ts_ref[0].astype(f32) / 1000.0
    for h in (0, 1):
        at = half_cols[h]

        @pl.when(second)
        def _():
            wait_recv(gen_in.at[at], one_recv.at[h])
            gen[at, :] = gen_in[at, :]

        noisy[p.block, at, :] = (
            (1.0 - level) * gen[at, :].astype(f32) + level * noise_t[at, :].astype(f32)
        ).astype(jnp.bfloat16)
        over_noisy.begin(h)

    def first_q(k):
        pl.when(first)(lambda: ring_qs[0].advance(k))
        pl.when(second)(lambda: ring_ts[1].advance(k))

    def first_t(k):
        pl.when(first)(lambda: ring_ts[0].advance(k))

    @pl.when(first)
    def _():
        pred[...] = (gen[...].astype(f32) - noisy[p.block].astype(f32)).T

    over_noisy.forward(0, 0)
    first_q(1)
    over_noisy.crossed(0)
    over_noisy.step(1, 0)
    over_noisy.forward(0, 1)
    over_noisy.crossed(1)
    over_noisy.step(1, 1)
    first_q(2)
    over_noisy.forward(1, 0)
    over_noisy.forward(1, 1)
    first_q(3)
    over_noisy.arrived(0)
    over_noisy.arrived(1)

    @pl.when(second)
    def _():
        ho_arrived(second_moved)

    total = jnp.zeros((1, tokens), f32)
    for f in range(fans):
        block = noisy[f].astype(f32)
        total += jnp.sum(block * block, axis=0, keepdims=True)
    factor = lax.rsqrt(total * (1.0 / (fans * cols)) + norm_eps)
    for f in range(fans):
        norm[f * cols : (f + 1) * cols, :] = (noisy[f].astype(f32) * factor).astype(jnp.bfloat16)
    first_q(4)
    for k in range(steps + 1):
        ring_qs[0].pair_arrived(k)

    def head_norm(value):
        scale = lax.rsqrt(jnp.mean(value * value, axis=1, keepdims=True) + norm_eps)
        return (value * scale).astype(jnp.bfloat16)

    own_rows = pl.ds(pl.multiple_of(home * tokens, 16), tokens)

    def proj(n):
        return lax.dot_general(
            norm[...], q_buf[n], (((0,), (0,)), ((), ())), preferred_element_type=f32
        )

    key_raw = proj(1)
    for h in range(heads):
        at = slice(h * HEAD_DIM, (h + 1) * HEAD_DIM)
        kv[0, own_rows, at] = head_norm(key_raw[:, at])
    ring_kv.begin((0,))
    kv[1, own_rows, :] = proj(2).astype(jnp.bfloat16)
    ring_kv.begin((1,))
    query_raw = proj(0)
    for h in range(heads):
        at = slice(h * HEAD_DIM, (h + 1) * HEAD_DIM)
        q_hat[:, at] = head_norm(query_raw[:, at])
    acc[...] = jnp.zeros_like(acc)
    lsum[...] = jnp.zeros_like(lsum)

    def attend(zz):
        at = pl.ds(pl.multiple_of(zz * 2 * tokens, 16), 2 * tokens)

        def one_head(h, carry):
            cut = pl.ds(pl.multiple_of(h * HEAD_DIM, HEAD_DIM), HEAD_DIM)
            scores = lax.dot_general(
                q_hat[:, cut], kv[0, at, cut], (((1,), (1,)), ((), ())), preferred_element_type=f32
            ) * (1.0 / math.sqrt(HEAD_DIM))
            weights = jnp.exp(scores)
            part = weights[:, :128]
            for j in range(1, 2 * tokens // 128):
                part += weights[:, j * 128 : (j + 1) * 128]
            lsum[h] += part
            acc[:, cut] += jnp.dot(
                weights.astype(jnp.bfloat16), kv[1, at, cut], preferred_element_type=f32
            )
            return carry

        lax.fori_loop(0, heads, one_head, 0)

    ring_kv.pair_arrived(0)
    attend(p.z)
    for k in range(1, steps + 1):
        for half in (0, 1):
            ring_kv.advance(k, (half,))
            if k > 1:
                if half == 0:
                    ring_kv.pair_arrived(k - 1)
                attend(ring_kv.zz(k - 1, half))
        if k == steps:

            @pl.when(first)
            def _():
                swapped(4)
                ring_ts[0].begin()

    ring_kv.pair_arrived(steps)
    attend(ring_kv.zz(steps, 0))

    for half in (0, 1):
        rr = half_rows[half]
        for h in range(heads):
            at = slice(h * HEAD_DIM, (h + 1) * HEAD_DIM)
            att[p.block, rr, at] = (
                acc[rr, at] / jnp.sum(lsum[h, rr, :], axis=1, keepdims=True)
            ).astype(jnp.bfloat16)
        over_att.begin(half)
    over_att.forward(0, 0)
    first_t(1)
    over_att.crossed(0)
    over_att.step(1, 0)
    over_att.forward(0, 1)
    first_t(2)
    over_att.crossed(1)
    over_att.step(1, 1)
    over_att.forward(1, 0)
    first_t(3)
    over_att.forward(1, 1)
    first_t(4)
    for k in range(steps + 1):
        ring_ts[0].pair_arrived(k)

    early = sends.take()

    def pass_branch(h):
        sends.start(
            lambda: (b_own.at[half_rows[h]], b_in.at[half_rows[h]]),
            lambda: one_send.at[2 + h],
            lambda: one_recv.at[2 + h],
            lambda: p.dev(g=0),
            second,
        )

    for h in (0, 1):
        rr = half_rows[h]
        over_att.arrived(h)
        value = jnp.zeros((tokens // 2, cols), f32)
        for j in range(fans):
            value += jnp.dot(
                att[j, rr, :], w_buf[1, j * wide : (j + 1) * wide, :], preferred_element_type=f32
            )
        b_own[rr, :] = value

        pl.when(second)(lambda: pass_branch(h))

    def pass_grad(h):
        sends.same(
            lambda h=h: grad.at[p.c, half_rows[h]],
            lambda: one_send.at[4 + h],
            lambda: one_recv.at[4 + h],
            lambda: p.dev(c=1 - p.c),
        )

    @pl.when(second)
    def _():
        swapped(1)
        swapped(5)
        predict(1)
        grad[p.c] = (
            (pred[...] + (bi_t[...].astype(f32) - target_t[...].astype(f32)).T) * (1.0 / math.sqrt(tokens * 2 * zs))
        ).astype(jnp.bfloat16)

    @pl.when(first)
    def _():
        gap = jnp.sum(jnp.abs(pred[...] - b_own[...]))
        gap_f[p.block] = jnp.full((8, 128), gap, f32)
        gap_spread()

    sends.finish(early)
    for h in (0, 1):
        rr = half_rows[h]

        @pl.when(first)
        def _():
            wait_recv(b_in.at[rr], one_recv.at[2 + h])
            grad[p.c, rr, :] = (b_in[rr, :] - b_own[rr, :]).astype(jnp.bfloat16)

        pass_grad(h)

    @pl.when(p.kept)
    def _():
        wait_recv(hob.at[1 - p.c], ho_recv.at[5])

    for h in (0, 1):
        wait_recv(grad.at[1 - p.c, half_rows[h]], one_recv.at[4 + h])

    def partial(zz):
        at = pl.ds(pl.multiple_of(zz * wide, 128), wide)
        value = jnp.zeros((wide, cols), f32)
        for block in range(2):
            value += lax.dot_general(
                hob[block, :, at],
                grad[block],
                (((0,), (0,)), ((), ())),
                preferred_element_type=f32,
            )
        tmp[...] = value
        return tmp[pl.ds(pl.multiple_of(p.c * rows, 16), rows), :]

    def span(j, way):
        if j > 1:
            return slice(0, rows)
        return slice(0, rows // 2) if way == 0 else slice(rows // 2, rows)

    def rs_start(j, way):
        at = span(j, way)
        sends.start(
            lambda: (rs_send.at[j - 1, way, at], rs_recv.at[j - 1, way, at]),
            lambda: rs_ssem.at[j - 1, way],
            lambda: rs_rsem.at[j - 1, way],
            lambda: p.dev(z=p.zp if way == 0 else p.zm),
        )

    def rs_wait(j, way):
        wait_recv(rs_recv.at[j - 1, way, span(j, way)], rs_rsem.at[j - 1, way])

    def gap_step(j):
        if j == 1:
            gap_gathered()
            gap_z[p.z] = jnp.sum(gap_f[...], axis=0)
            for dz in range(1, zs):
                sends.same(
                    lambda: gap_z.at[p.z],
                    lambda dz=dz: gz_send.at[dz],
                    lambda dz=dz: gz_recv.at[dz],
                    lambda dz=dz: p.dev(z=lax.rem(p.z + dz, zs)),
                    first,
                )
        if j == 2:
            for dz in range(1, zs):
                wait_recv(gap_z.at[lax.rem(p.z + zs - dz, zs)], gz_recv.at[dz])
            gap_c[p.c] = jnp.sum(gap_z[...], axis=0)
            sends.same(
                lambda: gap_c.at[p.c],
                lambda: one_send.at[6],
                lambda: one_recv.at[6],
                lambda: p.dev(c=1 - p.c),
                first,
            )
        if j == 3:
            wait_recv(gap_c.at[1 - p.c], one_recv.at[6])

    far = partial(lax.rem(p.z + steps, zs))
    for way in (0, 1):
        rs_send[0, way, span(1, way), :] = far[span(1, way)].astype(jnp.bfloat16)
        rs_start(1, way)
    pl.when(first)(lambda: gap_step(1))
    for j in range(2, steps + 1):
        for way in (0, 1):
            dist = steps - j + 1
            there = lax.rem(p.z + dist, zs) if way == 0 else lax.rem(p.z + zs - dist, zs)
            mine = partial(there)
            rs_wait(j - 1, way)
            at = span(j - 1, way)
            rs_send[j - 1, way] = mine.astype(jnp.bfloat16)
            rs_send[j - 1, way, at, :] = (
                mine[at] + rs_recv[j - 2, way, at, :].astype(f32)
            ).astype(jnp.bfloat16)
            rs_start(j, way)
        if j == 2:
            pl.when(first)(lambda: gap_step(2))
    if steps == 1:
        pl.when(first)(lambda: gap_step(2))
    mine = partial(p.z)
    pl.when(first)(lambda: gap_step(3))
    acc_w = tmp.at[0:rows]
    acc_w[...] = mine
    for way in (0, 1):
        rs_wait(steps, way)
        at = span(steps, way)
        acc_w[at, :] = acc_w[at, :] + rs_recv[steps - 1, way, at, :].astype(f32)

    @pl.when(first)
    def _():
        gap = (gap_c[0] + gap_c[1])[0:1, 0:1] * (1.0 / (tokens * 2 * zs * fans * cols))
        wg_out[...] = (acc_w[...] * (1.0 / (gap + norm_eps))).astype(jnp.bfloat16)

    @pl.when(second)
    def _():
        wg_out[...] = acc_w[...].astype(jnp.bfloat16)

    @pl.when(p.moved)
    def _():
        sends.start(
            lambda: (wg_out, wg_in),
            lambda: one_send.at[7],
            lambda: one_recv.at[7],
            lambda: p.dev(a=p.c, c=p.a),
            p.moved,
        )
        wait_recv(wg_in, one_recv.at[7])
        out_ref[...] = wg_in[...].astype(f32)

    @pl.when(p.kept)
    def _():
        out_ref[...] = wg_out[...].astype(f32)

    sends.finish(sends.take())


def weight_gradient(zs, xs, ts, bi, ho, ww, qw, to, noise, target, interpret=None):
    tokens, inner = ho.shape
    cols = bi.shape[0]
    rows = ww.shape[0]
    depth, local_inner = qw.shape[1:]
    heads = local_inner // HEAD_DIM
    seq, fans, steps = 2 * zs, 2 * xs, zs // 2
    b16, f32 = jnp.bfloat16, jnp.float32
    vmem, dma = pltpu.VMEM, pltpu.SemaphoreType.DMA
    scratch = [
        vmem((2, inner, cols), b16),
        vmem((3, seq * depth, local_inner), b16),
        vmem((2, tokens, inner), b16),
        vmem((cols, tokens), b16),
        vmem((cols, tokens), b16),
        vmem((cols, tokens), b16),
        vmem((cols, tokens), b16),
        vmem((cols, tokens), b16),
        vmem((fans, cols, tokens), b16),
        vmem((fans * cols, tokens), b16),
        vmem((2, seq * tokens, local_inner), b16),
        vmem((tokens, local_inner), b16),
        vmem((tokens, local_inner), f32),
        vmem((heads, tokens, 128), f32),
        vmem((fans, tokens, local_inner), b16),
        vmem((tokens, cols), f32),
        vmem((tokens, cols), f32),
        vmem((tokens, cols), f32),
        vmem((2, tokens, cols), b16),
        vmem((2 * rows, cols), f32),
        vmem((steps, 2, rows, cols), b16),
        vmem((steps, 2, rows, cols), b16),
        vmem((fans, 8, 128), f32),
        vmem((zs, 8, 128), f32),
        vmem((2, 8, 128), f32),
        vmem((rows, cols), b16),
        vmem((rows, cols), b16),
        dma((7,)),
        dma((7,)),
        dma((6,)),
        dma((6,)),
        dma((4, steps, 2, 2)),
        dma((4, steps, 2, 2)),
        dma((4, steps + 1, 2, 2)),
        dma((4, steps + 1, 2, 2)),
        dma((2, 18)),
        dma((2, 18)),
        dma((steps, 2)),
        dma((steps, 2)),
        dma((fans,)),
        dma((fans,)),
        dma((zs,)),
        dma((zs,)),
        dma((8,)),
        dma((8,)),
        dma((1,)),
    ]
    in_vmem = pl.BlockSpec(memory_space=pltpu.VMEM)
    return pl.pallas_call(
        functools.partial(kernel, zs, xs),
        out_shape=jax.ShapeDtypeStruct((rows, cols), f32),
        in_specs=[pl.BlockSpec(memory_space=pltpu.SMEM)] + [pl.BlockSpec(memory_space=pl.ANY)] * 7,
        out_specs=in_vmem,
        scratch_shapes=scratch,
        compiler_params=pltpu.CompilerParams(
            collective_id=0, has_side_effects=True, vmem_limit_bytes=62 * 1024 * 1024
        ),
        name="weight_gradient",
    )(ts, bi, ho, ww, qw, to, noise, target)


def body(
    block_input,
    head_outputs,
    out_master,
    first_moment,
    second_moment,
    score_qkv,
    teacher_out,
    noise,
    timestep,
    fake_target,
):
    zs, xs = lax.axis_size("seq") // 2, lax.axis_size("fsdp") // 2
    work_weight = out_master[0].astype(jnp.bfloat16)
    qw = score_qkv[0].transpose(0, 2, 1)
    weight_grad = weight_gradient(
        zs, xs, timestep, block_input[0].T, head_outputs[0], work_weight, qw, teacher_out, noise.T,
        fake_target.T,
    )
    new_first = 0.9 * first_moment[0] + 0.1 * weight_grad
    new_second = 0.95 * second_moment[0] + 0.05 * weight_grad * weight_grad
    new_master = out_master[0] - learn_rate * (new_first / first_fix) / (
        jnp.sqrt(new_second / second_fix) + 1e-08
    )
    return (new_master[None], new_first[None], new_second[None])


def solution(mesh):
    placed = (
        P("group", "seq", "fsdp"),
        P("group", "seq", None),
        P("group", "seq", "fsdp"),
        P("group", "seq", "fsdp"),
        P("group", "seq", "fsdp"),
        P("group", None, "fsdp", "seq"),
        P("seq", "fsdp"),
        P("seq", "fsdp"),
        P(),
        P("seq", "fsdp"),
    )
    return jax.shard_map(
        body,
        mesh=mesh,
        in_specs=placed,
        out_specs=(P("group", "seq", "fsdp"), P("group", "seq", "fsdp"), P("group", "seq", "fsdp")),
        check_vma=False,
    )
```

```python
import functools
import math

import jax
import jax.numpy as jnp
from jax import lax
from jax.experimental import pallas as pl
from jax.experimental.pallas import tpu as pltpu
from jax.sharding import PartitionSpec as P

D = 2560
HEAD_DIM = 128
MESH = pl.DeviceIdType.MESH

norm_eps = 1e-06
first_fix = 1.0 - 0.9**20
second_fix = 1.0 - 0.95**20
learn_rate = 0.003


class Sends:
    def __init__(self):
        self.open = []

    def start(self, ends, send_sem, recv_sem, device, when=None):
        def make():
            src, dst = ends()
            return pltpu.make_async_remote_copy(
                src_ref=src,
                dst_ref=dst,
                send_sem=send_sem(),
                recv_sem=recv_sem(),
                device_id=device(),
                device_id_type=MESH,
            )

        make().start()
        self.open.append((make, when))

    def same(self, ref, send_sem, recv_sem, device, when=None):
        def ends():
            here = ref()
            return here, here

        self.start(ends, send_sem, recv_sem, device, when)

    def take(self):
        taken, self.open = self.open, []
        return taken

    @staticmethod
    def finish(taken):
        for make, when in taken:
            if when is None:
                make().wait_send()
            else:
                pl.when(when)(lambda make=make: make().wait_send())


def wait_recv(dst, recv_sem):
    pltpu.make_async_copy(dst, dst, recv_sem).wait()


class Ring:
    def __init__(self, sends, place, buf, rows, sems, when=None, kind=None):
        self.sends, self.place, self.buf, self.rows, self.when = sends, place, buf, rows, when
        self.kind = kind
        self.ring_send, self.ring_recv, self.pair_send, self.pair_recv = sems
        self.steps = place.zs // 2

    def piece(self, zz, cc, half):
        if self.kind == 0:
            start = (2 * zz + cc) * self.rows
            return self.buf.at[half, pl.ds(pl.multiple_of(start, 16), self.rows)]
        each = self.rows // 2
        start = (2 * zz + cc) * self.rows + half * each
        if self.kind == 1:
            return self.buf.at[:, pl.ds(pl.multiple_of(start, 16), each), :]
        return self.buf.at[pl.ds(pl.multiple_of(start, 16), each)]

    def parts(self, k):
        if k < self.steps:
            return [(0, 0), (1, 0), (0, 1), (1, 1)]
        return [(0, 0), (1, 1)]

    def zz(self, k, way):
        p = self.place
        return lax.rem(p.z + p.zs - k, p.zs) if way == 0 else lax.rem(p.z + k, p.zs)

    def send(self, k, way, half):
        p = self.place
        self.sends.same(
            lambda: self.piece(self.zz(k - 1, way), p.c, half),
            lambda: self.ring_send.at[k - 1, way, half],
            lambda: self.ring_recv.at[k - 1, way, half],
            lambda: p.dev(z=p.zp if way == 0 else p.zm),
            self.when,
        )

    def pair(self, k, way, half):
        p = self.place
        self.sends.same(
            lambda: self.piece(self.zz(k, way), p.c, half),
            lambda: self.pair_send.at[k, way, half],
            lambda: self.pair_recv.at[k, way, half],
            lambda: p.dev(c=1 - p.c),
            self.when,
        )

    def begin(self, halves=(0, 1)):
        for way, half in self.parts(1):
            if half in halves:
                self.send(1, way, half)
        for half in halves:
            self.pair(0, 0, half)

    def advance(self, k, halves=(0, 1)):
        for way, half in self.parts(k):
            if half not in halves:
                continue
            wait_recv(
                self.piece(self.zz(k, way), self.place.c, half),
                self.ring_recv.at[k - 1, way, half],
            )
            if k < self.steps and (way, half) in self.parts(k + 1):
                self.send(k + 1, way, half)
            self.pair(k, way, half)

    def pair_arrived(self, k):
        for way, half in self.parts(k) if k else [(0, 0), (0, 1)]:
            wait_recv(
                self.piece(self.zz(k, way), 1 - self.place.c, half),
                self.pair_recv.at[k, way, half],
            )


class Across:
    def __init__(self, sends, place, buf, sems):
        self.sends, self.place, self.buf = sends, place, buf
        self.send_sem, self.recv_sem = sems
        self.rows = buf.shape[1]

    def part(self, dx, other, half, quarter=None):
        p = self.place
        block = 2 * lax.rem(p.x + dx + p.xs, p.xs) + (1 - p.a if other else p.a)
        each = self.rows // 2
        start = half * each
        if quarter is not None:
            each = each // 2
            start = start + quarter * each
        return self.buf.at[block, pl.ds(start, each)]

    def go(self, n, ref, device):
        self.sends.same(ref, lambda: self.send_sem.at[n], lambda: self.recv_sem.at[n], device)

    def beside(self, way):
        p = self.place
        return p.dev(x=lax.rem(p.x + (1 if way == 0 else p.xs - 1), p.xs))

    def cross(self, half):
        p = self.place
        self.go(half, lambda: self.part(0, False, half), lambda: p.dev(a=1 - p.a))

    def crossed(self, half):
        wait_recv(self.part(0, True, half), self.recv_sem.at[half])

    def step(self, other, half):
        for way in (0, 1):
            self.go(
                2 + 4 * other + 2 * half + way,
                lambda: self.part(0, other, half),
                lambda way=way: self.beside(way),
            )

    def forward(self, other, half):
        for way in (0, 1):
            near = -1 if way == 0 else 1
            n = 4 * other + 2 * half + way
            wait_recv(self.part(near, other, half), self.recv_sem.at[2 + n])
            self.go(
                10 + n,
                lambda near=near, way=way: self.part(near, other, half, way),
                lambda way=way: self.beside(way),
            )

    def arrived(self, half):
        for other in (0, 1):
            for way in (0, 1):
                n = 4 * other + 2 * half + way
                wait_recv(self.part(2, other, half, way), self.recv_sem.at[10 + n])

    def begin(self, half):
        self.cross(half)
        self.step(0, half)


class Place:
    def __init__(self, zs, xs):
        self.zs, self.xs = zs, xs
        seq, fsdp = lax.axis_index("seq"), lax.axis_index("fsdp")
        self.g = lax.axis_index("group")
        self.z, self.a = seq // 2, lax.rem(seq, 2)
        self.x, self.c = fsdp // 2, lax.rem(fsdp, 2)
        self.zp = lax.rem(self.z + 1, zs)
        self.zm = lax.rem(self.z + zs - 1, zs)
        self.block = 2 * self.x + self.a
        self.kept = self.a == self.c
        self.moved = self.a != self.c
        self.first = self.g == 0
        self.second = self.g == 1

    def dev(self, g=None, z=None, a=None, x=None, c=None):
        g = self.g if g is None else g
        z = self.z if z is None else z
        a = self.a if a is None else a
        x = self.x if x is None else x
        c = self.c if c is None else c
        return {"group": g, "seq": 2 * z + a, "fsdp": 2 * x + c}

    def fan(self):
        return [(2 * dx + da, dx, da) for dx in range(self.xs) for da in range(2) if dx or da]

    def beside(self, dx, da):
        return self.dev(x=lax.rem(self.x + dx, self.xs), a=lax.rem(self.a + da, 2))


def kernel(
    zs,
    xs,
    ts_ref,
    bi_ref,
    ho_ref,
    ww_ref,
    qw_ref,
    to_ref,
    noise_ref,
    target_ref,
    out_ref,
    w_buf,
    q_buf,
    hob,
    bi_t,
    noise_t,
    target_t,
    gen,
    gen_in,
    noisy,
    norm,
    kv,
    q_hat,
    acc,
    lsum,
    att,
    pred,
    gap_d,
    grad_s,
    hob_in,
    b_own,
    b_in,
    grad,
    tmp,
    rs_send,
    rs_recv,
    gap_f,
    gap_z,
    gap_c,
    wg_out,
    wg_in,
    t_send,
    t_recv,
    ho_send,
    ho_recv,
    ring_send,
    ring_recv,
    pair_send,
    pair_recv,
    fan_send,
    fan_recv,
    rs_ssem,
    rs_rsem,
    gf_send,
    gf_recv,
    gz_send,
    gz_recv,
    one_send,
    one_recv,
    local_sem,
):
    p = Place(zs, xs)
    sends = Sends()
    tokens, inner = ho_ref.shape
    cols = bi_ref.shape[0]
    rows = ww_ref.shape[0]
    depth = qw_ref.shape[1]
    local_inner = q_hat.shape[1]
    heads = local_inner // HEAD_DIM
    steps = zs // 2
    fans = 2 * xs
    first = p.first
    second = p.second
    f32 = jnp.float32

    barrier = pltpu.get_barrier_semaphore()
    peers = [p.dev(z=lax.rem(p.z + dz, zs)) for dz in range(1, zs)]
    peers += [p.beside(dx, da) for _, dx, da in p.fan()]
    peers += [p.dev(c=1 - p.c), p.dev(g=1 - p.g), p.dev(a=1 - p.a, c=1 - p.c)]
    peers += [p.dev(g=1 - p.g, a=1 - p.a, c=1 - p.c)]
    for peer in peers:
        pl.semaphore_signal(barrier, inc=1, device_id=peer, device_id_type=MESH)

    own_ho = pltpu.make_async_copy(ho_ref, hob.at[p.a], local_sem.at[0])
    own_ho.start()
    pl.semaphore_wait(barrier, len(peers))

    def rows_of(buf, each, at):
        return buf.at[pl.ds(pl.multiple_of(at * each, 16), each)]

    away, home = 2 * p.z + p.a, 2 * p.z + p.c
    swaps = [
        (ww_ref, lambda i: rows_of(w_buf.at[0], rows, i)),
        (bi_ref, lambda i: bi_t),
        (qw_ref, lambda i: q_buf.at[:, pl.ds(pl.multiple_of(i * depth, 16), depth), :]),
        (noise_ref, lambda i: noise_t),
        (to_ref, lambda i: rows_of(w_buf.at[1], rows, i)),
        (target_ref, lambda i: target_t),
        (ww_ref, lambda i: rows_of(w_buf.at[1], rows, i)),
    ]

    def swap(n, when):
        src, dst = swaps[n]

        @pl.when(p.kept)
        def _():
            pltpu.make_async_copy(src, dst(away), t_recv.at[n]).start()

        @pl.when(p.moved)
        def _():
            sends.start(
                lambda: (src, dst(away)),
                lambda: t_send.at[n],
                lambda: t_recv.at[n],
                lambda: p.dev(a=p.c, c=p.a),
                when,
            )

    first_moved, second_moved = first & p.moved, second & p.moved
    first_kept, second_kept = first & p.kept, second & p.kept

    def swapped(n):
        wait_recv(swaps[n][1](home), t_recv.at[n])

    share = tokens // xs

    def ho_rows(block, dx, half=None):
        start = lax.rem(p.x + dx + xs, xs) * share
        each = share
        if half is not None:
            each = share // 2
            start = start + half * each
        return hob.at[block, pl.ds(pl.multiple_of(start, 16), each)]

    def ho_cross(when):
        @pl.when(p.kept)
        def _():
            sends.start(
                lambda: (
                    ho_ref.at[pl.ds(pl.multiple_of(p.x * share, 16), share)],
                    ho_rows(p.a, 0),
                ),
                lambda: ho_send.at[0],
                lambda: ho_recv.at[0],
                lambda: p.dev(a=1 - p.a),
                when,
            )

    def beside(way):
        return p.dev(x=lax.rem(p.x + (1 if way == 0 else xs - 1), xs))

    def ho_step(when):
        @pl.when(p.moved)
        def _():
            wait_recv(ho_rows(p.c, 0), ho_recv.at[0])
            for way in (0, 1):
                sends.same(
                    lambda: ho_rows(p.c, 0),
                    lambda way=way: ho_send.at[1 + way],
                    lambda way=way: ho_recv.at[1 + way],
                    lambda way=way: beside(way),
                    when,
                )

    def ho_forward(when):
        @pl.when(p.moved)
        def _():
            for way in (0, 1):
                near = -1 if way == 0 else 1
                wait_recv(ho_rows(p.c, near), ho_recv.at[1 + way])
                sends.same(
                    lambda near=near, way=way: ho_rows(p.c, near, way),
                    lambda way=way: ho_send.at[3 + way],
                    lambda way=way: ho_recv.at[3 + way],
                    lambda way=way: beside(way),
                    when,
                )

    def ho_arrived():
        @pl.when(p.moved)
        def _():
            for way in (0, 1):
                wait_recv(ho_rows(p.c, 2, way), ho_recv.at[3 + way])

    def ring(buf, each, n, when=None, kind=None):
        sems = (ring_send.at[n], ring_recv.at[n], pair_send.at[n], pair_recv.at[n])
        return Ring(sends, p, buf, each, sems, when, kind)

    ring_w = ring(w_buf.at[0], rows, 0, first)
    ring_qs = [ring(q_buf, depth, 1, first, 1), ring(q_buf, depth, 1, second, 1)]
    ring_kv = ring(kv, tokens, 2, kind=0)
    ring_ts = [ring(w_buf.at[1], rows, 3, first), ring(w_buf.at[1], rows, 3, second)]
    over_noisy = Across(sends, p, noisy, (fan_send.at[0], fan_recv.at[0]))
    over_att = Across(sends, p, att, (fan_send.at[1], fan_recv.at[1]))

    wide = 2 * rows

    def project(lhs, which, out):
        def part(j, carry):
            at = pl.ds(pl.multiple_of(j * wide, 128), wide)
            out[...] += jnp.dot(
                lhs(j, at), w_buf[which, at, :], preferred_element_type=f32
            )
            return carry

        lax.fori_loop(0, inner // wide, part, 0)

    def gap_spread():
        for rank, dx, da in p.fan():
            sends.same(
                lambda: gap_f.at[p.block],
                lambda rank=rank: gf_send.at[rank],
                lambda rank=rank: gf_recv.at[rank],
                lambda dx=dx, da=da: p.beside(dx, da),
                second,
            )

    def gap_gathered():
        for rank, dx, da in p.fan():
            block = 2 * lax.rem(p.x + xs - dx, xs) + lax.rem(p.a + da, 2)
            wait_recv(gap_f.at[block], gf_recv.at[rank])

    def predict(which):
        pred[...] = jnp.zeros_like(pred)
        project(lambda j, at: hob[p.c, :, at], which, pred)

    half_rows = [slice(0, tokens // 2), slice(tokens // 2, tokens)]
    half_cols = [slice(0, cols // 2), slice(cols // 2, cols)]

    @pl.when(first)
    def _():
        ring_q = ring_qs[0]
        swap(0, first_moved)
        ho_cross(first_kept)
        swap(1, first_moved)
        swapped(0)
        ring_w.begin()
        swap(3, first_moved)
        swap(2, first_moved)
        ring_w.advance(1)
        ho_step(first_moved)
        ring_w.advance(2)
        ring_w.advance(3)
        ho_forward(first_moved)
        swapped(2)
        ring_q.begin()
        swap(4, first_moved)
        ring_w.advance(4)
        own_ho.wait()
        ho_arrived()
        for k in range(steps + 1):
            ring_w.pair_arrived(k)
        swapped(1)
        predict(0)
        gen[...] = (bi_t[...].astype(f32) + pred[...].T).astype(jnp.bfloat16)
        for h in (0, 1):
            sends.start(
                lambda h=h: (gen.at[half_cols[h]], gen_in.at[half_cols[h]]),
                lambda h=h: one_send.at[h],
                lambda h=h: one_recv.at[h],
                lambda: p.dev(g=1),
                first,
            )

    @pl.when(second)
    def _():
        ring_q = ring_qs[1]
        swap(2, second_moved)
        swapped(2)
        ring_q.begin()
        swap(3, second_moved)
        ring_q.advance(1)
        swap(6, second_moved)
        ring_q.advance(2)
        ho_cross(second_kept)
        swap(1, second_moved)
        ring_q.advance(3)
        ho_step(second_moved)
        swap(5, second_moved)
        ring_q.advance(4)
        ho_forward(second_moved)
        own_ho.wait()
        swapped(6)
        ring_ts[1].begin()

    swapped(3)
    level = ts_ref[0].astype(f32) / 1000.0
    for h in (0, 1):
        at = half_cols[h]

        @pl.when(second)
        def _():
            wait_recv(gen_in.at[at], one_recv.at[h])
            gen[at, :] = gen_in[at, :]

        noisy[p.block, at, :] = (
            (1.0 - level) * gen[at, :].astype(f32) + level * noise_t[at, :].astype(f32)
        ).astype(jnp.bfloat16)
        over_noisy.begin(h)

    def first_q(k):
        pl.when(first)(lambda: ring_qs[0].advance(k))
        pl.when(second)(lambda: ring_ts[1].advance(k))

    def first_t(k):
        pl.when(first)(lambda: ring_ts[0].advance(k))

    @pl.when(second)
    def _():
        gap_d[...] = (gen[...].astype(f32) - noisy[p.block].astype(f32)).T

    over_noisy.forward(0, 0)
    first_q(1)
    over_noisy.crossed(0)
    over_noisy.step(1, 0)
    over_noisy.forward(0, 1)
    over_noisy.crossed(1)
    over_noisy.step(1, 1)
    first_q(2)
    over_noisy.forward(1, 0)
    over_noisy.forward(1, 1)
    first_q(3)
    over_noisy.arrived(0)
    over_noisy.arrived(1)

    @pl.when(second)
    def _():
        ho_arrived()

    total = jnp.zeros((1, tokens), f32)
    for f in range(fans):
        block = noisy[f].astype(f32)
        total += jnp.sum(block * block, axis=0, keepdims=True)
    factor = lax.rsqrt(total * (1.0 / (fans * cols)) + norm_eps)
    for f in range(fans):
        norm[f * cols : (f + 1) * cols, :] = (noisy[f].astype(f32) * factor).astype(jnp.bfloat16)
    first_q(4)
    for k in range(steps + 1):
        ring_qs[0].pair_arrived(k)

    def head_norm(value):
        scale = lax.rsqrt(jnp.mean(value * value, axis=1, keepdims=True) + norm_eps)
        return (value * scale).astype(jnp.bfloat16)

    own_rows = pl.ds(pl.multiple_of(home * tokens, 16), tokens)

    def proj(n):
        return lax.dot_general(
            norm[...], q_buf[n], (((0,), (0,)), ((), ())), preferred_element_type=f32
        )

    key_raw = proj(1)
    for h in range(heads):
        at = slice(h * HEAD_DIM, (h + 1) * HEAD_DIM)
        kv[0, own_rows, at] = head_norm(key_raw[:, at])
    ring_kv.begin((0,))
    kv[1, own_rows, :] = proj(2).astype(jnp.bfloat16)
    ring_kv.begin((1,))
    query_raw = proj(0)
    for h in range(heads):
        at = slice(h * HEAD_DIM, (h + 1) * HEAD_DIM)
        q_hat[:, at] = head_norm(query_raw[:, at])
    acc[...] = jnp.zeros_like(acc)
    lsum[...] = jnp.zeros_like(lsum)

    def attend(zz):
        at = pl.ds(pl.multiple_of(zz * 2 * tokens, 16), 2 * tokens)

        def one_head(h, carry):
            cut = pl.ds(pl.multiple_of(h * HEAD_DIM, HEAD_DIM), HEAD_DIM)
            scores = lax.dot_general(
                q_hat[:, cut], kv[0, at, cut], (((1,), (1,)), ((), ())), preferred_element_type=f32
            ) * (1.0 / math.sqrt(HEAD_DIM))
            weights = jnp.exp(scores)
            part = weights[:, :128]
            for j in range(1, 2 * tokens // 128):
                part += weights[:, j * 128 : (j + 1) * 128]
            lsum[h] += part
            acc[:, cut] += jnp.dot(
                weights.astype(jnp.bfloat16), kv[1, at, cut], preferred_element_type=f32
            )
            return carry

        lax.fori_loop(0, heads, one_head, 0)

    early = sends.take()
    sends.start(
        lambda: (hob.at[p.c], hob_in.at[p.c]),
        lambda: one_send.at[8],
        lambda: one_recv.at[8],
        lambda: p.dev(g=1 - p.g),
    )
    ring_kv.pair_arrived(0)
    attend(p.z)

    @pl.when(second)
    def _():
        for k in range(steps + 1):
            ring_ts[1].pair_arrived(k)
        swapped(1)
        swapped(5)
        predict(1)
        grad_s[...] = (
            (pred[...] + (bi_t[...].astype(f32) - target_t[...].astype(f32)).T)
            * (1.0 / math.sqrt(tokens * 2 * zs))
        ).astype(jnp.bfloat16)
        sends.start(
            lambda: (grad_s, grad.at[p.c]),
            lambda: one_send.at[9],
            lambda: one_recv.at[9],
            lambda: p.dev(g=0),
            second,
        )

    for k in range(1, steps + 1):
        for half in (0, 1):
            ring_kv.advance(k, (half,))
            if k > 1:
                if half == 0:
                    ring_kv.pair_arrived(k - 1)
                attend(ring_kv.zz(k - 1, half))
        if k == 2:
            sends.finish(early)
        if k == steps:

            @pl.when(first)
            def _():
                swapped(4)
                ring_ts[0].begin()

    ring_kv.pair_arrived(steps)
    attend(ring_kv.zz(steps, 0))

    for half in (0, 1):
        rr = half_rows[half]
        for h in range(heads):
            at = slice(h * HEAD_DIM, (h + 1) * HEAD_DIM)
            att[p.block, rr, at] = (
                acc[rr, at] / jnp.sum(lsum[h, rr, :], axis=1, keepdims=True)
            ).astype(jnp.bfloat16)
        over_att.begin(half)
    over_att.forward(0, 0)
    first_t(1)
    over_att.crossed(0)
    over_att.step(1, 0)
    over_att.forward(0, 1)
    first_t(2)
    over_att.crossed(1)
    over_att.step(1, 1)
    over_att.forward(1, 0)
    first_t(3)
    over_att.forward(1, 1)
    first_t(4)

    @pl.when(first)
    def _():
        for k in range(steps + 1):
            ring_ts[0].pair_arrived(k)

    wait_recv(hob_in.at[p.c], one_recv.at[8])
    sends.same(
        lambda: hob_in.at[p.c],
        lambda: one_send.at[10],
        lambda: one_recv.at[10],
        lambda: p.dev(c=1 - p.c),
    )
    early = sends.take()

    def pass_branch(h):
        sends.start(
            lambda: (b_own.at[half_rows[h]], b_in.at[half_rows[h]]),
            lambda: one_send.at[2 + h],
            lambda: one_recv.at[2 + h],
            lambda: p.dev(g=1),
            first,
        )

    for h in (0, 1):
        rr = half_rows[h]
        over_att.arrived(h)
        value = jnp.zeros((tokens // 2, cols), f32)
        for j in range(fans):
            value += jnp.dot(
                att[j, rr, :], w_buf[1, j * wide : (j + 1) * wide, :], preferred_element_type=f32
            )
        b_own[rr, :] = value

        pl.when(first)(lambda: pass_branch(h))

    def pass_grad(h):
        sends.same(
            lambda h=h: grad.at[p.c, half_rows[h]],
            lambda: one_send.at[4 + h],
            lambda: one_recv.at[4 + h],
            lambda: p.dev(c=1 - p.c),
        )

    @pl.when(first)
    def _():
        wait_recv(grad.at[p.c], one_recv.at[9])

    for h in (0, 1):
        rr = half_rows[h]

        @pl.when(second)
        def _():
            wait_recv(b_in.at[rr], one_recv.at[2 + h])
            grad[p.c, rr, :] = (b_own[rr, :] - b_in[rr, :]).astype(jnp.bfloat16)

        pass_grad(h)

    @pl.when(second)
    def _():
        gap = jnp.sum(jnp.abs(gap_d[...] - b_in[...]))
        gap_f[p.block] = jnp.full((8, 128), gap, f32)
        gap_spread()

    wait_recv(hob_in.at[1 - p.c], one_recv.at[10])
    for h in (0, 1):
        wait_recv(grad.at[1 - p.c, half_rows[h]], one_recv.at[4 + h])

    def partial(zz):
        at = pl.ds(pl.multiple_of(zz * wide, 128), wide)
        value = jnp.zeros((wide, cols), f32)
        for block in range(2):
            value += lax.dot_general(
                hob_in[block, :, at],
                grad[block],
                (((0,), (0,)), ((), ())),
                preferred_element_type=f32,
            )
        tmp[...] = value
        return tmp[pl.ds(pl.multiple_of(p.c * rows, 16), rows), :]

    each = rows // 2
    half_chunk = [slice(0, each), slice(each, rows)]

    def rs_parts(j):
        return [(0, 0), (1, 1)] if j == 1 else [(0, 1), (1, 0), (0, 0), (1, 1)]

    def rs_start(j, way, half):
        sends.start(
            lambda: (rs_send.at[j - 1, way, half], rs_recv.at[j - 1, way, half]),
            lambda: rs_ssem.at[j - 1, way, half],
            lambda: rs_rsem.at[j - 1, way, half],
            lambda: p.dev(z=p.zp if way == 0 else p.zm),
        )

    def rs_wait(j, way, half):
        wait_recv(rs_recv.at[j - 1, way, half], rs_rsem.at[j - 1, way, half])

    def gap_step(j):
        if j == 1:
            gap_gathered()
            gap_z[p.z] = jnp.sum(gap_f[...], axis=0)
            for dz in range(1, zs):
                sends.same(
                    lambda: gap_z.at[p.z],
                    lambda dz=dz: gz_send.at[dz],
                    lambda dz=dz: gz_recv.at[dz],
                    lambda dz=dz: p.dev(z=lax.rem(p.z + dz, zs)),
                    second,
                )
        if j == 2:
            for dz in range(1, zs):
                wait_recv(gap_z.at[lax.rem(p.z + zs - dz, zs)], gz_recv.at[dz])
            gap_c[p.c] = jnp.sum(gap_z[...], axis=0)
            sends.same(
                lambda: gap_c.at[p.c],
                lambda: one_send.at[6],
                lambda: one_recv.at[6],
                lambda: p.dev(c=1 - p.c),
                second,
            )
        if j == 3:
            wait_recv(gap_c.at[1 - p.c], one_recv.at[6])

    far = partial(lax.rem(p.z + steps, zs))
    for way, half in rs_parts(1):
        rs_send[0, way, half] = far[half_chunk[half]].astype(jnp.bfloat16)
        rs_start(1, way, half)
    for j in range(2, steps + 1):
        dist = steps - j + 1
        mine = [partial(lax.rem(p.z + dist, zs)), partial(lax.rem(p.z + zs - dist, zs))]
        for way, half in rs_parts(j):
            value = mine[way][half_chunk[half]]
            if (way, half) in rs_parts(j - 1):
                rs_wait(j - 1, way, half)
                value = value + rs_recv[j - 2, way, half].astype(f32)
            rs_send[j - 1, way, half] = value.astype(jnp.bfloat16)
            rs_start(j, way, half)
        if j == 2:
            pl.when(second)(lambda: gap_step(1))
        if j == 3:
            sends.finish(early)
            pl.when(second)(lambda: gap_step(2))
    mine = partial(p.z)
    pl.when(second)(lambda: gap_step(3))
    acc_w = tmp.at[0:rows]
    acc_w[...] = mine
    for way, half in rs_parts(2):
        rs_wait(steps, way, half)
        at = half_chunk[half]
        acc_w[at, :] = acc_w[at, :] + rs_recv[steps - 1, way, half].astype(f32)

    @pl.when(second)
    def _():
        gap = (gap_c[0] + gap_c[1])[0:1, 0:1] * (1.0 / (tokens * 2 * zs * fans * cols))
        wg_out[...] = (acc_w[...] * (1.0 / (gap + norm_eps))).astype(jnp.bfloat16)

    @pl.when(first)
    def _():
        wg_out[...] = acc_w[...].astype(jnp.bfloat16)

    sends.start(
        lambda: (wg_out, wg_in),
        lambda: one_send.at[7],
        lambda: one_recv.at[7],
        lambda: p.dev(g=1 - p.g, a=p.c, c=p.a),
    )
    wait_recv(wg_in, one_recv.at[7])
    out_ref[...] = wg_in[...].astype(f32)
    sends.finish(sends.take())


def weight_gradient(zs, xs, ts, bi, ho, ww, qw, to, noise, target, interpret=None):
    tokens, inner = ho.shape
    cols = bi.shape[0]
    rows = ww.shape[0]
    depth, local_inner = qw.shape[1:]
    heads = local_inner // HEAD_DIM
    seq, fans, steps = 2 * zs, 2 * xs, zs // 2
    b16, f32 = jnp.bfloat16, jnp.float32
    vmem, dma = pltpu.VMEM, pltpu.SemaphoreType.DMA
    scratch = [
        vmem((2, inner, cols), b16),
        vmem((3, seq * depth, local_inner), b16),
        vmem((2, tokens, inner), b16),
        vmem((cols, tokens), b16),
        vmem((cols, tokens), b16),
        vmem((cols, tokens), b16),
        vmem((cols, tokens), b16),
        vmem((cols, tokens), b16),
        vmem((fans, cols, tokens), b16),
        vmem((fans * cols, tokens), b16),
        vmem((2, seq * tokens, local_inner), b16),
        vmem((tokens, local_inner), b16),
        vmem((tokens, local_inner), f32),
        vmem((heads, tokens, 128), f32),
        vmem((fans, tokens, local_inner), b16),
        vmem((tokens, cols), f32),
        vmem((tokens, cols), f32),
        vmem((tokens, cols), b16),
        vmem((2, tokens, inner), b16),
        vmem((tokens, cols), f32),
        vmem((tokens, cols), f32),
        vmem((2, tokens, cols), b16),
        vmem((2 * rows, cols), f32),
        vmem((steps, 2, 2, rows // 2, cols), b16),
        vmem((steps, 2, 2, rows // 2, cols), b16),
        vmem((fans, 8, 128), f32),
        vmem((zs, 8, 128), f32),
        vmem((2, 8, 128), f32),
        vmem((rows, cols), b16),
        vmem((rows, cols), b16),
        dma((7,)),
        dma((7,)),
        dma((6,)),
        dma((6,)),
        dma((4, steps, 2, 2)),
        dma((4, steps, 2, 2)),
        dma((4, steps + 1, 2, 2)),
        dma((4, steps + 1, 2, 2)),
        dma((2, 18)),
        dma((2, 18)),
        dma((steps, 2, 2)),
        dma((steps, 2, 2)),
        dma((fans,)),
        dma((fans,)),
        dma((zs,)),
        dma((zs,)),
        dma((11,)),
        dma((11,)),
        dma((1,)),
    ]
    in_vmem = pl.BlockSpec(memory_space=pltpu.VMEM)
    return pl.pallas_call(
        functools.partial(kernel, zs, xs),
        out_shape=jax.ShapeDtypeStruct((rows, cols), f32),
        in_specs=[pl.BlockSpec(memory_space=pltpu.SMEM)] + [pl.BlockSpec(memory_space=pl.ANY)] * 7,
        out_specs=in_vmem,
        scratch_shapes=scratch,
        compiler_params=pltpu.CompilerParams(
            collective_id=0, has_side_effects=True, vmem_limit_bytes=62 * 1024 * 1024
        ),
        name="weight_gradient",
    )(ts, bi, ho, ww, qw, to, noise, target)


def body(
    block_input,
    head_outputs,
    out_master,
    first_moment,
    second_moment,
    score_qkv,
    teacher_out,
    noise,
    timestep,
    fake_target,
):
    zs, xs = lax.axis_size("seq") // 2, lax.axis_size("fsdp") // 2
    work_weight = out_master[0].astype(jnp.bfloat16)
    qw = score_qkv[0].transpose(0, 2, 1)
    weight_grad = weight_gradient(
        zs, xs, timestep, block_input[0].T, head_outputs[0], work_weight, qw, teacher_out, noise.T,
        fake_target.T,
    )
    new_first = 0.9 * first_moment[0] + 0.1 * weight_grad
    new_second = 0.95 * second_moment[0] + 0.05 * weight_grad * weight_grad
    new_master = out_master[0] - learn_rate * (new_first / first_fix) / (
        jnp.sqrt(new_second / second_fix) + 1e-08
    )
    return (new_master[None], new_first[None], new_second[None])


def solution(mesh):
    placed = (
        P("group", "seq", "fsdp"),
        P("group", "seq", None),
        P("group", "seq", "fsdp"),
        P("group", "seq", "fsdp"),
        P("group", "seq", "fsdp"),
        P("group", None, "fsdp", "seq"),
        P("seq", "fsdp"),
        P("seq", "fsdp"),
        P(),
        P("seq", "fsdp"),
    )
    return jax.shard_map(
        body,
        mesh=mesh,
        in_specs=placed,
        out_specs=(P("group", "seq", "fsdp"), P("group", "seq", "fsdp"), P("group", "seq", "fsdp")),
        check_vma=False,
    )
```

```python
import functools
import math

import jax
import jax.numpy as jnp
from jax import lax
from jax.experimental import pallas as pl
from jax.experimental.pallas import tpu as pltpu
from jax.sharding import PartitionSpec as P

D = 2560
HEAD_DIM = 128
MESH = pl.DeviceIdType.MESH

norm_eps = 1e-06
first_fix = 1.0 - 0.9**20
second_fix = 1.0 - 0.95**20
learn_rate = 0.003


class Sends:
    def __init__(self):
        self.open = []

    def start(self, ends, send_sem, recv_sem, device, when=None):
        def make():
            src, dst = ends()
            return pltpu.make_async_remote_copy(
                src_ref=src,
                dst_ref=dst,
                send_sem=send_sem(),
                recv_sem=recv_sem(),
                device_id=device(),
                device_id_type=MESH,
            )

        make().start()
        self.open.append((make, when))

    def same(self, ref, send_sem, recv_sem, device, when=None):
        def ends():
            here = ref()
            return here, here

        self.start(ends, send_sem, recv_sem, device, when)

    def take(self):
        taken, self.open = self.open, []
        return taken

    @staticmethod
    def finish(taken):
        for make, when in taken:
            if when is None:
                make().wait_send()
            else:
                pl.when(when)(lambda make=make: make().wait_send())


def wait_recv(dst, recv_sem):
    pltpu.make_async_copy(dst, dst, recv_sem).wait()


class Ring:
    def __init__(self, sends, place, buf, rows, sems, when=None, kind=None):
        self.sends, self.place, self.buf, self.rows, self.when = sends, place, buf, rows, when
        self.kind = kind
        self.ring_send, self.ring_recv, self.pair_send, self.pair_recv = sems
        self.steps = place.zs // 2

    def piece(self, zz, cc, half):
        if self.kind == 0:
            start = (2 * zz + cc) * self.rows
            return self.buf.at[half, pl.ds(pl.multiple_of(start, 16), self.rows)]
        each = self.rows // 2
        start = (2 * zz + cc) * self.rows + half * each
        if self.kind == 1:
            return self.buf.at[:, pl.ds(pl.multiple_of(start, 16), each), :]
        return self.buf.at[pl.ds(pl.multiple_of(start, 16), each)]

    def parts(self, k):
        if k < self.steps:
            return [(0, 0), (1, 0), (0, 1), (1, 1)]
        return [(0, 0), (1, 1)]

    def zz(self, k, way):
        p = self.place
        return lax.rem(p.z + p.zs - k, p.zs) if way == 0 else lax.rem(p.z + k, p.zs)

    def send(self, k, way, half):
        p = self.place
        self.sends.same(
            lambda: self.piece(self.zz(k - 1, way), p.c, half),
            lambda: self.ring_send.at[k - 1, way, half],
            lambda: self.ring_recv.at[k - 1, way, half],
            lambda: p.dev(z=p.zp if way == 0 else p.zm),
            self.when,
        )

    def pair(self, k, way, half):
        p = self.place
        self.sends.same(
            lambda: self.piece(self.zz(k, way), p.c, half),
            lambda: self.pair_send.at[k, way, half],
            lambda: self.pair_recv.at[k, way, half],
            lambda: p.dev(c=1 - p.c),
            self.when,
        )

    def begin(self, halves=(0, 1)):
        for way, half in self.parts(1):
            if half in halves:
                self.send(1, way, half)
        for half in halves:
            self.pair(0, 0, half)

    def advance(self, k, halves=(0, 1)):
        for way, half in self.parts(k):
            if half not in halves:
                continue
            wait_recv(
                self.piece(self.zz(k, way), self.place.c, half),
                self.ring_recv.at[k - 1, way, half],
            )
            if k < self.steps and (way, half) in self.parts(k + 1):
                self.send(k + 1, way, half)
            self.pair(k, way, half)

    def pair_arrived(self, k):
        for way, half in self.parts(k) if k else [(0, 0), (0, 1)]:
            wait_recv(
                self.piece(self.zz(k, way), 1 - self.place.c, half),
                self.pair_recv.at[k, way, half],
            )


class Across:
    def __init__(self, sends, place, buf, sems):
        self.sends, self.place, self.buf = sends, place, buf
        self.send_sem, self.recv_sem = sems
        self.rows = buf.shape[1]

    def part(self, dx, other, half, quarter=None):
        p = self.place
        block = 2 * lax.rem(p.x + dx + p.xs, p.xs) + (1 - p.a if other else p.a)
        each = self.rows // 2
        start = half * each
        if quarter is not None:
            each = each // 2
            start = start + quarter * each
        return self.buf.at[block, pl.ds(start, each)]

    def go(self, n, ref, device):
        self.sends.same(ref, lambda: self.send_sem.at[n], lambda: self.recv_sem.at[n], device)

    def beside(self, way):
        p = self.place
        return p.dev(x=lax.rem(p.x + (1 if way == 0 else p.xs - 1), p.xs))

    def cross(self, half):
        p = self.place
        self.go(half, lambda: self.part(0, False, half), lambda: p.dev(a=1 - p.a))

    def crossed(self, half):
        wait_recv(self.part(0, True, half), self.recv_sem.at[half])

    def step(self, other, half):
        for way in (0, 1):
            self.go(
                2 + 4 * other + 2 * half + way,
                lambda: self.part(0, other, half),
                lambda way=way: self.beside(way),
            )

    def forward(self, other, half):
        for way in (0, 1):
            near = -1 if way == 0 else 1
            n = 4 * other + 2 * half + way
            wait_recv(self.part(near, other, half), self.recv_sem.at[2 + n])
            self.go(
                10 + n,
                lambda near=near, way=way: self.part(near, other, half, way),
                lambda way=way: self.beside(way),
            )

    def arrived(self, half):
        for other in (0, 1):
            for way in (0, 1):
                n = 4 * other + 2 * half + way
                wait_recv(self.part(2, other, half, way), self.recv_sem.at[10 + n])

    def begin(self, half):
        self.cross(half)
        self.step(0, half)


class Place:
    def __init__(self, zs, xs):
        self.zs, self.xs = zs, xs
        seq, fsdp = lax.axis_index("seq"), lax.axis_index("fsdp")
        self.g = lax.axis_index("group")
        self.z, self.a = seq // 2, lax.rem(seq, 2)
        self.x, self.c = fsdp // 2, lax.rem(fsdp, 2)
        self.zp = lax.rem(self.z + 1, zs)
        self.zm = lax.rem(self.z + zs - 1, zs)
        self.block = 2 * self.x + self.a
        self.kept = self.a == self.c
        self.moved = self.a != self.c
        self.first = self.g == 0
        self.second = self.g == 1

    def dev(self, g=None, z=None, a=None, x=None, c=None):
        g = self.g if g is None else g
        z = self.z if z is None else z
        a = self.a if a is None else a
        x = self.x if x is None else x
        c = self.c if c is None else c
        return {"group": g, "seq": 2 * z + a, "fsdp": 2 * x + c}

    def fan(self):
        return [(2 * dx + da, dx, da) for dx in range(self.xs) for da in range(2) if dx or da]

    def beside(self, dx, da):
        return self.dev(x=lax.rem(self.x + dx, self.xs), a=lax.rem(self.a + da, 2))


def kernel(
    zs,
    xs,
    ts_ref,
    bi_ref,
    ho_ref,
    ww_ref,
    qw_ref,
    to_ref,
    noise_ref,
    target_ref,
    out_ref,
    w_buf,
    q_buf,
    hob,
    bi_t,
    noise_t,
    target_t,
    gen,
    gen_in,
    noisy,
    norm,
    kv,
    q_hat,
    acc,
    lsum,
    att,
    pred,
    b_own,
    b_in,
    grad,
    tmp,
    rs_send,
    rs_recv,
    gap_f,
    gap_z,
    gap_c,
    wg_out,
    wg_in,
    t_send,
    t_recv,
    ho_send,
    ho_recv,
    ring_send,
    ring_recv,
    pair_send,
    pair_recv,
    fan_send,
    fan_recv,
    rs_ssem,
    rs_rsem,
    gf_send,
    gf_recv,
    gz_send,
    gz_recv,
    one_send,
    one_recv,
    local_sem,
):
    p = Place(zs, xs)
    sends = Sends()
    tokens, inner = ho_ref.shape
    cols = bi_ref.shape[0]
    rows = ww_ref.shape[0]
    depth = qw_ref.shape[1]
    local_inner = q_hat.shape[1]
    heads = local_inner // HEAD_DIM
    steps = zs // 2
    fans = 2 * xs
    first = p.first
    second = p.second
    f32 = jnp.float32

    barrier = pltpu.get_barrier_semaphore()
    peers = [p.dev(z=lax.rem(p.z + dz, zs)) for dz in range(1, zs)]
    peers += [p.beside(dx, da) for _, dx, da in p.fan()]
    peers += [p.dev(c=1 - p.c), p.dev(g=1 - p.g), p.dev(a=1 - p.a, c=1 - p.c)]
    for peer in peers:
        pl.semaphore_signal(barrier, inc=1, device_id=peer, device_id_type=MESH)

    own_ho = pltpu.make_async_copy(ho_ref, hob.at[p.a], local_sem.at[0])
    own_ho.start()
    pl.semaphore_wait(barrier, len(peers))

    def rows_of(buf, each, at):
        return buf.at[pl.ds(pl.multiple_of(at * each, 16), each)]

    away, home = 2 * p.z + p.a, 2 * p.z + p.c
    swaps = [
        (ww_ref, lambda i: rows_of(w_buf.at[0], rows, i)),
        (bi_ref, lambda i: bi_t),
        (qw_ref, lambda i: q_buf.at[:, pl.ds(pl.multiple_of(i * depth, 16), depth), :]),
        (noise_ref, lambda i: noise_t),
        (to_ref, lambda i: rows_of(w_buf.at[1], rows, i)),
        (target_ref, lambda i: target_t),
        (ww_ref, lambda i: rows_of(w_buf.at[1], rows, i)),
    ]

    def swap(n, when):
        src, dst = swaps[n]

        @pl.when(p.kept)
        def _():
            pltpu.make_async_copy(src, dst(away), t_recv.at[n]).start()

        @pl.when(p.moved)
        def _():
            sends.start(
                lambda: (src, dst(away)),
                lambda: t_send.at[n],
                lambda: t_recv.at[n],
                lambda: p.dev(a=p.c, c=p.a),
                when,
            )

    first_moved, second_moved = first & p.moved, second & p.moved
    first_kept, second_kept = first & p.kept, second & p.kept

    def swapped(n):
        wait_recv(swaps[n][1](home), t_recv.at[n])

    share = tokens // xs

    def ho_rows(block, dx, half=None):
        start = lax.rem(p.x + dx + xs, xs) * share
        each = share
        if half is not None:
            each = share // 2
            start = start + half * each
        return hob.at[block, pl.ds(pl.multiple_of(start, 16), each)]

    def ho_cross(when):
        @pl.when(p.kept)
        def _():
            sends.start(
                lambda: (
                    ho_ref.at[pl.ds(pl.multiple_of(p.x * share, 16), share)],
                    ho_rows(p.a, 0),
                ),
                lambda: ho_send.at[0],
                lambda: ho_recv.at[0],
                lambda: p.dev(a=1 - p.a),
                when,
            )

    def beside(way):
        return p.dev(x=lax.rem(p.x + (1 if way == 0 else xs - 1), xs))

    def ho_step(when):
        @pl.when(p.moved)
        def _():
            wait_recv(ho_rows(p.c, 0), ho_recv.at[0])
            for way in (0, 1):
                sends.same(
                    lambda: ho_rows(p.c, 0),
                    lambda way=way: ho_send.at[1 + way],
                    lambda way=way: ho_recv.at[1 + way],
                    lambda way=way: beside(way),
                    when,
                )

    def ho_forward(when):
        @pl.when(p.moved)
        def _():
            for way in (0, 1):
                near = -1 if way == 0 else 1
                wait_recv(ho_rows(p.c, near), ho_recv.at[1 + way])
                sends.same(
                    lambda near=near, way=way: ho_rows(p.c, near, way),
                    lambda way=way: ho_send.at[3 + way],
                    lambda way=way: ho_recv.at[3 + way],
                    lambda way=way: beside(way),
                    when,
                )

    def ho_arrived(when):
        @pl.when(p.moved)
        def _():
            for way in (0, 1):
                wait_recv(ho_rows(p.c, 2, way), ho_recv.at[3 + way])
            sends.same(
                lambda: hob.at[p.c],
                lambda: ho_send.at[5],
                lambda: ho_recv.at[5],
                lambda: p.dev(c=1 - p.c),
                when,
            )

    def ring(buf, each, n, when=None, kind=None):
        sems = (ring_send.at[n], ring_recv.at[n], pair_send.at[n], pair_recv.at[n])
        return Ring(sends, p, buf, each, sems, when, kind)

    ring_w = ring(w_buf.at[0], rows, 0, first)
    ring_qs = [ring(q_buf, depth, 1, first, 1), ring(q_buf, depth, 1, second, 1)]
    ring_kv = ring(kv, tokens, 2, kind=0)
    ring_ts = [ring(w_buf.at[1], rows, 3, first), ring(w_buf.at[1], rows, 3, second)]
    over_noisy = Across(sends, p, noisy, (fan_send.at[0], fan_recv.at[0]))
    over_att = Across(sends, p, att, (fan_send.at[1], fan_recv.at[1]))

    wide = 2 * rows

    def project(lhs, which, out):
        def part(j, carry):
            at = pl.ds(pl.multiple_of(j * wide, 128), wide)
            out[...] += jnp.dot(
                lhs(j, at), w_buf[which, at, :], preferred_element_type=f32
            )
            return carry

        lax.fori_loop(0, inner // wide, part, 0)

    def gap_spread():
        for rank, dx, da in p.fan():
            sends.same(
                lambda: gap_f.at[p.block],
                lambda rank=rank: gf_send.at[rank],
                lambda rank=rank: gf_recv.at[rank],
                lambda dx=dx, da=da: p.beside(dx, da),
                first,
            )

    def gap_gathered():
        for rank, dx, da in p.fan():
            block = 2 * lax.rem(p.x + xs - dx, xs) + lax.rem(p.a + da, 2)
            wait_recv(gap_f.at[block], gf_recv.at[rank])

    def predict(which):
        pred[...] = jnp.zeros_like(pred)
        project(lambda j, at: hob[p.c, :, at], which, pred)

    half_rows = [slice(0, tokens // 2), slice(tokens // 2, tokens)]
    half_cols = [slice(0, cols // 2), slice(cols // 2, cols)]

    @pl.when(first)
    def _():
        ring_q = ring_qs[0]
        swap(0, first_moved)
        ho_cross(first_kept)
        swap(1, first_moved)
        swapped(0)
        ring_w.begin()
        swap(3, first_moved)
        swap(2, first_moved)
        ring_w.advance(1)
        ho_step(first_moved)
        ring_w.advance(2)
        ring_w.advance(3)
        ho_forward(first_moved)
        swapped(2)
        ring_q.begin()
        swap(4, first_moved)
        ring_w.advance(4)
        own_ho.wait()
        ho_arrived(first_moved)
        for k in range(steps + 1):
            ring_w.pair_arrived(k)
        swapped(1)
        predict(0)
        gen[...] = (bi_t[...].astype(f32) + pred[...].T).astype(jnp.bfloat16)
        for h in (0, 1):
            sends.start(
                lambda h=h: (gen.at[half_cols[h]], gen_in.at[half_cols[h]]),
                lambda h=h: one_send.at[h],
                lambda h=h: one_recv.at[h],
                lambda: p.dev(g=1),
                first,
            )

    @pl.when(second)
    def _():
        ring_q = ring_qs[1]
        swap(2, second_moved)
        swapped(2)
        ring_q.begin()
        swap(3, second_moved)
        ring_q.advance(1)
        swap(6, second_moved)
        ring_q.advance(2)
        ho_cross(second_kept)
        swap(1, second_moved)
        ring_q.advance(3)
        ho_step(second_moved)
        swap(5, second_moved)
        ring_q.advance(4)
        ho_forward(second_moved)
        own_ho.wait()
        swapped(6)
        ring_ts[1].begin()

    swapped(3)
    level = ts_ref[0].astype(f32) / 1000.0
    for h in (0, 1):
        at = half_cols[h]

        @pl.when(second)
        def _():
            wait_recv(gen_in.at[at], one_recv.at[h])
            gen[at, :] = gen_in[at, :]

        noisy[p.block, at, :] = (
            (1.0 - level) * gen[at, :].astype(f32) + level * noise_t[at, :].astype(f32)
        ).astype(jnp.bfloat16)
        over_noisy.begin(h)

    def first_q(k):
        pl.when(first)(lambda: ring_qs[0].advance(k))
        pl.when(second)(lambda: ring_ts[1].advance(k))

    def first_t(k):
        pl.when(first)(lambda: ring_ts[0].advance(k))

    @pl.when(first)
    def _():
        pred[...] = (gen[...].astype(f32) - noisy[p.block].astype(f32)).T

    over_noisy.forward(0, 0)
    first_q(1)
    over_noisy.crossed(0)
    over_noisy.step(1, 0)
    over_noisy.forward(0, 1)
    over_noisy.crossed(1)
    over_noisy.step(1, 1)
    first_q(2)
    over_noisy.forward(1, 0)
    over_noisy.forward(1, 1)
    first_q(3)
    over_noisy.arrived(0)
    over_noisy.arrived(1)

    @pl.when(second)
    def _():
        ho_arrived(second_moved)

    total = jnp.zeros((1, tokens), f32)
    for f in range(fans):
        block = noisy[f].astype(f32)
        total += jnp.sum(block * block, axis=0, keepdims=True)
    factor = lax.rsqrt(total * (1.0 / (fans * cols)) + norm_eps)
    for f in range(fans):
        norm[f * cols : (f + 1) * cols, :] = (noisy[f].astype(f32) * factor).astype(jnp.bfloat16)
    first_q(4)
    for k in range(steps + 1):
        ring_qs[0].pair_arrived(k)

    def head_norm(value):
        scale = lax.rsqrt(jnp.mean(value * value, axis=1, keepdims=True) + norm_eps)
        return (value * scale).astype(jnp.bfloat16)

    own_rows = pl.ds(pl.multiple_of(home * tokens, 16), tokens)

    def proj(n):
        return lax.dot_general(
            norm[...], q_buf[n], (((0,), (0,)), ((), ())), preferred_element_type=f32
        )

    key_raw = proj(1)
    for h in range(heads):
        at = slice(h * HEAD_DIM, (h + 1) * HEAD_DIM)
        kv[0, own_rows, at] = head_norm(key_raw[:, at])
    ring_kv.begin((0,))
    kv[1, own_rows, :] = proj(2).astype(jnp.bfloat16)
    ring_kv.begin((1,))
    query_raw = proj(0)
    for h in range(heads):
        at = slice(h * HEAD_DIM, (h + 1) * HEAD_DIM)
        q_hat[:, at] = head_norm(query_raw[:, at])
    acc[...] = jnp.zeros_like(acc)
    lsum[...] = jnp.zeros_like(lsum)

    def attend(zz):
        at = pl.ds(pl.multiple_of(zz * 2 * tokens, 16), 2 * tokens)

        def one_head(h, carry):
            cut = pl.ds(pl.multiple_of(h * HEAD_DIM, HEAD_DIM), HEAD_DIM)
            scores = lax.dot_general(
                q_hat[:, cut], kv[0, at, cut], (((1,), (1,)), ((), ())), preferred_element_type=f32
            ) * (1.0 / math.sqrt(HEAD_DIM))
            weights = jnp.exp(scores)
            part = weights[:, :128]
            for j in range(1, 2 * tokens // 128):
                part += weights[:, j * 128 : (j + 1) * 128]
            lsum[h] += part
            acc[:, cut] += jnp.dot(
                weights.astype(jnp.bfloat16), kv[1, at, cut], preferred_element_type=f32
            )
            return carry

        lax.fori_loop(0, heads, one_head, 0)

    ring_kv.pair_arrived(0)
    attend(p.z)
    for k in range(1, steps + 1):
        for half in (0, 1):
            ring_kv.advance(k, (half,))
            if k > 1:
                if half == 0:
                    ring_kv.pair_arrived(k - 1)
                attend(ring_kv.zz(k - 1, half))
        if k == steps:

            @pl.when(first)
            def _():
                swapped(4)
                ring_ts[0].begin()

    ring_kv.pair_arrived(steps)
    attend(ring_kv.zz(steps, 0))

    for half in (0, 1):
        rr = half_rows[half]
        for h in range(heads):
            at = slice(h * HEAD_DIM, (h + 1) * HEAD_DIM)
            att[p.block, rr, at] = (
                acc[rr, at] / jnp.sum(lsum[h, rr, :], axis=1, keepdims=True)
            ).astype(jnp.bfloat16)
        over_att.begin(half)
    over_att.forward(0, 0)
    first_t(1)
    over_att.crossed(0)
    over_att.step(1, 0)
    over_att.forward(0, 1)
    first_t(2)
    over_att.crossed(1)
    over_att.step(1, 1)
    over_att.forward(1, 0)
    first_t(3)
    over_att.forward(1, 1)
    first_t(4)
    for k in range(steps + 1):
        ring_ts[0].pair_arrived(k)

    early = sends.take()

    def pass_branch(h):
        sends.start(
            lambda: (b_own.at[half_rows[h]], b_in.at[half_rows[h]]),
            lambda: one_send.at[2 + h],
            lambda: one_recv.at[2 + h],
            lambda: p.dev(g=0),
            second,
        )

    for h in (0, 1):
        rr = half_rows[h]
        over_att.arrived(h)
        value = jnp.zeros((tokens // 2, cols), f32)
        for j in range(fans):
            value += jnp.dot(
                att[j, rr, :], w_buf[1, j * wide : (j + 1) * wide, :], preferred_element_type=f32
            )
        b_own[rr, :] = value

        pl.when(second)(lambda: pass_branch(h))

    def pass_grad(h):
        sends.same(
            lambda h=h: grad.at[p.c, half_rows[h]],
            lambda: one_send.at[4 + h],
            lambda: one_recv.at[4 + h],
            lambda: p.dev(c=1 - p.c),
        )

    @pl.when(second)
    def _():
        swapped(1)
        swapped(5)
        predict(1)
        grad[p.c] = (
            (pred[...] + (bi_t[...].astype(f32) - target_t[...].astype(f32)).T) * (1.0 / math.sqrt(tokens * 2 * zs))
        ).astype(jnp.bfloat16)

    @pl.when(first)
    def _():
        gap = jnp.sum(jnp.abs(pred[...] - b_own[...]))
        gap_f[p.block] = jnp.full((8, 128), gap, f32)
        gap_spread()

    sends.finish(early)
    for h in (0, 1):
        rr = half_rows[h]

        @pl.when(first)
        def _():
            wait_recv(b_in.at[rr], one_recv.at[2 + h])
            grad[p.c, rr, :] = (b_in[rr, :] - b_own[rr, :]).astype(jnp.bfloat16)

        pass_grad(h)

    @pl.when(p.kept)
    def _():
        wait_recv(hob.at[1 - p.c], ho_recv.at[5])

    for h in (0, 1):
        wait_recv(grad.at[1 - p.c, half_rows[h]], one_recv.at[4 + h])

    def partial(zz):
        at = pl.ds(pl.multiple_of(zz * wide, 128), wide)
        value = jnp.zeros((wide, cols), f32)
        for block in range(2):
            value += lax.dot_general(
                hob[block, :, at],
                grad[block],
                (((0,), (0,)), ((), ())),
                preferred_element_type=f32,
            )
        tmp[...] = value
        return tmp[pl.ds(pl.multiple_of(p.c * rows, 16), rows), :]

    each = rows // 2
    half_chunk = [slice(0, each), slice(each, rows)]

    def rs_parts(j):
        return [(0, 0), (1, 1)] if j == 1 else [(0, 1), (1, 0), (0, 0), (1, 1)]

    def rs_start(j, way, half):
        sends.start(
            lambda: (rs_send.at[j - 1, way, half], rs_recv.at[j - 1, way, half]),
            lambda: rs_ssem.at[j - 1, way, half],
            lambda: rs_rsem.at[j - 1, way, half],
            lambda: p.dev(z=p.zp if way == 0 else p.zm),
        )

    def rs_wait(j, way, half):
        wait_recv(rs_recv.at[j - 1, way, half], rs_rsem.at[j - 1, way, half])

    def gap_step(j):
        if j == 1:
            gap_gathered()
            gap_z[p.z] = jnp.sum(gap_f[...], axis=0)
            for dz in range(1, zs):
                sends.same(
                    lambda: gap_z.at[p.z],
                    lambda dz=dz: gz_send.at[dz],
                    lambda dz=dz: gz_recv.at[dz],
                    lambda dz=dz: p.dev(z=lax.rem(p.z + dz, zs)),
                    first,
                )
        if j == 2:
            for dz in range(1, zs):
                wait_recv(gap_z.at[lax.rem(p.z + zs - dz, zs)], gz_recv.at[dz])
            gap_c[p.c] = jnp.sum(gap_z[...], axis=0)
            sends.same(
                lambda: gap_c.at[p.c],
                lambda: one_send.at[6],
                lambda: one_recv.at[6],
                lambda: p.dev(c=1 - p.c),
                first,
            )
        if j == 3:
            wait_recv(gap_c.at[1 - p.c], one_recv.at[6])

    far = partial(lax.rem(p.z + steps, zs))
    for way, half in rs_parts(1):
        rs_send[0, way, half] = far[half_chunk[half]].astype(jnp.bfloat16)
        rs_start(1, way, half)
    for j in range(2, steps + 1):
        dist = steps - j + 1
        mine = [partial(lax.rem(p.z + dist, zs)), partial(lax.rem(p.z + zs - dist, zs))]
        for way, half in rs_parts(j):
            value = mine[way][half_chunk[half]]
            if (way, half) in rs_parts(j - 1):
                rs_wait(j - 1, way, half)
                value = value + rs_recv[j - 2, way, half].astype(f32)
            rs_send[j - 1, way, half] = value.astype(jnp.bfloat16)
            rs_start(j, way, half)
        if j == 2:
            pl.when(first)(lambda: gap_step(1))
        if j == 3:
            pl.when(first)(lambda: gap_step(2))
    mine = partial(p.z)
    pl.when(first)(lambda: gap_step(3))
    acc_w = tmp.at[0:rows]
    acc_w[...] = mine
    for way, half in rs_parts(2):
        rs_wait(steps, way, half)
        at = half_chunk[half]
        acc_w[at, :] = acc_w[at, :] + rs_recv[steps - 1, way, half].astype(f32)

    @pl.when(first)
    def _():
        gap = (gap_c[0] + gap_c[1])[0:1, 0:1] * (1.0 / (tokens * 2 * zs * fans * cols))
        wg_out[...] = (acc_w[...] * (1.0 / (gap + norm_eps))).astype(jnp.bfloat16)

    @pl.when(second)
    def _():
        wg_out[...] = acc_w[...].astype(jnp.bfloat16)

    @pl.when(p.moved)
    def _():
        sends.start(
            lambda: (wg_out, wg_in),
            lambda: one_send.at[7],
            lambda: one_recv.at[7],
            lambda: p.dev(a=p.c, c=p.a),
            p.moved,
        )
        wait_recv(wg_in, one_recv.at[7])
        out_ref[...] = wg_in[...].astype(f32)

    @pl.when(p.kept)
    def _():
        out_ref[...] = wg_out[...].astype(f32)

    sends.finish(sends.take())


def weight_gradient(zs, xs, ts, bi, ho, ww, qw, to, noise, target, interpret=None):
    tokens, inner = ho.shape
    cols = bi.shape[0]
    rows = ww.shape[0]
    depth, local_inner = qw.shape[1:]
    heads = local_inner // HEAD_DIM
    seq, fans, steps = 2 * zs, 2 * xs, zs // 2
    b16, f32 = jnp.bfloat16, jnp.float32
    vmem, dma = pltpu.VMEM, pltpu.SemaphoreType.DMA
    scratch = [
        vmem((2, inner, cols), b16),
        vmem((3, seq * depth, local_inner), b16),
        vmem((2, tokens, inner), b16),
        vmem((cols, tokens), b16),
        vmem((cols, tokens), b16),
        vmem((cols, tokens), b16),
        vmem((cols, tokens), b16),
        vmem((cols, tokens), b16),
        vmem((fans, cols, tokens), b16),
        vmem((fans * cols, tokens), b16),
        vmem((2, seq * tokens, local_inner), b16),
        vmem((tokens, local_inner), b16),
        vmem((tokens, local_inner), f32),
        vmem((heads, tokens, 128), f32),
        vmem((fans, tokens, local_inner), b16),
        vmem((tokens, cols), f32),
        vmem((tokens, cols), f32),
        vmem((tokens, cols), f32),
        vmem((2, tokens, cols), b16),
        vmem((2 * rows, cols), f32),
        vmem((steps, 2, 2, rows // 2, cols), b16),
        vmem((steps, 2, 2, rows // 2, cols), b16),
        vmem((fans, 8, 128), f32),
        vmem((zs, 8, 128), f32),
        vmem((2, 8, 128), f32),
        vmem((rows, cols), b16),
        vmem((rows, cols), b16),
        dma((7,)),
        dma((7,)),
        dma((6,)),
        dma((6,)),
        dma((4, steps, 2, 2)),
        dma((4, steps, 2, 2)),
        dma((4, steps + 1, 2, 2)),
        dma((4, steps + 1, 2, 2)),
        dma((2, 18)),
        dma((2, 18)),
        dma((steps, 2, 2)),
        dma((steps, 2, 2)),
        dma((fans,)),
        dma((fans,)),
        dma((zs,)),
        dma((zs,)),
        dma((8,)),
        dma((8,)),
        dma((1,)),
    ]
    in_vmem = pl.BlockSpec(memory_space=pltpu.VMEM)
    return pl.pallas_call(
        functools.partial(kernel, zs, xs),
        out_shape=jax.ShapeDtypeStruct((rows, cols), f32),
        in_specs=[pl.BlockSpec(memory_space=pltpu.SMEM)] + [pl.BlockSpec(memory_space=pl.ANY)] * 7,
        out_specs=in_vmem,
        scratch_shapes=scratch,
        compiler_params=pltpu.CompilerParams(
            collective_id=0, has_side_effects=True, vmem_limit_bytes=62 * 1024 * 1024
        ),
        name="weight_gradient",
    )(ts, bi, ho, ww, qw, to, noise, target)


def body(
    block_input,
    head_outputs,
    out_master,
    first_moment,
    second_moment,
    score_qkv,
    teacher_out,
    noise,
    timestep,
    fake_target,
):
    zs, xs = lax.axis_size("seq") // 2, lax.axis_size("fsdp") // 2
    work_weight = out_master[0].astype(jnp.bfloat16)
    qw = score_qkv[0].transpose(0, 2, 1)
    weight_grad = weight_gradient(
        zs, xs, timestep, block_input[0].T, head_outputs[0], work_weight, qw, teacher_out, noise.T,
        fake_target.T,
    )
    new_first = 0.9 * first_moment[0] + 0.1 * weight_grad
    new_second = 0.95 * second_moment[0] + 0.05 * weight_grad * weight_grad
    new_master = out_master[0] - learn_rate * (new_first / first_fix) / (
        jnp.sqrt(new_second / second_fix) + 1e-08
    )
    return (new_master[None], new_first[None], new_second[None])


def solution(mesh):
    placed = (
        P("group", "seq", "fsdp"),
        P("group", "seq", None),
        P("group", "seq", "fsdp"),
        P("group", "seq", "fsdp"),
        P("group", "seq", "fsdp"),
        P("group", None, "fsdp", "seq"),
        P("seq", "fsdp"),
        P("seq", "fsdp"),
        P(),
        P("seq", "fsdp"),
    )
    return jax.shard_map(
        body,
        mesh=mesh,
        in_specs=placed,
        out_specs=(P("group", "seq", "fsdp"), P("group", "seq", "fsdp"), P("group", "seq", "fsdp")),
        check_vma=False,
    )
```

```python
import functools
import math

import jax
import jax.numpy as jnp
from jax import lax
from jax.experimental import pallas as pl
from jax.experimental.pallas import tpu as pltpu
from jax.sharding import PartitionSpec as P

D = 2560
HEAD_DIM = 128
MESH = pl.DeviceIdType.MESH

norm_eps = 1e-06
first_fix = 1.0 - 0.9**20
second_fix = 1.0 - 0.95**20
learn_rate = 0.003


class Sends:
    def __init__(self):
        self.open = []

    def start(self, ends, send_sem, recv_sem, device, when=None):
        def make():
            src, dst = ends()
            return pltpu.make_async_remote_copy(
                src_ref=src,
                dst_ref=dst,
                send_sem=send_sem(),
                recv_sem=recv_sem(),
                device_id=device(),
                device_id_type=MESH,
            )

        make().start()
        self.open.append((make, when))

    def same(self, ref, send_sem, recv_sem, device, when=None):
        def ends():
            here = ref()
            return here, here

        self.start(ends, send_sem, recv_sem, device, when)

    def take(self):
        taken, self.open = self.open, []
        return taken

    @staticmethod
    def finish(taken):
        for make, when in taken:
            if when is None:
                make().wait_send()
            else:
                pl.when(when)(lambda make=make: make().wait_send())


def wait_recv(dst, recv_sem):
    pltpu.make_async_copy(dst, dst, recv_sem).wait()


class Ring:
    def __init__(self, sends, place, buf, rows, sems, when=None, kind=None):
        self.sends, self.place, self.buf, self.rows, self.when = sends, place, buf, rows, when
        self.kind = kind
        self.ring_send, self.ring_recv, self.pair_send, self.pair_recv = sems
        self.steps = place.zs // 2

    def piece(self, zz, cc, half):
        if self.kind == 0:
            start = (2 * zz + cc) * self.rows
            return self.buf.at[half, pl.ds(pl.multiple_of(start, 16), self.rows)]
        each = self.rows // 2
        start = (2 * zz + cc) * self.rows + half * each
        if self.kind == 1:
            return self.buf.at[:, pl.ds(pl.multiple_of(start, 16), each), :]
        return self.buf.at[pl.ds(pl.multiple_of(start, 16), each)]

    def parts(self, k):
        if k < self.steps:
            return [(0, 0), (1, 0), (0, 1), (1, 1)]
        return [(0, 0), (1, 1)]

    def zz(self, k, way):
        p = self.place
        return lax.rem(p.z + p.zs - k, p.zs) if way == 0 else lax.rem(p.z + k, p.zs)

    def send(self, k, way, half):
        p = self.place
        self.sends.same(
            lambda: self.piece(self.zz(k - 1, way), p.c, half),
            lambda: self.ring_send.at[k - 1, way, half],
            lambda: self.ring_recv.at[k - 1, way, half],
            lambda: p.dev(z=p.zp if way == 0 else p.zm),
            self.when,
        )

    def pair(self, k, way, half):
        p = self.place
        self.sends.same(
            lambda: self.piece(self.zz(k, way), p.c, half),
            lambda: self.pair_send.at[k, way, half],
            lambda: self.pair_recv.at[k, way, half],
            lambda: p.dev(c=1 - p.c),
            self.when,
        )

    def begin(self, halves=(0, 1)):
        for way, half in self.parts(1):
            if half in halves:
                self.send(1, way, half)
        for half in halves:
            self.pair(0, 0, half)

    def advance(self, k, halves=(0, 1)):
        for way, half in self.parts(k):
            if half not in halves:
                continue
            wait_recv(
                self.piece(self.zz(k, way), self.place.c, half),
                self.ring_recv.at[k - 1, way, half],
            )
            if k < self.steps and (way, half) in self.parts(k + 1):
                self.send(k + 1, way, half)
            self.pair(k, way, half)

    def pair_arrived(self, k):
        for way, half in self.parts(k) if k else [(0, 0), (0, 1)]:
            wait_recv(
                self.piece(self.zz(k, way), 1 - self.place.c, half),
                self.pair_recv.at[k, way, half],
            )


class Across:
    def __init__(self, sends, place, buf, sems):
        self.sends, self.place, self.buf = sends, place, buf
        self.send_sem, self.recv_sem = sems
        self.rows = buf.shape[1]

    def part(self, dx, other, half, quarter=None):
        p = self.place
        block = 2 * lax.rem(p.x + dx + p.xs, p.xs) + (1 - p.a if other else p.a)
        each = self.rows // 2
        start = half * each
        if quarter is not None:
            each = each // 2
            start = start + quarter * each
        return self.buf.at[block, pl.ds(start, each)]

    def go(self, n, ref, device):
        self.sends.same(ref, lambda: self.send_sem.at[n], lambda: self.recv_sem.at[n], device)

    def beside(self, way):
        p = self.place
        return p.dev(x=lax.rem(p.x + (1 if way == 0 else p.xs - 1), p.xs))

    def cross(self, half):
        p = self.place
        self.go(half, lambda: self.part(0, False, half), lambda: p.dev(a=1 - p.a))

    def crossed(self, half):
        wait_recv(self.part(0, True, half), self.recv_sem.at[half])

    def step(self, other, half):
        for way in (0, 1):
            self.go(
                2 + 4 * other + 2 * half + way,
                lambda: self.part(0, other, half),
                lambda way=way: self.beside(way),
            )

    def forward(self, other, half):
        for way in (0, 1):
            near = -1 if way == 0 else 1
            n = 4 * other + 2 * half + way
            wait_recv(self.part(near, other, half), self.recv_sem.at[2 + n])
            self.go(
                10 + n,
                lambda near=near, way=way: self.part(near, other, half, way),
                lambda way=way: self.beside(way),
            )

    def arrived(self, half):
        for other in (0, 1):
            for way in (0, 1):
                n = 4 * other + 2 * half + way
                wait_recv(self.part(2, other, half, way), self.recv_sem.at[10 + n])

    def begin(self, half):
        self.cross(half)
        self.step(0, half)


class Place:
    def __init__(self, zs, xs):
        self.zs, self.xs = zs, xs
        seq, fsdp = lax.axis_index("seq"), lax.axis_index("fsdp")
        self.g = lax.axis_index("group")
        self.z, self.a = seq // 2, lax.rem(seq, 2)
        self.x, self.c = fsdp // 2, lax.rem(fsdp, 2)
        self.zp = lax.rem(self.z + 1, zs)
        self.zm = lax.rem(self.z + zs - 1, zs)
        self.block = 2 * self.x + self.a
        self.kept = self.a == self.c
        self.moved = self.a != self.c
        self.first = self.g == 0
        self.second = self.g == 1

    def dev(self, g=None, z=None, a=None, x=None, c=None):
        g = self.g if g is None else g
        z = self.z if z is None else z
        a = self.a if a is None else a
        x = self.x if x is None else x
        c = self.c if c is None else c
        return {"group": g, "seq": 2 * z + a, "fsdp": 2 * x + c}

    def fan(self):
        return [(2 * dx + da, dx, da) for dx in range(self.xs) for da in range(2) if dx or da]

    def beside(self, dx, da):
        return self.dev(x=lax.rem(self.x + dx, self.xs), a=lax.rem(self.a + da, 2))


def kernel(
    zs,
    xs,
    ts_ref,
    bi_ref,
    ho_ref,
    ww_ref,
    qw_ref,
    to_ref,
    noise_ref,
    target_ref,
    out_ref,
    w_buf,
    q_buf,
    hob,
    bi_t,
    noise_t,
    target_t,
    gen,
    gen_in,
    noisy,
    norm,
    kv,
    q_hat,
    acc,
    lsum,
    att,
    pred,
    b_own,
    b_in,
    grad,
    tmp,
    rs_send,
    rs_recv,
    gap_f,
    gap_z,
    gap_c,
    wg_out,
    wg_in,
    t_send,
    t_recv,
    ho_send,
    ho_recv,
    ring_send,
    ring_recv,
    pair_send,
    pair_recv,
    fan_send,
    fan_recv,
    rs_ssem,
    rs_rsem,
    gf_send,
    gf_recv,
    gz_send,
    gz_recv,
    one_send,
    one_recv,
    local_sem,
):
    p = Place(zs, xs)
    sends = Sends()
    tokens, inner = ho_ref.shape
    cols = bi_ref.shape[0]
    rows = ww_ref.shape[0]
    depth = qw_ref.shape[1]
    local_inner = q_hat.shape[1]
    heads = local_inner // HEAD_DIM
    steps = zs // 2
    fans = 2 * xs
    first = p.first
    second = p.second
    f32 = jnp.float32

    barrier = pltpu.get_barrier_semaphore()
    peers = [p.dev(z=lax.rem(p.z + dz, zs)) for dz in range(1, zs)]
    peers += [p.beside(dx, da) for _, dx, da in p.fan()]
    peers += [p.dev(c=1 - p.c), p.dev(g=1 - p.g), p.dev(a=1 - p.a, c=1 - p.c)]
    for peer in peers:
        pl.semaphore_signal(barrier, inc=1, device_id=peer, device_id_type=MESH)

    own_ho = pltpu.make_async_copy(ho_ref, hob.at[p.a], local_sem.at[0])
    own_ho.start()
    pl.semaphore_wait(barrier, len(peers))

    def rows_of(buf, each, at):
        return buf.at[pl.ds(pl.multiple_of(at * each, 16), each)]

    away, home = 2 * p.z + p.a, 2 * p.z + p.c
    swaps = [
        (ww_ref, lambda i: rows_of(w_buf.at[0], rows, i)),
        (bi_ref, lambda i: bi_t),
        (qw_ref, lambda i: q_buf.at[:, pl.ds(pl.multiple_of(i * depth, 16), depth), :]),
        (noise_ref, lambda i: noise_t),
        (to_ref, lambda i: rows_of(w_buf.at[1], rows, i)),
        (target_ref, lambda i: target_t),
        (ww_ref, lambda i: rows_of(w_buf.at[1], rows, i)),
    ]

    def swap(n, when):
        src, dst = swaps[n]

        @pl.when(p.kept)
        def _():
            pltpu.make_async_copy(src, dst(away), t_recv.at[n]).start()

        @pl.when(p.moved)
        def _():
            sends.start(
                lambda: (src, dst(away)),
                lambda: t_send.at[n],
                lambda: t_recv.at[n],
                lambda: p.dev(a=p.c, c=p.a),
                when,
            )

    first_moved, second_moved = first & p.moved, second & p.moved
    first_kept, second_kept = first & p.kept, second & p.kept

    def swapped(n):
        wait_recv(swaps[n][1](home), t_recv.at[n])

    share = tokens // xs

    def ho_rows(block, dx, half=None):
        start = lax.rem(p.x + dx + xs, xs) * share
        each = share
        if half is not None:
            each = share // 2
            start = start + half * each
        return hob.at[block, pl.ds(pl.multiple_of(start, 16), each)]

    def ho_cross(when):
        @pl.when(p.kept)
        def _():
            sends.start(
                lambda: (
                    ho_ref.at[pl.ds(pl.multiple_of(p.x * share, 16), share)],
                    ho_rows(p.a, 0),
                ),
                lambda: ho_send.at[0],
                lambda: ho_recv.at[0],
                lambda: p.dev(a=1 - p.a),
                when,
            )

    def beside(way):
        return p.dev(x=lax.rem(p.x + (1 if way == 0 else xs - 1), xs))

    def ho_step(when):
        @pl.when(p.moved)
        def _():
            wait_recv(ho_rows(p.c, 0), ho_recv.at[0])
            for way in (0, 1):
                sends.same(
                    lambda: ho_rows(p.c, 0),
                    lambda way=way: ho_send.at[1 + way],
                    lambda way=way: ho_recv.at[1 + way],
                    lambda way=way: beside(way),
                    when,
                )

    def ho_forward(when):
        @pl.when(p.moved)
        def _():
            for way in (0, 1):
                near = -1 if way == 0 else 1
                wait_recv(ho_rows(p.c, near), ho_recv.at[1 + way])
                sends.same(
                    lambda near=near, way=way: ho_rows(p.c, near, way),
                    lambda way=way: ho_send.at[3 + way],
                    lambda way=way: ho_recv.at[3 + way],
                    lambda way=way: beside(way),
                    when,
                )

    def ho_arrived(when):
        @pl.when(p.moved)
        def _():
            for way in (0, 1):
                wait_recv(ho_rows(p.c, 2, way), ho_recv.at[3 + way])
            sends.same(
                lambda: hob.at[p.c],
                lambda: ho_send.at[5],
                lambda: ho_recv.at[5],
                lambda: p.dev(c=1 - p.c),
                when,
            )

    def ring(buf, each, n, when=None, kind=None):
        sems = (ring_send.at[n], ring_recv.at[n], pair_send.at[n], pair_recv.at[n])
        return Ring(sends, p, buf, each, sems, when, kind)

    ring_w = ring(w_buf.at[0], rows, 0, first)
    ring_qs = [ring(q_buf, depth, 1, first, 1), ring(q_buf, depth, 1, second, 1)]
    ring_kv = ring(kv, tokens, 2, kind=0)
    ring_ts = [ring(w_buf.at[1], rows, 3, first), ring(w_buf.at[1], rows, 3, second)]
    over_noisy = Across(sends, p, noisy, (fan_send.at[0], fan_recv.at[0]))
    over_att = Across(sends, p, att, (fan_send.at[1], fan_recv.at[1]))

    wide = 2 * rows

    def project(lhs, which, out):
        def part(j, carry):
            at = pl.ds(pl.multiple_of(j * wide, 128), wide)
            out[...] += jnp.dot(
                lhs(j, at), w_buf[which, at, :], preferred_element_type=f32
            )
            return carry

        lax.fori_loop(0, inner // wide, part, 0)

    def gap_spread():
        for rank, dx, da in p.fan():
            sends.same(
                lambda: gap_f.at[p.block],
                lambda rank=rank: gf_send.at[rank],
                lambda rank=rank: gf_recv.at[rank],
                lambda dx=dx, da=da: p.beside(dx, da),
                first,
            )

    def gap_gathered():
        for rank, dx, da in p.fan():
            block = 2 * lax.rem(p.x + xs - dx, xs) + lax.rem(p.a + da, 2)
            wait_recv(gap_f.at[block], gf_recv.at[rank])

    def predict(which):
        pred[...] = jnp.zeros_like(pred)
        project(lambda j, at: hob[p.c, :, at], which, pred)

    half_rows = [slice(0, tokens // 2), slice(tokens // 2, tokens)]
    half_cols = [slice(0, cols // 2), slice(cols // 2, cols)]

    @pl.when(first)
    def _():
        ring_q = ring_qs[0]
        swap(0, first_moved)
        ho_cross(first_kept)
        swap(1, first_moved)
        swapped(0)
        ring_w.begin()
        swap(3, first_moved)
        swap(2, first_moved)
        ring_w.advance(1)
        ho_step(first_moved)
        ring_w.advance(2)
        ring_w.advance(3)
        ho_forward(first_moved)
        swapped(2)
        ring_q.begin()
        swap(4, first_moved)
        ring_w.advance(4)
        own_ho.wait()
        ho_arrived(first_moved)
        for k in range(steps + 1):
            ring_w.pair_arrived(k)
        swapped(1)
        predict(0)
        gen[...] = (bi_t[...].astype(f32) + pred[...].T).astype(jnp.bfloat16)
        for h in (0, 1):
            sends.start(
                lambda h=h: (gen.at[half_cols[h]], gen_in.at[half_cols[h]]),
                lambda h=h: one_send.at[h],
                lambda h=h: one_recv.at[h],
                lambda: p.dev(g=1),
                first,
            )

    @pl.when(second)
    def _():
        ring_q = ring_qs[1]
        swap(2, second_moved)
        swapped(2)
        ring_q.begin()
        swap(3, second_moved)
        ring_q.advance(1)
        swap(6, second_moved)
        ring_q.advance(2)
        own_ho.wait()

    swapped(3)
    level = ts_ref[0].astype(f32) / 1000.0
    for h in (0, 1):
        at = half_cols[h]

        @pl.when(second)
        def _():
            wait_recv(gen_in.at[at], one_recv.at[h])
            gen[at, :] = gen_in[at, :]

        noisy[p.block, at, :] = (
            (1.0 - level) * gen[at, :].astype(f32) + level * noise_t[at, :].astype(f32)
        ).astype(jnp.bfloat16)
        over_noisy.begin(h)

    def first_q(k):
        pl.when(first)(lambda: ring_qs[0].advance(k))

        @pl.when(second)
        def _():
            if k == 1:
                ring_qs[1].advance(3)
            if k == 2:
                ring_qs[1].advance(4)
                swapped(6)
                ring_ts[1].begin()
            if k == 4:
                ring_ts[1].advance(1)

    def second_later(k):
        if k == 0:
            ho_cross(second_kept)
            swap(1, second_moved)
            swap(5, second_moved)
        if k == 1:
            ho_step(second_moved)
        if k == 2:
            ho_forward(second_moved)
        if k == 3:
            ho_arrived(second_moved)
        if 1 <= k <= 3:
            ring_ts[1].advance(k + 1)

    def first_t(k):
        pl.when(first)(lambda: ring_ts[0].advance(k))

    @pl.when(first)
    def _():
        pred[...] = (gen[...].astype(f32) - noisy[p.block].astype(f32)).T

    over_noisy.forward(0, 0)
    first_q(1)
    over_noisy.crossed(0)
    over_noisy.step(1, 0)
    over_noisy.forward(0, 1)
    over_noisy.crossed(1)
    over_noisy.step(1, 1)
    first_q(2)
    over_noisy.forward(1, 0)
    over_noisy.forward(1, 1)
    first_q(3)
    over_noisy.arrived(0)
    over_noisy.arrived(1)

    total = jnp.zeros((1, tokens), f32)
    for f in range(fans):
        block = noisy[f].astype(f32)
        total += jnp.sum(block * block, axis=0, keepdims=True)
    factor = lax.rsqrt(total * (1.0 / (fans * cols)) + norm_eps)
    for f in range(fans):
        norm[f * cols : (f + 1) * cols, :] = (noisy[f].astype(f32) * factor).astype(jnp.bfloat16)
    first_q(4)
    for k in range(steps + 1):
        ring_qs[0].pair_arrived(k)

    def head_norm(value):
        scale = lax.rsqrt(jnp.mean(value * value, axis=1, keepdims=True) + norm_eps)
        return (value * scale).astype(jnp.bfloat16)

    own_rows = pl.ds(pl.multiple_of(home * tokens, 16), tokens)

    def proj(n):
        return lax.dot_general(
            norm[...], q_buf[n], (((0,), (0,)), ((), ())), preferred_element_type=f32
        )

    key_raw = proj(1)
    for h in range(heads):
        at = slice(h * HEAD_DIM, (h + 1) * HEAD_DIM)
        kv[0, own_rows, at] = head_norm(key_raw[:, at])
    ring_kv.begin((0,))
    kv[1, own_rows, :] = proj(2).astype(jnp.bfloat16)
    ring_kv.begin((1,))
    query_raw = proj(0)
    for h in range(heads):
        at = slice(h * HEAD_DIM, (h + 1) * HEAD_DIM)
        q_hat[:, at] = head_norm(query_raw[:, at])
    acc[...] = jnp.zeros_like(acc)
    lsum[...] = jnp.zeros_like(lsum)

    def attend(zz):
        at = pl.ds(pl.multiple_of(zz * 2 * tokens, 16), 2 * tokens)

        def one_head(h, carry):
            cut = pl.ds(pl.multiple_of(h * HEAD_DIM, HEAD_DIM), HEAD_DIM)
            scores = lax.dot_general(
                q_hat[:, cut], kv[0, at, cut], (((1,), (1,)), ((), ())), preferred_element_type=f32
            ) * (1.0 / math.sqrt(HEAD_DIM))
            weights = jnp.exp(scores)
            part = weights[:, :128]
            for j in range(1, 2 * tokens // 128):
                part += weights[:, j * 128 : (j + 1) * 128]
            lsum[h] += part
            acc[:, cut] += jnp.dot(
                weights.astype(jnp.bfloat16), kv[1, at, cut], preferred_element_type=f32
            )
            return carry

        lax.fori_loop(0, heads, one_head, 0)

    ring_kv.pair_arrived(0)
    attend(p.z)
    pl.when(second)(lambda: second_later(0))
    for k in range(1, steps + 1):
        for half in (0, 1):
            ring_kv.advance(k, (half,))
            if k > 1:
                if half == 0:
                    ring_kv.pair_arrived(k - 1)
                attend(ring_kv.zz(k - 1, half))
        pl.when(second)(lambda: second_later(k))
        if k == steps:

            @pl.when(first)
            def _():
                swapped(4)
                ring_ts[0].begin()

    ring_kv.pair_arrived(steps)
    attend(ring_kv.zz(steps, 0))

    for half in (0, 1):
        rr = half_rows[half]
        for h in range(heads):
            at = slice(h * HEAD_DIM, (h + 1) * HEAD_DIM)
            att[p.block, rr, at] = (
                acc[rr, at] / jnp.sum(lsum[h, rr, :], axis=1, keepdims=True)
            ).astype(jnp.bfloat16)
        over_att.begin(half)
    over_att.forward(0, 0)
    first_t(1)
    over_att.crossed(0)
    over_att.step(1, 0)
    over_att.forward(0, 1)
    first_t(2)
    over_att.crossed(1)
    over_att.step(1, 1)
    over_att.forward(1, 0)
    first_t(3)
    over_att.forward(1, 1)
    first_t(4)
    for k in range(steps + 1):
        ring_ts[0].pair_arrived(k)

    early = sends.take()

    def pass_branch(h):
        sends.start(
            lambda: (b_own.at[half_rows[h]], b_in.at[half_rows[h]]),
            lambda: one_send.at[2 + h],
            lambda: one_recv.at[2 + h],
            lambda: p.dev(g=0),
            second,
        )

    for h in (0, 1):
        rr = half_rows[h]
        over_att.arrived(h)
        value = jnp.zeros((tokens // 2, cols), f32)
        for j in range(fans):
            value += jnp.dot(
                att[j, rr, :], w_buf[1, j * wide : (j + 1) * wide, :], preferred_element_type=f32
            )
        b_own[rr, :] = value

        pl.when(second)(lambda: pass_branch(h))

    def pass_grad(h):
        sends.same(
            lambda h=h: grad.at[p.c, half_rows[h]],
            lambda: one_send.at[4 + h],
            lambda: one_recv.at[4 + h],
            lambda: p.dev(c=1 - p.c),
        )

    @pl.when(second)
    def _():
        swapped(1)
        swapped(5)
        predict(1)
        grad[p.c] = (
            (pred[...] + (bi_t[...].astype(f32) - target_t[...].astype(f32)).T) * (1.0 / math.sqrt(tokens * 2 * zs))
        ).astype(jnp.bfloat16)

    @pl.when(first)
    def _():
        gap = jnp.sum(jnp.abs(pred[...] - b_own[...]))
        gap_f[p.block] = jnp.full((8, 128), gap, f32)
        gap_spread()

    sends.finish(early)
    for h in (0, 1):
        rr = half_rows[h]

        @pl.when(first)
        def _():
            wait_recv(b_in.at[rr], one_recv.at[2 + h])
            grad[p.c, rr, :] = (b_in[rr, :] - b_own[rr, :]).astype(jnp.bfloat16)

        pass_grad(h)

    @pl.when(p.kept)
    def _():
        wait_recv(hob.at[1 - p.c], ho_recv.at[5])

    for h in (0, 1):
        wait_recv(grad.at[1 - p.c, half_rows[h]], one_recv.at[4 + h])

    def partial(zz):
        at = pl.ds(pl.multiple_of(zz * wide, 128), wide)
        value = jnp.zeros((wide, cols), f32)
        for block in range(2):
            value += lax.dot_general(
                hob[block, :, at],
                grad[block],
                (((0,), (0,)), ((), ())),
                preferred_element_type=f32,
            )
        tmp[...] = value
        return tmp[pl.ds(pl.multiple_of(p.c * rows, 16), rows), :]

    each = rows // 2
    half_chunk = [slice(0, each), slice(each, rows)]

    def rs_parts(j):
        return [(0, 0), (1, 1)] if j == 1 else [(0, 1), (1, 0), (0, 0), (1, 1)]

    def rs_start(j, way, half):
        sends.start(
            lambda: (rs_send.at[j - 1, way, half], rs_recv.at[j - 1, way, half]),
            lambda: rs_ssem.at[j - 1, way, half],
            lambda: rs_rsem.at[j - 1, way, half],
            lambda: p.dev(z=p.zp if way == 0 else p.zm),
        )

    def rs_wait(j, way, half):
        wait_recv(rs_recv.at[j - 1, way, half], rs_rsem.at[j - 1, way, half])

    def gap_step(j):
        if j == 1:
            gap_gathered()
            gap_z[p.z] = jnp.sum(gap_f[...], axis=0)
            for dz in range(1, zs):
                sends.same(
                    lambda: gap_z.at[p.z],
                    lambda dz=dz: gz_send.at[dz],
                    lambda dz=dz: gz_recv.at[dz],
                    lambda dz=dz: p.dev(z=lax.rem(p.z + dz, zs)),
                    first,
                )
        if j == 2:
            for dz in range(1, zs):
                wait_recv(gap_z.at[lax.rem(p.z + zs - dz, zs)], gz_recv.at[dz])
            gap_c[p.c] = jnp.sum(gap_z[...], axis=0)
            sends.same(
                lambda: gap_c.at[p.c],
                lambda: one_send.at[6],
                lambda: one_recv.at[6],
                lambda: p.dev(c=1 - p.c),
                first,
            )
        if j == 3:
            wait_recv(gap_c.at[1 - p.c], one_recv.at[6])

    far = partial(lax.rem(p.z + steps, zs))
    for way, half in rs_parts(1):
        rs_send[0, way, half] = far[half_chunk[half]].astype(jnp.bfloat16)
        rs_start(1, way, half)
    for j in range(2, steps + 1):
        dist = steps - j + 1
        mine = [partial(lax.rem(p.z + dist, zs)), partial(lax.rem(p.z + zs - dist, zs))]
        for way, half in rs_parts(j):
            value = mine[way][half_chunk[half]]
            if (way, half) in rs_parts(j - 1):
                rs_wait(j - 1, way, half)
                value = value + rs_recv[j - 2, way, half].astype(f32)
            rs_send[j - 1, way, half] = value.astype(jnp.bfloat16)
            rs_start(j, way, half)
        if j == 2:
            pl.when(first)(lambda: gap_step(1))
        if j == 3:
            pl.when(first)(lambda: gap_step(2))
    mine = partial(p.z)
    pl.when(first)(lambda: gap_step(3))
    acc_w = tmp.at[0:rows]
    acc_w[...] = mine
    for way, half in rs_parts(2):
        rs_wait(steps, way, half)
        at = half_chunk[half]
        acc_w[at, :] = acc_w[at, :] + rs_recv[steps - 1, way, half].astype(f32)

    @pl.when(first)
    def _():
        gap = (gap_c[0] + gap_c[1])[0:1, 0:1] * (1.0 / (tokens * 2 * zs * fans * cols))
        wg_out[...] = (acc_w[...] * (1.0 / (gap + norm_eps))).astype(jnp.bfloat16)

    @pl.when(second)
    def _():
        wg_out[...] = acc_w[...].astype(jnp.bfloat16)

    @pl.when(p.moved)
    def _():
        sends.start(
            lambda: (wg_out, wg_in),
            lambda: one_send.at[7],
            lambda: one_recv.at[7],
            lambda: p.dev(a=p.c, c=p.a),
            p.moved,
        )
        wait_recv(wg_in, one_recv.at[7])
        out_ref[...] = wg_in[...].astype(f32)

    @pl.when(p.kept)
    def _():
        out_ref[...] = wg_out[...].astype(f32)

    sends.finish(sends.take())


def weight_gradient(zs, xs, ts, bi, ho, ww, qw, to, noise, target, interpret=None):
    tokens, inner = ho.shape
    cols = bi.shape[0]
    rows = ww.shape[0]
    depth, local_inner = qw.shape[1:]
    heads = local_inner // HEAD_DIM
    seq, fans, steps = 2 * zs, 2 * xs, zs // 2
    b16, f32 = jnp.bfloat16, jnp.float32
    vmem, dma = pltpu.VMEM, pltpu.SemaphoreType.DMA
    scratch = [
        vmem((2, inner, cols), b16),
        vmem((3, seq * depth, local_inner), b16),
        vmem((2, tokens, inner), b16),
        vmem((cols, tokens), b16),
        vmem((cols, tokens), b16),
        vmem((cols, tokens), b16),
        vmem((cols, tokens), b16),
        vmem((cols, tokens), b16),
        vmem((fans, cols, tokens), b16),
        vmem((fans * cols, tokens), b16),
        vmem((2, seq * tokens, local_inner), b16),
        vmem((tokens, local_inner), b16),
        vmem((tokens, local_inner), f32),
        vmem((heads, tokens, 128), f32),
        vmem((fans, tokens, local_inner), b16),
        vmem((tokens, cols), f32),
        vmem((tokens, cols), f32),
        vmem((tokens, cols), f32),
        vmem((2, tokens, cols), b16),
        vmem((2 * rows, cols), f32),
        vmem((steps, 2, 2, rows // 2, cols), b16),
        vmem((steps, 2, 2, rows // 2, cols), b16),
        vmem((fans, 8, 128), f32),
        vmem((zs, 8, 128), f32),
        vmem((2, 8, 128), f32),
        vmem((rows, cols), b16),
        vmem((rows, cols), b16),
        dma((7,)),
        dma((7,)),
        dma((6,)),
        dma((6,)),
        dma((4, steps, 2, 2)),
        dma((4, steps, 2, 2)),
        dma((4, steps + 1, 2, 2)),
        dma((4, steps + 1, 2, 2)),
        dma((2, 18)),
        dma((2, 18)),
        dma((steps, 2, 2)),
        dma((steps, 2, 2)),
        dma((fans,)),
        dma((fans,)),
        dma((zs,)),
        dma((zs,)),
        dma((8,)),
        dma((8,)),
        dma((1,)),
    ]
    in_vmem = pl.BlockSpec(memory_space=pltpu.VMEM)
    return pl.pallas_call(
        functools.partial(kernel, zs, xs),
        out_shape=jax.ShapeDtypeStruct((rows, cols), f32),
        in_specs=[pl.BlockSpec(memory_space=pltpu.SMEM)] + [pl.BlockSpec(memory_space=pl.ANY)] * 7,
        out_specs=in_vmem,
        scratch_shapes=scratch,
        compiler_params=pltpu.CompilerParams(
            collective_id=0, has_side_effects=True, vmem_limit_bytes=62 * 1024 * 1024
        ),
        name="weight_gradient",
    )(ts, bi, ho, ww, qw, to, noise, target)


def body(
    block_input,
    head_outputs,
    out_master,
    first_moment,
    second_moment,
    score_qkv,
    teacher_out,
    noise,
    timestep,
    fake_target,
):
    zs, xs = lax.axis_size("seq") // 2, lax.axis_size("fsdp") // 2
    work_weight = out_master[0].astype(jnp.bfloat16)
    qw = score_qkv[0].transpose(0, 2, 1)
    weight_grad = weight_gradient(
        zs, xs, timestep, block_input[0].T, head_outputs[0], work_weight, qw, teacher_out, noise.T,
        fake_target.T,
    )
    new_first = 0.9 * first_moment[0] + 0.1 * weight_grad
    new_second = 0.95 * second_moment[0] + 0.05 * weight_grad * weight_grad
    new_master = out_master[0] - learn_rate * (new_first / first_fix) / (
        jnp.sqrt(new_second / second_fix) + 1e-08
    )
    return (new_master[None], new_first[None], new_second[None])


def solution(mesh):
    placed = (
        P("group", "seq", "fsdp"),
        P("group", "seq", None),
        P("group", "seq", "fsdp"),
        P("group", "seq", "fsdp"),
        P("group", "seq", "fsdp"),
        P("group", None, "fsdp", "seq"),
        P("seq", "fsdp"),
        P("seq", "fsdp"),
        P(),
        P("seq", "fsdp"),
    )
    return jax.shard_map(
        body,
        mesh=mesh,
        in_specs=placed,
        out_specs=(P("group", "seq", "fsdp"), P("group", "seq", "fsdp"), P("group", "seq", "fsdp")),
        check_vma=False,
    )
```

```python
import functools
import math

import jax
import jax.numpy as jnp
from jax import lax
from jax.experimental import pallas as pl
from jax.experimental.pallas import tpu as pltpu
from jax.sharding import PartitionSpec as P

D = 2560
HEAD_DIM = 128
MESH = pl.DeviceIdType.MESH

norm_eps = 1e-06
first_fix = 1.0 - 0.9**20
second_fix = 1.0 - 0.95**20
learn_rate = 0.003


class Sends:
    def __init__(self):
        self.open = []

    def start(self, ends, send_sem, recv_sem, device, when=None):
        def make():
            src, dst = ends()
            return pltpu.make_async_remote_copy(
                src_ref=src,
                dst_ref=dst,
                send_sem=send_sem(),
                recv_sem=recv_sem(),
                device_id=device(),
                device_id_type=MESH,
            )

        make().start()
        self.open.append((make, when))

    def same(self, ref, send_sem, recv_sem, device, when=None):
        def ends():
            here = ref()
            return here, here

        self.start(ends, send_sem, recv_sem, device, when)

    def take(self):
        taken, self.open = self.open, []
        return taken

    @staticmethod
    def finish(taken):
        for make, when in taken:
            if when is None:
                make().wait_send()
            else:
                pl.when(when)(lambda make=make: make().wait_send())


def wait_recv(dst, recv_sem):
    pltpu.make_async_copy(dst, dst, recv_sem).wait()


class Ring:
    def __init__(self, sends, place, buf, rows, sems, when=None, kind=None):
        self.sends, self.place, self.buf, self.rows, self.when = sends, place, buf, rows, when
        self.kind = kind
        self.ring_send, self.ring_recv, self.pair_send, self.pair_recv = sems
        self.steps = place.zs // 2

    def piece(self, zz, cc, half):
        if self.kind == 0:
            start = (2 * zz + cc) * self.rows
            return self.buf.at[half, pl.ds(pl.multiple_of(start, 16), self.rows)]
        each = self.rows // 2
        start = (2 * zz + cc) * self.rows + half * each
        if self.kind == 1:
            return self.buf.at[:, pl.ds(pl.multiple_of(start, 16), each), :]
        return self.buf.at[pl.ds(pl.multiple_of(start, 16), each)]

    def parts(self, k):
        if k < self.steps:
            return [(0, 0), (1, 0), (0, 1), (1, 1)]
        return [(0, 0), (1, 1)]

    def zz(self, k, way):
        p = self.place
        return lax.rem(p.z + p.zs - k, p.zs) if way == 0 else lax.rem(p.z + k, p.zs)

    def send(self, k, way, half):
        p = self.place
        self.sends.same(
            lambda: self.piece(self.zz(k - 1, way), p.c, half),
            lambda: self.ring_send.at[k - 1, way, half],
            lambda: self.ring_recv.at[k - 1, way, half],
            lambda: p.dev(z=p.zp if way == 0 else p.zm),
            self.when,
        )

    def pair(self, k, way, half):
        p = self.place
        self.sends.same(
            lambda: self.piece(self.zz(k, way), p.c, half),
            lambda: self.pair_send.at[k, way, half],
            lambda: self.pair_recv.at[k, way, half],
            lambda: p.dev(c=1 - p.c),
            self.when,
        )

    def begin(self, halves=(0, 1)):
        for way, half in self.parts(1):
            if half in halves:
                self.send(1, way, half)
        for half in halves:
            self.pair(0, 0, half)

    def advance(self, k, halves=(0, 1)):
        for way, half in self.parts(k):
            if half not in halves:
                continue
            wait_recv(
                self.piece(self.zz(k, way), self.place.c, half),
                self.ring_recv.at[k - 1, way, half],
            )
            if k < self.steps and (way, half) in self.parts(k + 1):
                self.send(k + 1, way, half)
            self.pair(k, way, half)

    def pair_arrived(self, k):
        for way, half in self.parts(k) if k else [(0, 0), (0, 1)]:
            wait_recv(
                self.piece(self.zz(k, way), 1 - self.place.c, half),
                self.pair_recv.at[k, way, half],
            )


class Across:
    def __init__(self, sends, place, buf, sems):
        self.sends, self.place, self.buf = sends, place, buf
        self.send_sem, self.recv_sem = sems
        self.rows = buf.shape[1]

    def part(self, dx, other, half, quarter=None):
        p = self.place
        block = 2 * lax.rem(p.x + dx + p.xs, p.xs) + (1 - p.a if other else p.a)
        each = self.rows // 2
        start = half * each
        if quarter is not None:
            each = each // 2
            start = start + quarter * each
        return self.buf.at[block, pl.ds(start, each)]

    def go(self, n, ref, device):
        self.sends.same(ref, lambda: self.send_sem.at[n], lambda: self.recv_sem.at[n], device)

    def beside(self, way):
        p = self.place
        return p.dev(x=lax.rem(p.x + (1 if way == 0 else p.xs - 1), p.xs))

    def cross(self, half):
        p = self.place
        self.go(half, lambda: self.part(0, False, half), lambda: p.dev(a=1 - p.a))

    def crossed(self, half):
        wait_recv(self.part(0, True, half), self.recv_sem.at[half])

    def step(self, other, half):
        for way in (0, 1):
            self.go(
                2 + 4 * other + 2 * half + way,
                lambda: self.part(0, other, half),
                lambda way=way: self.beside(way),
            )

    def forward(self, other, half):
        for way in (0, 1):
            near = -1 if way == 0 else 1
            n = 4 * other + 2 * half + way
            wait_recv(self.part(near, other, half), self.recv_sem.at[2 + n])
            self.go(
                10 + n,
                lambda near=near, way=way: self.part(near, other, half, way),
                lambda way=way: self.beside(way),
            )

    def arrived(self, half):
        for other in (0, 1):
            for way in (0, 1):
                n = 4 * other + 2 * half + way
                wait_recv(self.part(2, other, half, way), self.recv_sem.at[10 + n])

    def begin(self, half):
        self.cross(half)
        self.step(0, half)


class Place:
    def __init__(self, zs, xs):
        self.zs, self.xs = zs, xs
        seq, fsdp = lax.axis_index("seq"), lax.axis_index("fsdp")
        self.g = lax.axis_index("group")
        self.z, self.a = seq // 2, lax.rem(seq, 2)
        self.x, self.c = fsdp // 2, lax.rem(fsdp, 2)
        self.zp = lax.rem(self.z + 1, zs)
        self.zm = lax.rem(self.z + zs - 1, zs)
        self.block = 2 * self.x + self.a
        self.kept = self.a == self.c
        self.moved = self.a != self.c
        self.first = self.g == 0
        self.second = self.g == 1

    def dev(self, g=None, z=None, a=None, x=None, c=None):
        g = self.g if g is None else g
        z = self.z if z is None else z
        a = self.a if a is None else a
        x = self.x if x is None else x
        c = self.c if c is None else c
        return {"group": g, "seq": 2 * z + a, "fsdp": 2 * x + c}

    def fan(self):
        return [(2 * dx + da, dx, da) for dx in range(self.xs) for da in range(2) if dx or da]

    def beside(self, dx, da):
        return self.dev(x=lax.rem(self.x + dx, self.xs), a=lax.rem(self.a + da, 2))


def kernel(
    zs,
    xs,
    ts_ref,
    bi_ref,
    ho_ref,
    ww_ref,
    qw_ref,
    to_ref,
    noise_ref,
    target_ref,
    out_ref,
    w_buf,
    q_buf,
    hob,
    bi_t,
    noise_t,
    target_t,
    gen,
    gen_in,
    noisy,
    norm,
    kv,
    q_hat,
    acc,
    lsum,
    att,
    pred,
    b_own,
    b_in,
    grad,
    tmp,
    rs_send,
    rs_recv,
    gap_f,
    gap_z,
    gap_c,
    wg_out,
    wg_in,
    t_send,
    t_recv,
    ho_send,
    ho_recv,
    ring_send,
    ring_recv,
    pair_send,
    pair_recv,
    fan_send,
    fan_recv,
    rs_ssem,
    rs_rsem,
    gf_send,
    gf_recv,
    gz_send,
    gz_recv,
    one_send,
    one_recv,
    local_sem,
):
    p = Place(zs, xs)
    sends = Sends()
    tokens, inner = ho_ref.shape
    cols = bi_ref.shape[0]
    rows = ww_ref.shape[0]
    depth = qw_ref.shape[1]
    local_inner = q_hat.shape[1]
    heads = local_inner // HEAD_DIM
    steps = zs // 2
    fans = 2 * xs
    first = p.first
    second = p.second
    f32 = jnp.float32

    barrier = pltpu.get_barrier_semaphore()
    peers = [p.dev(z=lax.rem(p.z + dz, zs)) for dz in range(1, zs)]
    peers += [p.beside(dx, da) for _, dx, da in p.fan()]
    peers += [p.dev(c=1 - p.c), p.dev(g=1 - p.g), p.dev(a=1 - p.a, c=1 - p.c)]
    for peer in peers:
        pl.semaphore_signal(barrier, inc=1, device_id=peer, device_id_type=MESH)

    own_ho = pltpu.make_async_copy(ho_ref, hob.at[p.a], local_sem.at[0])
    own_ho.start()
    pl.semaphore_wait(barrier, len(peers))

    def rows_of(buf, each, at):
        return buf.at[pl.ds(pl.multiple_of(at * each, 16), each)]

    away, home = 2 * p.z + p.a, 2 * p.z + p.c
    swaps = [
        (ww_ref, lambda i: rows_of(w_buf.at[0], rows, i)),
        (bi_ref, lambda i: bi_t),
        (qw_ref, lambda i: q_buf.at[:, pl.ds(pl.multiple_of(i * depth, 16), depth), :]),
        (noise_ref, lambda i: noise_t),
        (to_ref, lambda i: rows_of(w_buf.at[1], rows, i)),
        (target_ref, lambda i: target_t),
        (ww_ref, lambda i: rows_of(w_buf.at[1], rows, i)),
    ]

    def swap(n, when):
        src, dst = swaps[n]

        @pl.when(p.kept)
        def _():
            pltpu.make_async_copy(src, dst(away), t_recv.at[n]).start()

        @pl.when(p.moved)
        def _():
            sends.start(
                lambda: (src, dst(away)),
                lambda: t_send.at[n],
                lambda: t_recv.at[n],
                lambda: p.dev(a=p.c, c=p.a),
                when,
            )

    first_moved, second_moved = first & p.moved, second & p.moved
    first_kept, second_kept = first & p.kept, second & p.kept

    def swapped(n):
        wait_recv(swaps[n][1](home), t_recv.at[n])

    share = tokens // xs

    def ho_rows(block, dx, half=None):
        start = lax.rem(p.x + dx + xs, xs) * share
        each = share
        if half is not None:
            each = share // 2
            start = start + half * each
        return hob.at[block, pl.ds(pl.multiple_of(start, 16), each)]

    def ho_cross(when):
        @pl.when(p.kept)
        def _():
            sends.start(
                lambda: (
                    ho_ref.at[pl.ds(pl.multiple_of(p.x * share, 16), share)],
                    ho_rows(p.a, 0),
                ),
                lambda: ho_send.at[0],
                lambda: ho_recv.at[0],
                lambda: p.dev(a=1 - p.a),
                when,
            )

    def beside(way):
        return p.dev(x=lax.rem(p.x + (1 if way == 0 else xs - 1), xs))

    def ho_step(when):
        @pl.when(p.moved)
        def _():
            wait_recv(ho_rows(p.c, 0), ho_recv.at[0])
            for way in (0, 1):
                sends.same(
                    lambda: ho_rows(p.c, 0),
                    lambda way=way: ho_send.at[1 + way],
                    lambda way=way: ho_recv.at[1 + way],
                    lambda way=way: beside(way),
                    when,
                )

    def ho_forward(when):
        @pl.when(p.moved)
        def _():
            for way in (0, 1):
                near = -1 if way == 0 else 1
                wait_recv(ho_rows(p.c, near), ho_recv.at[1 + way])
                sends.same(
                    lambda near=near, way=way: ho_rows(p.c, near, way),
                    lambda way=way: ho_send.at[3 + way],
                    lambda way=way: ho_recv.at[3 + way],
                    lambda way=way: beside(way),
                    when,
                )

    def ho_arrived(when):
        @pl.when(p.moved)
        def _():
            for way in (0, 1):
                wait_recv(ho_rows(p.c, 2, way), ho_recv.at[3 + way])
            sends.same(
                lambda: hob.at[p.c],
                lambda: ho_send.at[5],
                lambda: ho_recv.at[5],
                lambda: p.dev(c=1 - p.c),
                when,
            )

    def ring(buf, each, n, when=None, kind=None):
        sems = (ring_send.at[n], ring_recv.at[n], pair_send.at[n], pair_recv.at[n])
        return Ring(sends, p, buf, each, sems, when, kind)

    ring_w = ring(w_buf.at[0], rows, 0, first)
    ring_qs = [ring(q_buf, depth, 1, first, 1), ring(q_buf, depth, 1, second, 1)]
    ring_kv = ring(kv, tokens, 2, kind=0)
    ring_ts = [ring(w_buf.at[1], rows, 3, first), ring(w_buf.at[1], rows, 3, second)]
    over_noisy = Across(sends, p, noisy, (fan_send.at[0], fan_recv.at[0]))
    over_att = Across(sends, p, att, (fan_send.at[1], fan_recv.at[1]))

    wide = 2 * rows

    def project(lhs, which, out):
        def part(j, carry):
            at = pl.ds(pl.multiple_of(j * wide, 128), wide)
            out[...] += jnp.dot(
                lhs(j, at), w_buf[which, at, :], preferred_element_type=f32
            )
            return carry

        lax.fori_loop(0, inner // wide, part, 0)

    def gap_spread():
        for rank, dx, da in p.fan():
            sends.same(
                lambda: gap_f.at[p.block],
                lambda rank=rank: gf_send.at[rank],
                lambda rank=rank: gf_recv.at[rank],
                lambda dx=dx, da=da: p.beside(dx, da),
                first,
            )

    def gap_gathered():
        for rank, dx, da in p.fan():
            block = 2 * lax.rem(p.x + xs - dx, xs) + lax.rem(p.a + da, 2)
            wait_recv(gap_f.at[block], gf_recv.at[rank])

    def predict(which):
        pred[...] = jnp.zeros_like(pred)
        project(lambda j, at: hob[p.c, :, at], which, pred)

    half_rows = [slice(0, tokens // 2), slice(tokens // 2, tokens)]
    half_cols = [slice(0, cols // 2), slice(cols // 2, cols)]

    @pl.when(first)
    def _():
        ring_q = ring_qs[0]
        swap(0, first_moved)
        ho_cross(first_kept)
        swapped(0)
        ring_w.begin()
        ring_w.advance(1)
        ho_step(first_moved)
        swap(2, first_moved)
        swap(1, first_moved)
        swap(3, first_moved)
        ring_w.advance(2)
        ring_w.advance(3)
        ho_forward(first_moved)
        swapped(2)
        ring_q.begin()
        swap(4, first_moved)
        ring_w.advance(4)
        own_ho.wait()
        ho_arrived(first_moved)
        for k in range(steps + 1):
            ring_w.pair_arrived(k)
        swapped(1)
        predict(0)
        gen[...] = (bi_t[...].astype(f32) + pred[...].T).astype(jnp.bfloat16)
        for h in (0, 1):
            sends.start(
                lambda h=h: (gen.at[half_cols[h]], gen_in.at[half_cols[h]]),
                lambda h=h: one_send.at[h],
                lambda h=h: one_recv.at[h],
                lambda: p.dev(g=1),
                first,
            )

    @pl.when(second)
    def _():
        ring_q = ring_qs[1]
        swap(2, second_moved)
        swapped(2)
        ring_q.begin()
        swap(3, second_moved)
        ring_q.advance(1)
        swap(6, second_moved)
        ring_q.advance(2)
        own_ho.wait()

    swapped(3)
    level = ts_ref[0].astype(f32) / 1000.0
    for h in (0, 1):
        at = half_cols[h]

        @pl.when(second)
        def _():
            wait_recv(gen_in.at[at], one_recv.at[h])
            gen[at, :] = gen_in[at, :]

        noisy[p.block, at, :] = (
            (1.0 - level) * gen[at, :].astype(f32) + level * noise_t[at, :].astype(f32)
        ).astype(jnp.bfloat16)
        over_noisy.begin(h)

    def first_q(k):
        pl.when(first)(lambda: ring_qs[0].advance(k))

        @pl.when(second)
        def _():
            if k == 1:
                ring_qs[1].advance(3)
            if k == 2:
                ring_qs[1].advance(4)
                swapped(6)
                ring_ts[1].begin()
            if k == 4:
                ring_ts[1].advance(1)

    def second_later(k):
        if k == 0:
            ho_cross(second_kept)
            swap(1, second_moved)
            swap(5, second_moved)
        if k == 1:
            ho_step(second_moved)
        if k == 2:
            ho_forward(second_moved)
        if k == 3:
            ho_arrived(second_moved)
        if 1 <= k <= 3:
            ring_ts[1].advance(k + 1)

    def first_t(k):
        pl.when(first)(lambda: ring_ts[0].advance(k))

    @pl.when(first)
    def _():
        pred[...] = (gen[...].astype(f32) - noisy[p.block].astype(f32)).T

    over_noisy.forward(0, 0)
    first_q(1)
    over_noisy.crossed(0)
    over_noisy.step(1, 0)
    over_noisy.forward(0, 1)
    over_noisy.crossed(1)
    over_noisy.step(1, 1)
    first_q(2)
    over_noisy.forward(1, 0)
    over_noisy.forward(1, 1)
    first_q(3)
    over_noisy.arrived(0)
    over_noisy.arrived(1)

    total = jnp.zeros((1, tokens), f32)
    for f in range(fans):
        block = noisy[f].astype(f32)
        total += jnp.sum(block * block, axis=0, keepdims=True)
    factor = lax.rsqrt(total * (1.0 / (fans * cols)) + norm_eps)
    for f in range(fans):
        norm[f * cols : (f + 1) * cols, :] = (noisy[f].astype(f32) * factor).astype(jnp.bfloat16)
    first_q(4)
    for k in range(steps + 1):
        ring_qs[0].pair_arrived(k)

    def head_norm(value):
        scale = lax.rsqrt(jnp.mean(value * value, axis=1, keepdims=True) + norm_eps)
        return (value * scale).astype(jnp.bfloat16)

    own_rows = pl.ds(pl.multiple_of(home * tokens, 16), tokens)

    def proj(n):
        return lax.dot_general(
            norm[...], q_buf[n], (((0,), (0,)), ((), ())), preferred_element_type=f32
        )

    key_raw = proj(1)
    for h in range(heads):
        at = slice(h * HEAD_DIM, (h + 1) * HEAD_DIM)
        kv[0, own_rows, at] = head_norm(key_raw[:, at])
    ring_kv.begin((0,))
    kv[1, own_rows, :] = proj(2).astype(jnp.bfloat16)
    ring_kv.begin((1,))
    query_raw = proj(0)
    for h in range(heads):
        at = slice(h * HEAD_DIM, (h + 1) * HEAD_DIM)
        q_hat[:, at] = head_norm(query_raw[:, at])
    acc[...] = jnp.zeros_like(acc)
    lsum[...] = jnp.zeros_like(lsum)

    def attend(zz):
        at = pl.ds(pl.multiple_of(zz * 2 * tokens, 16), 2 * tokens)

        def one_head(h, carry):
            cut = pl.ds(pl.multiple_of(h * HEAD_DIM, HEAD_DIM), HEAD_DIM)
            scores = lax.dot_general(
                q_hat[:, cut], kv[0, at, cut], (((1,), (1,)), ((), ())), preferred_element_type=f32
            ) * (1.0 / math.sqrt(HEAD_DIM))
            weights = jnp.exp(scores)
            part = weights[:, :128]
            for j in range(1, 2 * tokens // 128):
                part += weights[:, j * 128 : (j + 1) * 128]
            lsum[h] += part
            acc[:, cut] += jnp.dot(
                weights.astype(jnp.bfloat16), kv[1, at, cut], preferred_element_type=f32
            )
            return carry

        lax.fori_loop(0, heads, one_head, 0)

    ring_kv.pair_arrived(0)
    attend(p.z)
    pl.when(second)(lambda: second_later(0))
    for k in range(1, steps + 1):
        for half in (0, 1):
            ring_kv.advance(k, (half,))
            if k > 1:
                if half == 0:
                    ring_kv.pair_arrived(k - 1)
                attend(ring_kv.zz(k - 1, half))
        pl.when(second)(lambda: second_later(k))
        if k == steps:

            @pl.when(first)
            def _():
                swapped(4)
                ring_ts[0].begin()

    ring_kv.pair_arrived(steps)
    attend(ring_kv.zz(steps, 0))

    for half in (0, 1):
        rr = half_rows[half]
        for h in range(heads):
            at = slice(h * HEAD_DIM, (h + 1) * HEAD_DIM)
            att[p.block, rr, at] = (
                acc[rr, at] / jnp.sum(lsum[h, rr, :], axis=1, keepdims=True)
            ).astype(jnp.bfloat16)
        over_att.begin(half)
    over_att.forward(0, 0)
    first_t(1)
    over_att.crossed(0)
    over_att.step(1, 0)
    over_att.forward(0, 1)
    first_t(2)
    over_att.crossed(1)
    over_att.step(1, 1)
    over_att.forward(1, 0)
    first_t(3)
    over_att.forward(1, 1)
    first_t(4)
    for k in range(steps + 1):
        ring_ts[0].pair_arrived(k)

    early = sends.take()

    def pass_branch(h):
        sends.start(
            lambda: (b_own.at[half_rows[h]], b_in.at[half_rows[h]]),
            lambda: one_send.at[2 + h],
            lambda: one_recv.at[2 + h],
            lambda: p.dev(g=0),
            second,
        )

    for h in (0, 1):
        rr = half_rows[h]
        over_att.arrived(h)
        value = jnp.zeros((tokens // 2, cols), f32)
        for j in range(fans):
            value += jnp.dot(
                att[j, rr, :], w_buf[1, j * wide : (j + 1) * wide, :], preferred_element_type=f32
            )
        b_own[rr, :] = value

        pl.when(second)(lambda: pass_branch(h))

    def pass_grad(h):
        sends.same(
            lambda h=h: grad.at[p.c, half_rows[h]],
            lambda: one_send.at[4 + h],
            lambda: one_recv.at[4 + h],
            lambda: p.dev(c=1 - p.c),
        )

    @pl.when(second)
    def _():
        swapped(1)
        swapped(5)
        predict(1)
        grad[p.c] = (
            (pred[...] + (bi_t[...].astype(f32) - target_t[...].astype(f32)).T) * (1.0 / math.sqrt(tokens * 2 * zs))
        ).astype(jnp.bfloat16)

    @pl.when(first)
    def _():
        gap = jnp.sum(jnp.abs(pred[...] - b_own[...]))
        gap_f[p.block] = jnp.full((8, 128), gap, f32)
        gap_spread()

    sends.finish(early)
    for h in (0, 1):
        rr = half_rows[h]

        @pl.when(first)
        def _():
            wait_recv(b_in.at[rr], one_recv.at[2 + h])
            grad[p.c, rr, :] = (b_in[rr, :] - b_own[rr, :]).astype(jnp.bfloat16)

        pass_grad(h)

    @pl.when(p.kept)
    def _():
        wait_recv(hob.at[1 - p.c], ho_recv.at[5])

    for h in (0, 1):
        wait_recv(grad.at[1 - p.c, half_rows[h]], one_recv.at[4 + h])

    def partial(zz):
        at = pl.ds(pl.multiple_of(zz * wide, 128), wide)
        value = jnp.zeros((wide, cols), f32)
        for block in range(2):
            value += lax.dot_general(
                hob[block, :, at],
                grad[block],
                (((0,), (0,)), ((), ())),
                preferred_element_type=f32,
            )
        tmp[...] = value
        return tmp[pl.ds(pl.multiple_of(p.c * rows, 16), rows), :]

    each = rows // 2
    half_chunk = [slice(0, each), slice(each, rows)]

    def rs_parts(j):
        return [(0, 0), (1, 1)] if j == 1 else [(0, 1), (1, 0), (0, 0), (1, 1)]

    def rs_start(j, way, half):
        sends.start(
            lambda: (rs_send.at[j - 1, way, half], rs_recv.at[j - 1, way, half]),
            lambda: rs_ssem.at[j - 1, way, half],
            lambda: rs_rsem.at[j - 1, way, half],
            lambda: p.dev(z=p.zp if way == 0 else p.zm),
        )

    def rs_wait(j, way, half):
        wait_recv(rs_recv.at[j - 1, way, half], rs_rsem.at[j - 1, way, half])

    def gap_step(j):
        if j == 1:
            gap_gathered()
            gap_z[p.z] = jnp.sum(gap_f[...], axis=0)
            for dz in range(1, zs):
                sends.same(
                    lambda: gap_z.at[p.z],
                    lambda dz=dz: gz_send.at[dz],
                    lambda dz=dz: gz_recv.at[dz],
                    lambda dz=dz: p.dev(z=lax.rem(p.z + dz, zs)),
                    first,
                )
        if j == 2:
            for dz in range(1, zs):
                wait_recv(gap_z.at[lax.rem(p.z + zs - dz, zs)], gz_recv.at[dz])
            gap_c[p.c] = jnp.sum(gap_z[...], axis=0)
            sends.same(
                lambda: gap_c.at[p.c],
                lambda: one_send.at[6],
                lambda: one_recv.at[6],
                lambda: p.dev(c=1 - p.c),
                first,
            )
        if j == 3:
            wait_recv(gap_c.at[1 - p.c], one_recv.at[6])

    far = partial(lax.rem(p.z + steps, zs))
    for way, half in rs_parts(1):
        rs_send[0, way, half] = far[half_chunk[half]].astype(jnp.bfloat16)
        rs_start(1, way, half)
    for j in range(2, steps + 1):
        dist = steps - j + 1
        mine = [partial(lax.rem(p.z + dist, zs)), partial(lax.rem(p.z + zs - dist, zs))]
        for way, half in rs_parts(j):
            value = mine[way][half_chunk[half]]
            if (way, half) in rs_parts(j - 1):
                rs_wait(j - 1, way, half)
                value = value + rs_recv[j - 2, way, half].astype(f32)
            rs_send[j - 1, way, half] = value.astype(jnp.bfloat16)
            rs_start(j, way, half)
        if j == 2:
            pl.when(first)(lambda: gap_step(1))
        if j == 3:
            pl.when(first)(lambda: gap_step(2))
    mine = partial(p.z)
    pl.when(first)(lambda: gap_step(3))
    acc_w = tmp.at[0:rows]
    acc_w[...] = mine
    for way, half in rs_parts(2):
        rs_wait(steps, way, half)
        at = half_chunk[half]
        acc_w[at, :] = acc_w[at, :] + rs_recv[steps - 1, way, half].astype(f32)

    @pl.when(first)
    def _():
        gap = (gap_c[0] + gap_c[1])[0:1, 0:1] * (1.0 / (tokens * 2 * zs * fans * cols))
        wg_out[...] = (acc_w[...] * (1.0 / (gap + norm_eps))).astype(jnp.bfloat16)

    @pl.when(second)
    def _():
        wg_out[...] = acc_w[...].astype(jnp.bfloat16)

    @pl.when(p.moved)
    def _():
        sends.start(
            lambda: (wg_out, wg_in),
            lambda: one_send.at[7],
            lambda: one_recv.at[7],
            lambda: p.dev(a=p.c, c=p.a),
            p.moved,
        )
        wait_recv(wg_in, one_recv.at[7])
        out_ref[...] = wg_in[...].astype(f32)

    @pl.when(p.kept)
    def _():
        out_ref[...] = wg_out[...].astype(f32)

    sends.finish(sends.take())


def weight_gradient(zs, xs, ts, bi, ho, ww, qw, to, noise, target, interpret=None):
    tokens, inner = ho.shape
    cols = bi.shape[0]
    rows = ww.shape[0]
    depth, local_inner = qw.shape[1:]
    heads = local_inner // HEAD_DIM
    seq, fans, steps = 2 * zs, 2 * xs, zs // 2
    b16, f32 = jnp.bfloat16, jnp.float32
    vmem, dma = pltpu.VMEM, pltpu.SemaphoreType.DMA
    scratch = [
        vmem((2, inner, cols), b16),
        vmem((3, seq * depth, local_inner), b16),
        vmem((2, tokens, inner), b16),
        vmem((cols, tokens), b16),
        vmem((cols, tokens), b16),
        vmem((cols, tokens), b16),
        vmem((cols, tokens), b16),
        vmem((cols, tokens), b16),
        vmem((fans, cols, tokens), b16),
        vmem((fans * cols, tokens), b16),
        vmem((2, seq * tokens, local_inner), b16),
        vmem((tokens, local_inner), b16),
        vmem((tokens, local_inner), f32),
        vmem((heads, tokens, 128), f32),
        vmem((fans, tokens, local_inner), b16),
        vmem((tokens, cols), f32),
        vmem((tokens, cols), f32),
        vmem((tokens, cols), f32),
        vmem((2, tokens, cols), b16),
        vmem((2 * rows, cols), f32),
        vmem((steps, 2, 2, rows // 2, cols), b16),
        vmem((steps, 2, 2, rows // 2, cols), b16),
        vmem((fans, 8, 128), f32),
        vmem((zs, 8, 128), f32),
        vmem((2, 8, 128), f32),
        vmem((rows, cols), b16),
        vmem((rows, cols), b16),
        dma((7,)),
        dma((7,)),
        dma((6,)),
        dma((6,)),
        dma((4, steps, 2, 2)),
        dma((4, steps, 2, 2)),
        dma((4, steps + 1, 2, 2)),
        dma((4, steps + 1, 2, 2)),
        dma((2, 18)),
        dma((2, 18)),
        dma((steps, 2, 2)),
        dma((steps, 2, 2)),
        dma((fans,)),
        dma((fans,)),
        dma((zs,)),
        dma((zs,)),
        dma((8,)),
        dma((8,)),
        dma((1,)),
    ]
    in_vmem = pl.BlockSpec(memory_space=pltpu.VMEM)
    return pl.pallas_call(
        functools.partial(kernel, zs, xs),
        out_shape=jax.ShapeDtypeStruct((rows, cols), f32),
        in_specs=[pl.BlockSpec(memory_space=pltpu.SMEM)] + [pl.BlockSpec(memory_space=pl.ANY)] * 7,
        out_specs=in_vmem,
        scratch_shapes=scratch,
        compiler_params=pltpu.CompilerParams(
            collective_id=0, has_side_effects=True, vmem_limit_bytes=62 * 1024 * 1024
        ),
        name="weight_gradient",
    )(ts, bi, ho, ww, qw, to, noise, target)


def body(
    block_input,
    head_outputs,
    out_master,
    first_moment,
    second_moment,
    score_qkv,
    teacher_out,
    noise,
    timestep,
    fake_target,
):
    zs, xs = lax.axis_size("seq") // 2, lax.axis_size("fsdp") // 2
    work_weight = out_master[0].astype(jnp.bfloat16)
    qw = score_qkv[0].transpose(0, 2, 1)
    weight_grad = weight_gradient(
        zs, xs, timestep, block_input[0].T, head_outputs[0], work_weight, qw, teacher_out, noise.T,
        fake_target.T,
    )
    new_first = 0.9 * first_moment[0] + 0.1 * weight_grad
    new_second = 0.95 * second_moment[0] + 0.05 * weight_grad * weight_grad
    new_master = out_master[0] - learn_rate * (new_first / first_fix) / (
        jnp.sqrt(new_second / second_fix) + 1e-08
    )
    return (new_master[None], new_first[None], new_second[None])


def solution(mesh):
    placed = (
        P("group", "seq", "fsdp"),
        P("group", "seq", None),
        P("group", "seq", "fsdp"),
        P("group", "seq", "fsdp"),
        P("group", "seq", "fsdp"),
        P("group", None, "fsdp", "seq"),
        P("seq", "fsdp"),
        P("seq", "fsdp"),
        P(),
        P("seq", "fsdp"),
    )
    return jax.shard_map(
        body,
        mesh=mesh,
        in_specs=placed,
        out_specs=(P("group", "seq", "fsdp"), P("group", "seq", "fsdp"), P("group", "seq", "fsdp")),
        check_vma=False,
    )
```

```python
import functools
import math

import jax
import jax.numpy as jnp
from jax import lax
from jax.experimental import pallas as pl
from jax.experimental.pallas import tpu as pltpu
from jax.sharding import PartitionSpec as P

D = 2560
HEAD_DIM = 128
MESH = pl.DeviceIdType.MESH

norm_eps = 1e-06
first_fix = 1.0 - 0.9**20
second_fix = 1.0 - 0.95**20
learn_rate = 0.003


class Sends:
    def __init__(self):
        self.open = []

    def start(self, ends, send_sem, recv_sem, device, when=None):
        def make():
            src, dst = ends()
            return pltpu.make_async_remote_copy(
                src_ref=src,
                dst_ref=dst,
                send_sem=send_sem(),
                recv_sem=recv_sem(),
                device_id=device(),
                device_id_type=MESH,
            )

        make().start()
        self.open.append((make, when))

    def same(self, ref, send_sem, recv_sem, device, when=None):
        def ends():
            here = ref()
            return here, here

        self.start(ends, send_sem, recv_sem, device, when)

    def take(self):
        taken, self.open = self.open, []
        return taken

    @staticmethod
    def finish(taken):
        for make, when in taken:
            if when is None:
                make().wait_send()
            else:
                pl.when(when)(lambda make=make: make().wait_send())


def wait_recv(dst, recv_sem):
    pltpu.make_async_copy(dst, dst, recv_sem).wait()


class Ring:
    def __init__(self, sends, place, buf, rows, sems, when=None, kind=None):
        self.sends, self.place, self.buf, self.rows, self.when = sends, place, buf, rows, when
        self.kind = kind
        self.ring_send, self.ring_recv, self.pair_send, self.pair_recv = sems
        self.steps = place.zs // 2

    def piece(self, zz, cc, half):
        if self.kind == 0:
            start = (2 * zz + cc) * self.rows
            return self.buf.at[half, pl.ds(pl.multiple_of(start, 16), self.rows)]
        each = self.rows // 2
        start = (2 * zz + cc) * self.rows + half * each
        if self.kind == 1:
            return self.buf.at[:, pl.ds(pl.multiple_of(start, 16), each), :]
        return self.buf.at[pl.ds(pl.multiple_of(start, 16), each)]

    def parts(self, k):
        if k < self.steps:
            return [(0, 0), (1, 0), (0, 1), (1, 1)]
        return [(0, 0), (1, 1)]

    def zz(self, k, way):
        p = self.place
        return lax.rem(p.z + p.zs - k, p.zs) if way == 0 else lax.rem(p.z + k, p.zs)

    def send(self, k, way, half):
        p = self.place
        self.sends.same(
            lambda: self.piece(self.zz(k - 1, way), p.c, half),
            lambda: self.ring_send.at[k - 1, way, half],
            lambda: self.ring_recv.at[k - 1, way, half],
            lambda: p.dev(z=p.zp if way == 0 else p.zm),
            self.when,
        )

    def pair(self, k, way, half):
        p = self.place
        self.sends.same(
            lambda: self.piece(self.zz(k, way), p.c, half),
            lambda: self.pair_send.at[k, way, half],
            lambda: self.pair_recv.at[k, way, half],
            lambda: p.dev(c=1 - p.c),
            self.when,
        )

    def begin(self, halves=(0, 1)):
        for way, half in self.parts(1):
            if half in halves:
                self.send(1, way, half)
        for half in halves:
            self.pair(0, 0, half)

    def advance(self, k, halves=(0, 1)):
        for way, half in self.parts(k):
            if half not in halves:
                continue
            wait_recv(
                self.piece(self.zz(k, way), self.place.c, half),
                self.ring_recv.at[k - 1, way, half],
            )
            if k < self.steps and (way, half) in self.parts(k + 1):
                self.send(k + 1, way, half)
            self.pair(k, way, half)

    def pair_arrived(self, k):
        for way, half in self.parts(k) if k else [(0, 0), (0, 1)]:
            wait_recv(
                self.piece(self.zz(k, way), 1 - self.place.c, half),
                self.pair_recv.at[k, way, half],
            )


class Across:
    def __init__(self, sends, place, buf, sems):
        self.sends, self.place, self.buf = sends, place, buf
        self.send_sem, self.recv_sem = sems
        self.rows = buf.shape[1]

    def part(self, dx, other, half, quarter=None):
        p = self.place
        block = 2 * lax.rem(p.x + dx + p.xs, p.xs) + (1 - p.a if other else p.a)
        each = self.rows // 2
        start = half * each
        if quarter is not None:
            each = each // 2
            start = start + quarter * each
        return self.buf.at[block, pl.ds(start, each)]

    def go(self, n, ref, device):
        self.sends.same(ref, lambda: self.send_sem.at[n], lambda: self.recv_sem.at[n], device)

    def beside(self, way):
        p = self.place
        return p.dev(x=lax.rem(p.x + (1 if way == 0 else p.xs - 1), p.xs))

    def cross(self, half):
        p = self.place
        self.go(half, lambda: self.part(0, False, half), lambda: p.dev(a=1 - p.a))

    def crossed(self, half):
        wait_recv(self.part(0, True, half), self.recv_sem.at[half])

    def step(self, other, half):
        for way in (0, 1):
            self.go(
                2 + 4 * other + 2 * half + way,
                lambda: self.part(0, other, half),
                lambda way=way: self.beside(way),
            )

    def forward(self, other, half):
        for way in (0, 1):
            near = -1 if way == 0 else 1
            n = 4 * other + 2 * half + way
            wait_recv(self.part(near, other, half), self.recv_sem.at[2 + n])
            self.go(
                10 + n,
                lambda near=near, way=way: self.part(near, other, half, way),
                lambda way=way: self.beside(way),
            )

    def arrived(self, half):
        for other in (0, 1):
            for way in (0, 1):
                n = 4 * other + 2 * half + way
                wait_recv(self.part(2, other, half, way), self.recv_sem.at[10 + n])

    def begin(self, half):
        self.cross(half)
        self.step(0, half)


class Place:
    def __init__(self, zs, xs):
        self.zs, self.xs = zs, xs
        seq, fsdp = lax.axis_index("seq"), lax.axis_index("fsdp")
        self.g = lax.axis_index("group")
        self.z, self.a = seq // 2, lax.rem(seq, 2)
        self.x, self.c = fsdp // 2, lax.rem(fsdp, 2)
        self.zp = lax.rem(self.z + 1, zs)
        self.zm = lax.rem(self.z + zs - 1, zs)
        self.block = 2 * self.x + self.a
        self.kept = self.a == self.c
        self.moved = self.a != self.c
        self.first = self.g == 0
        self.second = self.g == 1

    def dev(self, g=None, z=None, a=None, x=None, c=None):
        g = self.g if g is None else g
        z = self.z if z is None else z
        a = self.a if a is None else a
        x = self.x if x is None else x
        c = self.c if c is None else c
        return {"group": g, "seq": 2 * z + a, "fsdp": 2 * x + c}

    def fan(self):
        return [(2 * dx + da, dx, da) for dx in range(self.xs) for da in range(2) if dx or da]

    def beside(self, dx, da):
        return self.dev(x=lax.rem(self.x + dx, self.xs), a=lax.rem(self.a + da, 2))


def kernel(
    zs,
    xs,
    ts_ref,
    bi_ref,
    ho_ref,
    ww_ref,
    qw_ref,
    to_ref,
    noise_ref,
    target_ref,
    out_ref,
    w_buf,
    q_buf,
    hob,
    bi_t,
    noise_t,
    target_t,
    gen,
    gen_in,
    noisy,
    norm,
    kv,
    q_hat,
    acc,
    lsum,
    att,
    pred,
    b_own,
    b_in,
    grad,
    tmp,
    rs_send,
    rs_recv,
    gap_f,
    gap_z,
    gap_c,
    wg_out,
    wg_in,
    t_send,
    t_recv,
    ho_send,
    ho_recv,
    ring_send,
    ring_recv,
    pair_send,
    pair_recv,
    fan_send,
    fan_recv,
    rs_ssem,
    rs_rsem,
    gf_send,
    gf_recv,
    gz_send,
    gz_recv,
    one_send,
    one_recv,
    local_sem,
):
    p = Place(zs, xs)
    sends = Sends()
    tokens, inner = ho_ref.shape
    cols = bi_ref.shape[0]
    rows = ww_ref.shape[0]
    depth = qw_ref.shape[1]
    local_inner = q_hat.shape[1]
    heads = local_inner // HEAD_DIM
    steps = zs // 2
    fans = 2 * xs
    first = p.first
    second = p.second
    f32 = jnp.float32

    barrier = pltpu.get_barrier_semaphore()
    peers = [p.dev(z=lax.rem(p.z + dz, zs)) for dz in range(1, zs)]
    peers += [p.beside(dx, da) for _, dx, da in p.fan()]
    peers += [p.dev(c=1 - p.c), p.dev(g=1 - p.g), p.dev(a=1 - p.a, c=1 - p.c)]
    for peer in peers:
        pl.semaphore_signal(barrier, inc=1, device_id=peer, device_id_type=MESH)

    own_ho = pltpu.make_async_copy(ho_ref, hob.at[p.a], local_sem.at[0])
    own_ho.start()
    pl.semaphore_wait(barrier, len(peers))

    def rows_of(buf, each, at):
        return buf.at[pl.ds(pl.multiple_of(at * each, 16), each)]

    away, home = 2 * p.z + p.a, 2 * p.z + p.c
    swaps = [
        (ww_ref, lambda i: rows_of(w_buf.at[0], rows, i)),
        (bi_ref, lambda i: bi_t),
        (qw_ref, lambda i: q_buf.at[:, pl.ds(pl.multiple_of(i * depth, 16), depth), :]),
        (noise_ref, lambda i: noise_t),
        (to_ref, lambda i: rows_of(w_buf.at[1], rows, i)),
        (target_ref, lambda i: target_t),
        (ww_ref, lambda i: rows_of(w_buf.at[1], rows, i)),
    ]

    def swap(n, when):
        src, dst = swaps[n]

        @pl.when(p.kept)
        def _():
            pltpu.make_async_copy(src, dst(away), t_recv.at[n]).start()

        @pl.when(p.moved)
        def _():
            sends.start(
                lambda: (src, dst(away)),
                lambda: t_send.at[n],
                lambda: t_recv.at[n],
                lambda: p.dev(a=p.c, c=p.a),
                when,
            )

    first_moved, second_moved = first & p.moved, second & p.moved
    first_kept, second_kept = first & p.kept, second & p.kept

    def swapped(n):
        wait_recv(swaps[n][1](home), t_recv.at[n])

    share = tokens // xs

    def ho_rows(block, dx, half=None):
        start = lax.rem(p.x + dx + xs, xs) * share
        each = share
        if half is not None:
            each = share // 2
            start = start + half * each
        return hob.at[block, pl.ds(pl.multiple_of(start, 16), each)]

    def ho_cross(when):
        @pl.when(p.kept)
        def _():
            sends.start(
                lambda: (
                    ho_ref.at[pl.ds(pl.multiple_of(p.x * share, 16), share)],
                    ho_rows(p.a, 0),
                ),
                lambda: ho_send.at[0],
                lambda: ho_recv.at[0],
                lambda: p.dev(a=1 - p.a),
                when,
            )

    def beside(way):
        return p.dev(x=lax.rem(p.x + (1 if way == 0 else xs - 1), xs))

    def ho_step(when):
        @pl.when(p.moved)
        def _():
            wait_recv(ho_rows(p.c, 0), ho_recv.at[0])
            for way in (0, 1):
                sends.same(
                    lambda: ho_rows(p.c, 0),
                    lambda way=way: ho_send.at[1 + way],
                    lambda way=way: ho_recv.at[1 + way],
                    lambda way=way: beside(way),
                    when,
                )

    def ho_forward(when):
        @pl.when(p.moved)
        def _():
            for way in (0, 1):
                near = -1 if way == 0 else 1
                wait_recv(ho_rows(p.c, near), ho_recv.at[1 + way])
                sends.same(
                    lambda near=near, way=way: ho_rows(p.c, near, way),
                    lambda way=way: ho_send.at[3 + way],
                    lambda way=way: ho_recv.at[3 + way],
                    lambda way=way: beside(way),
                    when,
                )

    def ho_arrived(when):
        @pl.when(p.moved)
        def _():
            for way in (0, 1):
                wait_recv(ho_rows(p.c, 2, way), ho_recv.at[3 + way])
            sends.same(
                lambda: hob.at[p.c],
                lambda: ho_send.at[5],
                lambda: ho_recv.at[5],
                lambda: p.dev(c=1 - p.c),
                when,
            )

    def ring(buf, each, n, when=None, kind=None):
        sems = (ring_send.at[n], ring_recv.at[n], pair_send.at[n], pair_recv.at[n])
        return Ring(sends, p, buf, each, sems, when, kind)

    ring_w = ring(w_buf.at[0], rows, 0, first)
    ring_qs = [ring(q_buf, depth, 1, first, 1), ring(q_buf, depth, 1, second, 1)]
    ring_kv = ring(kv, tokens, 2, kind=0)
    ring_ts = [ring(w_buf.at[1], rows, 3, first), ring(w_buf.at[1], rows, 3, second)]
    over_noisy = Across(sends, p, noisy, (fan_send.at[0], fan_recv.at[0]))
    over_att = Across(sends, p, att, (fan_send.at[1], fan_recv.at[1]))

    wide = 2 * rows

    def gap_spread():
        for rank, dx, da in p.fan():
            sends.same(
                lambda: gap_f.at[p.block],
                lambda rank=rank: gf_send.at[rank],
                lambda rank=rank: gf_recv.at[rank],
                lambda dx=dx, da=da: p.beside(dx, da),
                first,
            )

    def gap_gathered():
        for rank, dx, da in p.fan():
            block = 2 * lax.rem(p.x + xs - dx, xs) + lax.rem(p.a + da, 2)
            wait_recv(gap_f.at[block], gf_recv.at[rank])

    def predict(which):
        value = jnp.zeros((tokens, cols), f32)
        for j in range(inner // wide):
            at = slice(j * wide, (j + 1) * wide)
            value += jnp.dot(hob[p.c, :, at], w_buf[which, at, :], preferred_element_type=f32)
        pred[...] = value

    half_rows = [slice(0, tokens // 2), slice(tokens // 2, tokens)]
    half_cols = [slice(0, cols // 2), slice(cols // 2, cols)]

    @pl.when(first)
    def _():
        ring_q = ring_qs[0]
        swap(0, first_moved)
        ho_cross(first_kept)
        swap(1, first_moved)
        swapped(0)
        ring_w.begin()
        swap(3, first_moved)
        swap(2, first_moved)
        ring_w.advance(1)
        ho_step(first_moved)
        ring_w.advance(2)
        ring_w.advance(3)
        ho_forward(first_moved)
        swapped(2)
        ring_q.begin()
        swap(4, first_moved)
        ring_w.advance(4)
        own_ho.wait()
        ho_arrived(first_moved)
        for k in range(steps + 1):
            ring_w.pair_arrived(k)
        swapped(1)
        predict(0)
        gen[...] = (bi_t[...].astype(f32) + pred[...].T).astype(jnp.bfloat16)
        for h in (0, 1):
            sends.start(
                lambda h=h: (gen.at[half_cols[h]], gen_in.at[half_cols[h]]),
                lambda h=h: one_send.at[h],
                lambda h=h: one_recv.at[h],
                lambda: p.dev(g=1),
                first,
            )

    @pl.when(second)
    def _():
        ring_q = ring_qs[1]
        swap(2, second_moved)
        swapped(2)
        ring_q.begin()
        swap(3, second_moved)
        ring_q.advance(1)
        swap(6, second_moved)
        ring_q.advance(2)
        own_ho.wait()

    swapped(3)
    level = ts_ref[0].astype(f32) / 1000.0
    for h in (0, 1):
        at = half_cols[h]

        @pl.when(second)
        def _():
            wait_recv(gen_in.at[at], one_recv.at[h])
            gen[at, :] = gen_in[at, :]

        noisy[p.block, at, :] = (
            (1.0 - level) * gen[at, :].astype(f32) + level * noise_t[at, :].astype(f32)
        ).astype(jnp.bfloat16)
        over_noisy.begin(h)

    def first_q(k):
        pl.when(first)(lambda: ring_qs[0].advance(k))

        @pl.when(second)
        def _():
            if k == 1:
                ring_qs[1].advance(3)
            if k == 2:
                ring_qs[1].advance(4)
                swapped(6)
                ring_ts[1].begin()
            if k == 4:
                ring_ts[1].advance(1)

    def second_later(k):
        if k == 0:
            ho_cross(second_kept)
            swap(1, second_moved)
            swap(5, second_moved)
        if k == 1:
            ho_step(second_moved)
        if k == 2:
            ho_forward(second_moved)
        if k == 3:
            ho_arrived(second_moved)
        if 1 <= k <= 3:
            ring_ts[1].advance(k + 1)

    def first_t(k):
        pl.when(first)(lambda: ring_ts[0].advance(k))

    @pl.when(first)
    def _():
        pred[...] = (gen[...].astype(f32) - noisy[p.block].astype(f32)).T

    over_noisy.forward(0, 0)
    first_q(1)
    over_noisy.crossed(0)
    over_noisy.step(1, 0)
    over_noisy.forward(0, 1)
    over_noisy.crossed(1)
    over_noisy.step(1, 1)
    first_q(2)
    over_noisy.forward(1, 0)
    over_noisy.forward(1, 1)
    first_q(3)
    over_noisy.arrived(0)
    over_noisy.arrived(1)

    total = jnp.zeros((1, tokens), f32)
    for f in range(fans):
        block = noisy[f].astype(f32)
        total += jnp.sum(block * block, axis=0, keepdims=True)
    factor = lax.rsqrt(total * (1.0 / (fans * cols)) + norm_eps)
    for f in range(fans):
        norm[f * cols : (f + 1) * cols, :] = (noisy[f].astype(f32) * factor).astype(jnp.bfloat16)
    first_q(4)
    for k in range(steps + 1):
        ring_qs[0].pair_arrived(k)

    def head_norm(value):
        scale = lax.rsqrt(jnp.mean(value * value, axis=1, keepdims=True) + norm_eps)
        return (value * scale).astype(jnp.bfloat16)

    own_rows = pl.ds(pl.multiple_of(home * tokens, 16), tokens)

    def proj(n):
        return lax.dot_general(
            norm[...], q_buf[n], (((0,), (0,)), ((), ())), preferred_element_type=f32
        )

    key_raw = proj(1)
    for h in range(heads):
        at = slice(h * HEAD_DIM, (h + 1) * HEAD_DIM)
        kv[0, own_rows, at] = head_norm(key_raw[:, at])
    ring_kv.begin((0,))
    kv[1, own_rows, :] = proj(2).astype(jnp.bfloat16)
    ring_kv.begin((1,))
    query_raw = proj(0)
    for h in range(heads):
        at = slice(h * HEAD_DIM, (h + 1) * HEAD_DIM)
        q_hat[:, at] = head_norm(query_raw[:, at])
    acc[...] = jnp.zeros_like(acc)
    lsum[...] = jnp.zeros_like(lsum)

    def attend(zz):
        at = pl.ds(pl.multiple_of(zz * 2 * tokens, 16), 2 * tokens)

        def one_head(h, carry):
            cut = pl.ds(pl.multiple_of(h * HEAD_DIM, HEAD_DIM), HEAD_DIM)
            scores = lax.dot_general(
                q_hat[:, cut], kv[0, at, cut], (((1,), (1,)), ((), ())), preferred_element_type=f32
            ) * (1.0 / math.sqrt(HEAD_DIM))
            weights = jnp.exp(scores)
            part = weights[:, :128]
            for j in range(1, 2 * tokens // 128):
                part += weights[:, j * 128 : (j + 1) * 128]
            lsum[h] += part
            acc[:, cut] += jnp.dot(
                weights.astype(jnp.bfloat16), kv[1, at, cut], preferred_element_type=f32
            )
            return carry

        lax.fori_loop(0, heads, one_head, 0)

    ring_kv.pair_arrived(0)
    attend(p.z)
    pl.when(second)(lambda: second_later(0))
    for k in range(1, steps + 1):
        for half in (0, 1):
            ring_kv.advance(k, (half,))
            if k > 1:
                if half == 0:
                    ring_kv.pair_arrived(k - 1)
                attend(ring_kv.zz(k - 1, half))
        pl.when(second)(lambda: second_later(k))
        if k == steps:

            @pl.when(first)
            def _():
                swapped(4)
                ring_ts[0].begin()

    ring_kv.pair_arrived(steps)
    attend(ring_kv.zz(steps, 0))

    for half in (0, 1):
        rr = half_rows[half]
        for h in range(heads):
            at = slice(h * HEAD_DIM, (h + 1) * HEAD_DIM)
            att[p.block, rr, at] = (
                acc[rr, at] / jnp.sum(lsum[h, rr, :], axis=1, keepdims=True)
            ).astype(jnp.bfloat16)
        over_att.begin(half)
    over_att.forward(0, 0)
    first_t(1)
    over_att.crossed(0)
    over_att.step(1, 0)
    over_att.forward(0, 1)
    first_t(2)
    over_att.crossed(1)
    over_att.step(1, 1)
    over_att.forward(1, 0)
    first_t(3)
    over_att.forward(1, 1)
    first_t(4)
    for k in range(steps + 1):
        ring_ts[0].pair_arrived(k)

    early = sends.take()

    def pass_branch(h):
        sends.start(
            lambda: (b_own.at[half_rows[h]], b_in.at[half_rows[h]]),
            lambda: one_send.at[2 + h],
            lambda: one_recv.at[2 + h],
            lambda: p.dev(g=0),
            second,
        )

    for h in (0, 1):
        rr = half_rows[h]
        over_att.arrived(h)
        value = jnp.zeros((tokens // 2, cols), f32)
        for j in range(fans):
            value += jnp.dot(
                att[j, rr, :], w_buf[1, j * wide : (j + 1) * wide, :], preferred_element_type=f32
            )
        b_own[rr, :] = value

        pl.when(second)(lambda: pass_branch(h))

    def pass_grad(h):
        sends.same(
            lambda h=h: grad.at[p.c, half_rows[h]],
            lambda: one_send.at[4 + h],
            lambda: one_recv.at[4 + h],
            lambda: p.dev(c=1 - p.c),
        )

    @pl.when(second)
    def _():
        swapped(1)
        swapped(5)
        predict(1)
        grad[p.c] = (
            (pred[...] + (bi_t[...].astype(f32) - target_t[...].astype(f32)).T) * (1.0 / math.sqrt(tokens * 2 * zs))
        ).astype(jnp.bfloat16)

    @pl.when(first)
    def _():
        gap = jnp.sum(jnp.abs(pred[...] - b_own[...]))
        gap_f[p.block] = jnp.full((8, 128), gap, f32)
        gap_spread()

    sends.finish(early)
    for h in (0, 1):
        rr = half_rows[h]

        @pl.when(first)
        def _():
            wait_recv(b_in.at[rr], one_recv.at[2 + h])
            grad[p.c, rr, :] = (b_in[rr, :] - b_own[rr, :]).astype(jnp.bfloat16)

        pass_grad(h)

    @pl.when(p.kept)
    def _():
        wait_recv(hob.at[1 - p.c], ho_recv.at[5])

    for h in (0, 1):
        wait_recv(grad.at[1 - p.c, half_rows[h]], one_recv.at[4 + h])

    def partial(zz):
        at = pl.ds(pl.multiple_of(zz * wide, 128), wide)
        value = jnp.zeros((wide, cols), f32)
        for block in range(2):
            value += lax.dot_general(
                hob[block, :, at],
                grad[block],
                (((0,), (0,)), ((), ())),
                preferred_element_type=f32,
            )
        tmp[...] = value
        return tmp[pl.ds(pl.multiple_of(p.c * rows, 16), rows), :]

    each = rows // 2
    half_chunk = [slice(0, each), slice(each, rows)]

    def rs_parts(j):
        return [(0, 0), (1, 1)] if j == 1 else [(0, 1), (1, 0), (0, 0), (1, 1)]

    def rs_start(j, way, half):
        sends.start(
            lambda: (rs_send.at[j - 1, way, half], rs_recv.at[j - 1, way, half]),
            lambda: rs_ssem.at[j - 1, way, half],
            lambda: rs_rsem.at[j - 1, way, half],
            lambda: p.dev(z=p.zp if way == 0 else p.zm),
        )

    def rs_wait(j, way, half):
        wait_recv(rs_recv.at[j - 1, way, half], rs_rsem.at[j - 1, way, half])

    def gap_step(j):
        if j == 1:
            gap_gathered()
            gap_z[p.z] = jnp.sum(gap_f[...], axis=0)
            for dz in range(1, zs):
                sends.same(
                    lambda: gap_z.at[p.z],
                    lambda dz=dz: gz_send.at[dz],
                    lambda dz=dz: gz_recv.at[dz],
                    lambda dz=dz: p.dev(z=lax.rem(p.z + dz, zs)),
                    first,
                )
        if j == 2:
            for dz in range(1, zs):
                wait_recv(gap_z.at[lax.rem(p.z + zs - dz, zs)], gz_recv.at[dz])
            gap_c[p.c] = jnp.sum(gap_z[...], axis=0)
            sends.same(
                lambda: gap_c.at[p.c],
                lambda: one_send.at[6],
                lambda: one_recv.at[6],
                lambda: p.dev(c=1 - p.c),
                first,
            )
        if j == 3:
            wait_recv(gap_c.at[1 - p.c], one_recv.at[6])

    far = partial(lax.rem(p.z + steps, zs))
    for way, half in rs_parts(1):
        rs_send[0, way, half] = far[half_chunk[half]].astype(jnp.bfloat16)
        rs_start(1, way, half)
    for j in range(2, steps + 1):
        dist = steps - j + 1
        mine = [partial(lax.rem(p.z + dist, zs)), partial(lax.rem(p.z + zs - dist, zs))]
        for way, half in rs_parts(j):
            value = mine[way][half_chunk[half]]
            if (way, half) in rs_parts(j - 1):
                rs_wait(j - 1, way, half)
                value = value + rs_recv[j - 2, way, half].astype(f32)
            rs_send[j - 1, way, half] = value.astype(jnp.bfloat16)
            rs_start(j, way, half)
        if j == 2:
            pl.when(first)(lambda: gap_step(1))
        if j == 3:
            pl.when(first)(lambda: gap_step(2))
    mine = partial(p.z)
    pl.when(first)(lambda: gap_step(3))
    acc_w = tmp.at[0:rows]
    acc_w[...] = mine
    for way, half in rs_parts(2):
        rs_wait(steps, way, half)
        at = half_chunk[half]
        acc_w[at, :] = acc_w[at, :] + rs_recv[steps - 1, way, half].astype(f32)

    @pl.when(first)
    def _():
        gap = (gap_c[0] + gap_c[1])[0:1, 0:1] * (1.0 / (tokens * 2 * zs * fans * cols))
        wg_out[...] = (acc_w[...] * (1.0 / (gap + norm_eps))).astype(jnp.bfloat16)

    @pl.when(second)
    def _():
        wg_out[...] = acc_w[...].astype(jnp.bfloat16)

    @pl.when(p.moved)
    def _():
        sends.start(
            lambda: (wg_out, wg_in),
            lambda: one_send.at[7],
            lambda: one_recv.at[7],
            lambda: p.dev(a=p.c, c=p.a),
            p.moved,
        )
        wait_recv(wg_in, one_recv.at[7])
        out_ref[...] = wg_in[...].astype(f32)

    @pl.when(p.kept)
    def _():
        out_ref[...] = wg_out[...].astype(f32)

    sends.finish(sends.take())


def weight_gradient(zs, xs, ts, bi, ho, ww, qw, to, noise, target, interpret=None):
    tokens, inner = ho.shape
    cols = bi.shape[0]
    rows = ww.shape[0]
    depth, local_inner = qw.shape[1:]
    heads = local_inner // HEAD_DIM
    seq, fans, steps = 2 * zs, 2 * xs, zs // 2
    b16, f32 = jnp.bfloat16, jnp.float32
    vmem, dma = pltpu.VMEM, pltpu.SemaphoreType.DMA
    scratch = [
        vmem((2, inner, cols), b16),
        vmem((3, seq * depth, local_inner), b16),
        vmem((2, tokens, inner), b16),
        vmem((cols, tokens), b16),
        vmem((cols, tokens), b16),
        vmem((cols, tokens), b16),
        vmem((cols, tokens), b16),
        vmem((cols, tokens), b16),
        vmem((fans, cols, tokens), b16),
        vmem((fans * cols, tokens), b16),
        vmem((2, seq * tokens, local_inner), b16),
        vmem((tokens, local_inner), b16),
        vmem((tokens, local_inner), f32),
        vmem((heads, tokens, 128), f32),
        vmem((fans, tokens, local_inner), b16),
        vmem((tokens, cols), f32),
        vmem((tokens, cols), f32),
        vmem((tokens, cols), f32),
        vmem((2, tokens, cols), b16),
        vmem((2 * rows, cols), f32),
        vmem((steps, 2, 2, rows // 2, cols), b16),
        vmem((steps, 2, 2, rows // 2, cols), b16),
        vmem((fans, 8, 128), f32),
        vmem((zs, 8, 128), f32),
        vmem((2, 8, 128), f32),
        vmem((rows, cols), b16),
        vmem((rows, cols), b16),
        dma((7,)),
        dma((7,)),
        dma((6,)),
        dma((6,)),
        dma((4, steps, 2, 2)),
        dma((4, steps, 2, 2)),
        dma((4, steps + 1, 2, 2)),
        dma((4, steps + 1, 2, 2)),
        dma((2, 18)),
        dma((2, 18)),
        dma((steps, 2, 2)),
        dma((steps, 2, 2)),
        dma((fans,)),
        dma((fans,)),
        dma((zs,)),
        dma((zs,)),
        dma((8,)),
        dma((8,)),
        dma((1,)),
    ]
    in_vmem = pl.BlockSpec(memory_space=pltpu.VMEM)
    return pl.pallas_call(
        functools.partial(kernel, zs, xs),
        out_shape=jax.ShapeDtypeStruct((rows, cols), f32),
        in_specs=[pl.BlockSpec(memory_space=pltpu.SMEM)] + [pl.BlockSpec(memory_space=pl.ANY)] * 7,
        out_specs=in_vmem,
        scratch_shapes=scratch,
        compiler_params=pltpu.CompilerParams(
            collective_id=0, has_side_effects=True, vmem_limit_bytes=62 * 1024 * 1024
        ),
        name="weight_gradient",
    )(ts, bi, ho, ww, qw, to, noise, target)


def body(
    block_input,
    head_outputs,
    out_master,
    first_moment,
    second_moment,
    score_qkv,
    teacher_out,
    noise,
    timestep,
    fake_target,
):
    zs, xs = lax.axis_size("seq") // 2, lax.axis_size("fsdp") // 2
    work_weight = out_master[0].astype(jnp.bfloat16)
    qw = score_qkv[0].transpose(0, 2, 1)
    weight_grad = weight_gradient(
        zs, xs, timestep, block_input[0].T, head_outputs[0], work_weight, qw, teacher_out, noise.T,
        fake_target.T,
    )
    new_first = 0.9 * first_moment[0] + 0.1 * weight_grad
    new_second = 0.95 * second_moment[0] + 0.05 * weight_grad * weight_grad
    new_master = out_master[0] - learn_rate * (new_first / first_fix) / (
        jnp.sqrt(new_second / second_fix) + 1e-08
    )
    return (new_master[None], new_first[None], new_second[None])


def solution(mesh):
    placed = (
        P("group", "seq", "fsdp"),
        P("group", "seq", None),
        P("group", "seq", "fsdp"),
        P("group", "seq", "fsdp"),
        P("group", "seq", "fsdp"),
        P("group", None, "fsdp", "seq"),
        P("seq", "fsdp"),
        P("seq", "fsdp"),
        P(),
        P("seq", "fsdp"),
    )
    return jax.shard_map(
        body,
        mesh=mesh,
        in_specs=placed,
        out_specs=(P("group", "seq", "fsdp"), P("group", "seq", "fsdp"), P("group", "seq", "fsdp")),
        check_vma=False,
    )
```
